32 devices in a mesh: chan: 8 (over y, x, core), facet: 4 (over z).
Axes of the slice: x: 2, y: 2, z: 4, core: 2. Of those that a mesh axis runs over, the one named last changes fastest.
Arguments:
- start_image: float32 [64, 8192], P(None, 'facet'), may hold values from 0 to 3
- visibilities: bfloat16 [32, 16, 4, 256], P(('chan', 'facet')), may hold values from -12 to 12
- strip_index: int32 [32, 16, 4, 2], P(('chan', 'facet')), may hold values from 0 to 4095
- live_counts: int32 [32, 16, 4], P(('chan', 'facet')), may hold values from 0 to 128
- uv_kernels: bfloat16 [16, 4, 256, 256], P('chan', 'facet'), may hold values from -0.375 to 0.375
Outputs:
- final_image: float32 [64, 8192], P(None, 'facet')
The draws below stay inside these ranges and needn't reach their ends.
Inputs may be any that keep to these rules, and one draw needn't show every extreme that they name: `strip_index`: each visibility block reads 2 image strips. The first live_counts of a block's 128 visibilities are live, the others are flagged.
All inputs are finite; a program needn't handle non-finite values.
Results may differ from the reference program's by a relative error of at most 0.0026.
Values may be sent and summed in bfloat16 or wider, within the bound.
No kernel may reach another device: no remote copies, remote signals or barrier semaphores. Data moves between devices by JAX's collectives and lax.ppermute only.
A program may use at most 64 MiB of HBM per device.

```python
import jax
import jax.numpy as jnp
from jax import lax

NPIX = 8192
STRIP = 128
VISB = 128
TERMS = 2
ITERS = 2
SLAB = 64
CHANNELS = 16
UVT = 4
SLOTS = 32
STRIPS = 4096


def with_ends(entries, stream_key, least, top_value):
    index_at = [jax.random.randint(jax.random.fold_in(stream_key, axis), (), 0, length) for axis, length in enumerate(entries.shape)]
    main_axis = entries.shape.index(max(entries.shape))
    beside = index_at[:main_axis] + [(index_at[main_axis] + 1) % entries.shape[main_axis]] + index_at[main_axis + 1:]
    return entries.at[tuple(index_at)].set(least).at[tuple(beside)].set(top_value)


def block_levels(rng, dims, cuts, low, top_value):
    def one(position, blocks):
        heights = jax.random.uniform(jax.random.fold_in(jax.random.fold_in(rng, 6), position), (blocks,), jnp.float32, low / len(cuts), top_value / len(cuts))
        return jnp.repeat(jnp.exp(heights), dims[position] // blocks).reshape((-1,) + (1,) * (len(dims) - position - 1))

    loudness = one(*cuts[0])
    for cut in cuts[1:]:
        loudness = loudness * one(*cut)
    return loudness


def noise(own_key, shape, scale, limit, cuts=(), held_as=jnp.bfloat16):
    level = block_levels(own_key, shape, cuts, -0.22, 0.18) if cuts else 1.0
    values = jax.random.normal(own_key, shape, jnp.float32) * scale * level
    return jnp.minimum(jnp.maximum(values, -limit), limit).astype(held_as)


def setup_inputs(seed: int = 0) -> dict:
    key_of = jax.random.split(jax.random.key(seed), 6)
    start_image = jnp.clip(3.0 * jax.random.uniform(key_of[0], (SLAB, NPIX), jnp.float32) ** block_levels(key_of[0], (SLAB, NPIX), ((1, 4),), -0.2, 0.2), 0.0, 3.0)
    visibilities = noise(key_of[1], (SLOTS, CHANNELS, UVT, 2 * VISB), 2.0, 12.0, ((0, 32),))
    strip_index = with_ends(jax.random.randint(key_of[2], (SLOTS, CHANNELS, UVT, TERMS), 0, STRIPS), jax.random.fold_in(key_of[2], 1), 0, STRIPS - 1).astype(jnp.int32)
    live_counts = with_ends(jax.random.randint(key_of[3], (SLOTS, CHANNELS, UVT), 0, VISB + 1), jax.random.fold_in(key_of[3], 1), 0, VISB).astype(jnp.int32)
    uv_kernels = noise(key_of[4], (CHANNELS, UVT, TERMS * STRIP, 2 * VISB), (TERMS * STRIP) ** -0.5, 0.375, ((0, 8), (1, 4)))
    return dict(start_image=start_image, visibilities=visibilities, strip_index=strip_index, live_counts=live_counts, uv_kernels=uv_kernels)


shrinkage = 0.05


def reference(start_image, visibilities, strip_index, live_counts, uv_kernels):
    strip_count = SLAB * NPIX // STRIP
    step_size = strip_count / (2.5 * SLOTS * CHANNELS * UVT)
    lane_ids = jnp.arange(2 * VISB, dtype=jnp.int32) % VISB
    estimate = start_image
    for iteration in range(ITERS):
        sky_strips = estimate.astype(jnp.bfloat16).reshape(strip_count, STRIP)

        def per_channel(channel, gradient):
            observed = lax.dynamic_index_in_dim(visibilities, channel, 1, keepdims=False)
            picked_ids = lax.dynamic_index_in_dim(strip_index, channel, 1, keepdims=False)
            live_now = lax.dynamic_index_in_dim(live_counts, channel, 1, keepdims=False)
            kernel_now = lax.dynamic_index_in_dim(uv_kernels, channel, 0, keepdims=False)
            gathered = sky_strips[picked_ids].reshape(SLOTS, UVT, TERMS * STRIP).astype(jnp.float32)
            kernel_wide = kernel_now.astype(jnp.float32)
            predicted = jnp.einsum("sup,upq->suq", gathered, kernel_wide)
            live_mask = lane_ids[None, None, :] < live_now[:, :, None]
            residual = jnp.where(live_mask, predicted - observed.astype(jnp.float32), jnp.float32(0.0)).astype(jnp.bfloat16)
            adjoint = jnp.einsum("suq,upq->sup", residual.astype(jnp.float32), kernel_wide)
            return gradient.at[picked_ids.reshape(-1)].add(adjoint.reshape(-1, STRIP))

        gradient = lax.fori_loop(0, CHANNELS, per_channel, jnp.zeros((strip_count, STRIP), jnp.float32))
        descent = estimate - step_size * gradient.reshape(SLAB, NPIX)
        estimate = jnp.maximum(descent - shrinkage, jnp.float32(0.0))
    return estimate
```

```python
import functools

import jax
import jax.numpy as jnp
from jax import lax
from jax.experimental import pallas as pl
from jax.experimental.pallas import tpu as pltpu
from jax.sharding import PartitionSpec as P

STRIP = 128
VISB = 128
TERMS = 2
ITERS = 2
TILE = 8
EXTRA = 16

shrinkage = 0.05
F32, BF16, I32, I16 = jnp.float32, jnp.bfloat16, jnp.int32, jnp.int16
VMEM_LIMIT = 48 * 1024 * 1024


def call(kernel, outs, args, flops, smem=0):
    spaces = [pl.BlockSpec(memory_space=pltpu.SMEM)] * smem
    spaces += [pl.BlockSpec(memory_space=pltpu.VMEM)] * (len(args) - smem)
    moved = sum(a.size * a.dtype.itemsize for a in list(args) + list(outs))
    return pl.pallas_call(
        kernel,
        out_shape=list(outs),
        in_specs=spaces,
        out_specs=[pl.BlockSpec(memory_space=pltpu.VMEM)] * len(outs),
        compiler_params=pltpu.CompilerParams(vmem_limit_bytes=VMEM_LIMIT),
        cost_estimate=pl.CostEstimate(flops=flops, bytes_accessed=moved, transcendentals=0),
    )(*args)


def split(x, parts):
    terms = []
    for _ in range(parts):
        term = x.astype(BF16)
        terms.append(term)
        x = x - term.astype(F32)
    return terms


def one_hot(hit):
    return jnp.where(hit, 1.0, 0.0).astype(BF16)


def sorted_rows(rx, slots, rows):
    total = slots * rows
    out = lax.broadcasted_iota(I32, (total, total), 0)
    src = lax.broadcasted_iota(I32, (total, total), 1)
    hit = src == (out % slots) * rows + out // slots
    return jnp.dot(one_hot(hit), rx, preferred_element_type=F32)


def ref_column(scalars, group, groups, each):
    lanes = groups * each
    ids = scalars[:, :lanes] * 64.0 + scalars[:, lanes : 2 * lanes]
    cols = [ids[:, group * each + i : group * each + i + 1] for i in range(each)]
    return jnp.concatenate(cols, axis=0).astype(I32)


def serve_kernel(slots, groups, each, rows, facet, rx, image, *outs):
    order = sorted_rows(rx[...], slots, rows)
    scalars = order[2 * (each // TERMS) * slots : (2 * (each // TERMS) + 1) * slots]
    height, width = image.shape
    tiles = [
        image[r : r + TILE, c : c + STRIP]
        for r in range(0, height, TILE)
        for c in range(0, width, STRIP)
    ]
    strips = jnp.concatenate(tiles, axis=0)
    count = strips.shape[0]
    table = jnp.concatenate(split(strips, 3), axis=1)
    base = facet[0] * count
    for group in range(groups):
        col = ref_column(scalars, group, groups, each) - base
        lane = lax.broadcasted_iota(I32, (col.shape[0], count), 1)
        got = jnp.dot(one_hot(lane == col), table, preferred_element_type=F32)
        outs[group][...] = (got[:, :STRIP] + got[:, STRIP : 2 * STRIP]) + got[:, 2 * STRIP :]


def measure(est, order, scalars, kernels, slots, groups, each):
    lanes = groups * each
    adjoints = []
    for ch in range(each // TERMS):
        first = ch * TERMS * slots
        sky = jnp.concatenate(
            [est[first : first + slots], est[first + slots : first + 2 * slots]], axis=1
        ).astype(BF16)
        seen = jnp.concatenate(
            [order[first : first + slots], order[first + slots : first + 2 * slots]], axis=1
        )
        kern = kernels[ch]
        predicted = jnp.dot(sky, kern, preferred_element_type=F32)
        live = scalars[:, 2 * lanes + ch : 2 * lanes + ch + 1].astype(I32)
        lane = lax.broadcasted_iota(I32, predicted.shape, 1) % VISB
        residual = jnp.where(lane < live, predicted - seen, 0.0).astype(BF16)
        adjoint = lax.dot_general(
            residual, kern, (((1,), (1,)), ((), ())), preferred_element_type=F32
        )
        adjoints += [adjoint[:, :STRIP], adjoint[:, STRIP:]]
    return jnp.concatenate(adjoints, axis=0)


def encode(adjoint, col, msg):
    refs = adjoint.shape[0]
    top = jnp.max(jnp.abs(adjoint), axis=(0, 1), keepdims=True)
    exponent = jnp.ceil(jnp.log2(jnp.maximum(top, 1e-30) * (1.0 / 32000.0)))
    code = jnp.round(adjoint * jnp.exp2(-exponent))
    msg[:refs] = code.astype(I32).astype(I16)
    eye = lax.broadcasted_iota(I32, (refs, STRIP), 0) == lax.broadcasted_iota(
        I32, (refs, STRIP), 1
    )
    ids = jnp.sum(jnp.where(eye, col.astype(F32), 0.0), axis=0, keepdims=True)
    row = lax.broadcasted_iota(I32, (EXTRA, STRIP), 0)
    extra = jnp.where(row == 0, ids, jnp.where(row == 1, exponent, 0.0))
    msg[refs:] = extra.astype(I32).astype(I16)


def decode(refs, *blocks):
    ids, rows = [], []
    size = refs + EXTRA
    for block in blocks:
        for at in range(0, block.shape[0], size):
            extra = block[at + refs : at + size].astype(I32)
            ids.append(extra[0:1])
            scale = jnp.exp2(extra[1:2].astype(F32))
            value = block[at : at + refs].astype(I32).astype(F32) * scale
            rows.append(jnp.concatenate(split(value, 2), axis=1))
    return jnp.concatenate(ids, axis=1), jnp.concatenate(rows, axis=0)


def first_kernel(slots, groups, each, rows, terms, *refs):
    rx, kernels = refs[0], refs[1]
    parts = refs[2 : 2 + terms]
    start_out, msg = refs[2 + terms :]
    order = sorted_rows(rx[...], slots, rows)
    scalars = order[2 * (each // TERMS) * slots : (2 * (each // TERMS) + 1) * slots]
    est = parts[0][...]
    for part in parts[1:]:
        est = est + part[...]
    start_out[...] = est
    adjoint = measure(est, order, scalars, kernels, slots, groups, each)
    encode(adjoint, ref_column(scalars, 0, groups, each), msg)


def next_kernel(slots, groups, each, rows, step, rx, kernels, est_in, mine, other, est_out, msg):
    order = sorted_rows(rx[...], slots, rows)
    scalars = order[2 * (each // TERMS) * slots : (2 * (each // TERMS) + 1) * slots]
    col = ref_column(scalars, 0, groups, each)
    refs = col.shape[0]
    ids, values = decode(refs, mine, other)
    both = jnp.dot(one_hot(ids == col), values, preferred_element_type=F32)
    gradient = both[:, :STRIP] + both[:, STRIP:]
    est = jnp.maximum(est_in[...] - step * gradient - shrinkage, 0.0)
    est_out[...] = est
    adjoint = measure(est, order, scalars, kernels, slots, groups, each)
    encode(adjoint, col, msg)


def settle_kernel(refs, step, facet, image, mine, other, out):
    ids, values = decode(refs, mine, other)
    height, width = image.shape
    count = height * width // STRIP
    per_band = width // STRIP * TILE
    chunk = min(256, count)
    for at in range(0, count, chunk):
        strip = lax.broadcasted_iota(I32, (chunk, 1), 0) + (facet[0] * count + at)
        both = jnp.dot(one_hot(ids == strip), values, preferred_element_type=F32)
        gradient = both[:, :STRIP] + both[:, STRIP:]
        for t in range(0, chunk, TILE):
            r = (at + t) // per_band * TILE
            c = (at + t) % per_band // TILE * STRIP
            old = image[r : r + TILE, c : c + STRIP]
            out[r : r + TILE, c : c + STRIP] = jnp.maximum(
                old - step * gradient[t : t + TILE] - shrinkage, 0.0
            )


def swap(x, axis, k):
    return lax.ppermute(x, axis, [(i, i ^ k) for i in range(lax.axis_size(axis))])


def spread(msg):
    near = jnp.concatenate(
        [msg] + [swap(msg, "facet", k) for k in range(1, lax.axis_size("facet"))], axis=0
    )
    mine = jnp.concatenate(
        [near] + [swap(near, "chan", k) for k in range(2, lax.axis_size("chan"), 2)], axis=0
    )
    return mine, swap(mine, "chan", 1)


def sparse_device(start_image, visibilities, strip_index, live_counts, uv_kernels):
    C, F = lax.axis_size("chan"), lax.axis_size("facet")
    L = uv_kernels.shape[0]
    each = L * TERMS
    S = C * F
    refs = S * each
    height, width = start_image.shape
    per_facet = height * width // STRIP
    step = float(per_facet * F / (2.5 * S * (L * C) * F))
    rows = 8

    strip_row, column = strip_index[0] // (F * width // STRIP), strip_index[0] % (F * width // STRIP)
    wide = width // STRIP
    numbers = (
        (column // wide) * per_facet
        + (strip_row // TILE) * (wide * TILE)
        + (column % wide) * TILE
        + strip_row % TILE
    )
    numbers = numbers.reshape(C, L, F, TERMS).transpose(0, 2, 1, 3)
    ordered = jnp.stack(
        [jnp.stack([numbers[:, f ^ k] for k in range(F)], axis=1) for f in range(F)], axis=1
    ).reshape(C, F, F * each)
    counts = live_counts[0].reshape(C, L, F).transpose(0, 2, 1)
    scalars = jnp.concatenate([ordered // 64, ordered % 64, counts], axis=2).astype(BF16)
    scalars = jnp.pad(scalars, ((0, 0), (0, 0), (0, STRIP - scalars.shape[2])))
    seen = visibilities[0].reshape(C, L, F, 2, VISB).transpose(0, 2, 1, 3, 4)
    seen = seen.reshape(C, F, 2 * L, VISB)
    sent = jnp.concatenate([seen, scalars[:, :, None]], axis=2)
    sent = jnp.pad(sent, ((0, 0), (0, 0), (0, rows - sent.shape[2]), (0, 0)))
    rx = lax.all_to_all(sent.reshape(S, rows, STRIP), ("chan", "facet"), 0, 0, tiled=True)
    rx = rx.reshape(S * rows, STRIP)

    facet = lax.axis_index("facet").astype(I32).reshape(1)
    piece = jax.ShapeDtypeStruct((refs, STRIP), F32)
    message = jax.ShapeDtypeStruct((refs + EXTRA, STRIP), I16)
    served = call(
        functools.partial(serve_kernel, S, F, each, rows),
        [piece] * F,
        [facet, rx, start_image],
        2 * F * refs * per_facet * 3 * STRIP,
        smem=1,
    )
    parts = [served[0]] + [swap(served[k], "facet", k) for k in range(1, F)]
    est, msg = call(
        functools.partial(first_kernel, S, F, each, rows, F),
        [piece, message],
        [rx, uv_kernels[:, 0]] + parts,
        8 * refs * 2 * STRIP * STRIP,
    )
    image = start_image
    for iteration in range(ITERS):
        mine, other = spread(msg)
        if iteration + 1 < ITERS:
            est, msg = call(
                functools.partial(next_kernel, S, F, each, rows, step),
                [piece, message],
                [rx, uv_kernels[:, 0], est, mine, other],
                4 * refs * S * refs * STRIP,
            )
        (image,) = call(
            functools.partial(settle_kernel, refs, step),
            [jax.ShapeDtypeStruct(image.shape, F32)],
            [facet, image, mine, other],
            4 * per_facet * S * refs * STRIP,
            smem=1,
        )
    return image


def dense_device(start_image, visibilities, strip_index, live_counts, uv_kernels):
    def to_owner(x):
        x = lax.all_to_all(x, "chan", split_axis=1, concat_axis=0, tiled=True)
        return lax.all_to_all(x, "facet", split_axis=2, concat_axis=0, tiled=True)

    observed, picked_ids, live_now = map(to_owner, (visibilities, strip_index, live_counts))
    slot_count = observed.shape[0]
    chan_local, uv_local = uv_kernels.shape[:2]
    slab_rows, facet_width = start_image.shape
    full_width = facet_width * lax.axis_size("facet")
    strip_count = slab_rows * full_width // STRIP
    blocks = slot_count * chan_local * lax.axis_size("chan") * uv_local * lax.axis_size("facet")
    step_size = strip_count / (2.5 * blocks)
    lane_ids = jnp.arange(2 * VISB, dtype=I32) % VISB
    live_mask = lane_ids < live_now[..., None]
    flat_ids = picked_ids.reshape(-1)
    estimate = start_image
    for iteration in range(ITERS):
        full_sky = lax.all_gather(estimate.astype(BF16), "facet", axis=1, tiled=True)
        sky_strips = full_sky.reshape(strip_count, STRIP)
        gathered = sky_strips[picked_ids].reshape(slot_count, chan_local, uv_local, TERMS * STRIP)
        predicted = jnp.einsum("scup,cupq->scuq", gathered, uv_kernels, preferred_element_type=F32)
        residual = jnp.where(live_mask, predicted - observed.astype(F32), 0.0).astype(BF16)
        adjoint = jnp.einsum("scuq,cupq->scup", residual, uv_kernels, preferred_element_type=F32)
        gradient = jnp.zeros((strip_count, STRIP), F32).at[flat_ids].add(adjoint.reshape(-1, STRIP))
        gradient = gradient.reshape(slab_rows, full_width)
        facet_part = lax.psum_scatter(gradient, "facet", scatter_dimension=1, tiled=True)
        facet_sum = lax.psum(facet_part, "chan")
        descent = estimate - step_size * facet_sum
        estimate = jnp.maximum(descent - shrinkage, 0.0)
    return estimate


def on_device(start_image, visibilities, strip_index, live_counts, uv_kernels):
    C, F = lax.axis_size("chan"), lax.axis_size("facet")
    L, uv_local = uv_kernels.shape[:2]
    strips = start_image.size * F // STRIP
    sparse = (
        visibilities.shape[0] == 1
        and uv_local == 1
        and C & (C - 1) == 0
        and F & (F - 1) == 0
        and C > 1
        and C * F * L * TERMS == STRIP
        and 2 * L + 1 <= 8
        and 2 * F * L * TERMS + L <= STRIP
        and strips <= 64 * 256
        and start_image.shape[0] % TILE == 0
        and start_image.shape[1] % STRIP == 0
    )
    run = sparse_device if sparse else dense_device
    return run(start_image, visibilities, strip_index, live_counts, uv_kernels)


def solution(mesh):
    placed = (
        P(None, "facet"),
        P(("chan", "facet"), None, None, None),
        P(("chan", "facet"), None, None, None),
        P(("chan", "facet"), None, None),
        P("chan", "facet", None, None),
    )
    return jax.shard_map(
        on_device, mesh=mesh, in_specs=placed, out_specs=P(None, "facet"), check_vma=False
    )
```

```python
import functools

import jax
import jax.numpy as jnp
from jax import lax
from jax.experimental import pallas as pl
from jax.experimental.pallas import tpu as pltpu
from jax.sharding import PartitionSpec as P

STRIP = 128
VISB = 128
TERMS = 2
ITERS = 2
TILE = 8
EXTRA = 16
BLOCK = 16
LEVELS = 65535.0 / 3.0
LEAST = 119

shrinkage = 0.05
F32, BF16, I32, I16 = jnp.float32, jnp.bfloat16, jnp.int32, jnp.int16
VMEM_LIMIT = 48 * 1024 * 1024


def call(kernel, outs, args, flops, smem=0):
    spaces = [pl.BlockSpec(memory_space=pltpu.SMEM)] * smem
    spaces += [pl.BlockSpec(memory_space=pltpu.VMEM)] * (len(args) - smem)
    moved = sum(a.size * a.dtype.itemsize for a in list(args) + list(outs))
    return pl.pallas_call(
        kernel,
        out_shape=list(outs),
        in_specs=spaces,
        out_specs=[pl.BlockSpec(memory_space=pltpu.VMEM)] * len(outs),
        compiler_params=pltpu.CompilerParams(vmem_limit_bytes=VMEM_LIMIT),
        cost_estimate=pl.CostEstimate(flops=flops, bytes_accessed=moved, transcendentals=0),
    )(*args)


def split(x, parts):
    terms = []
    for _ in range(parts):
        term = x.astype(BF16)
        terms.append(term)
        x = x - term.astype(F32)
    return terms


def one_hot(hit):
    return jnp.where(hit, 1.0, 0.0).astype(BF16)


def iota(shape, dim):
    return lax.broadcasted_iota(I32, shape, dim)


def code_floats(x):
    size = jnp.abs(x)
    power = jnp.maximum(jnp.floor(jnp.log2(jnp.maximum(size, 1e-37))), -LEAST)
    code = (power + LEAST) * 128.0 + jnp.round(size * jnp.exp2(7.0 - power))
    return jnp.where(x < 0, -code, code).astype(I32)


def floats_of(code):
    size = jnp.abs(code)
    power = jnp.maximum((size >> 7) - 1, 0)
    lead = (size - power * 128).astype(F32)
    value = lead * jnp.exp2((power - (LEAST + 7)).astype(F32))
    return jnp.where(code < 0, -value, value).astype(BF16)


def halves(x):
    return jnp.concatenate([(x >> 6).astype(F32), (x & 63).astype(F32)], axis=1).astype(BF16)


def joined(x):
    return x[:, :STRIP] * 64.0 + x[:, STRIP:]


def tiled_strips(rows):
    height, width = rows.shape
    return jnp.concatenate(
        [
            rows[r : r + TILE, c : c + STRIP]
            for r in range(0, height, TILE)
            for c in range(0, width, STRIP)
        ],
        axis=0,
    )


def log2(n):
    return n.bit_length() - 1


def pack_kernel(C, F, L, place, image, seen, numbers, *outs):
    c, f = place[0], place[1]
    height, width = image.shape
    band = height // C
    wide = width // STRIP
    per_facet = height * wide
    piece = per_facet // C
    strips = tiled_strips(image[pl.ds(pl.multiple_of(c * band, TILE), band), :])
    share = (jnp.round(strips * LEVELS) - 32768.0).astype(I32).astype(I16)
    chips = C // 2
    size = chips * BLOCK
    rows = F * size
    row = iota((rows, 1), 0)
    k, j, i = row // size, (row // BLOCK) % chips, row % BLOCK
    uv = k ^ f
    channel = ((c >> 1) ^ j) * (2 * L) + (i >> 1)
    raw = numbers[...]
    across, column = raw >> log2(F * wide), raw & (F * wide - 1)
    strip = (
        (column >> log2(wide)) * per_facet
        + (across >> 3) * (wide * TILE)
        + (column & (wide - 1)) * TILE
        + (across & 7)
    )
    ids = jnp.where(iota(raw.shape, 0) < TERMS * F, strip, raw)
    is_seen = i < 4 * L
    pick = is_seen & (iota((rows, seen.shape[0]), 1) == channel * F + uv)
    both = jnp.dot(one_hot(pick), seen[...], preferred_element_type=F32)
    values = code_floats(jnp.where((i & 1) == 0, both[:, :VISB], both[:, VISB:]))
    pick = (i >= 4 * L) & (iota((rows, raw.shape[0]), 1) == (i - 4 * L) * F + uv)
    whole = joined(jnp.dot(one_hot(pick), halves(ids), preferred_element_type=F32))
    blocks = jnp.where(is_seen, values, whole.astype(I32)).astype(I16)
    for at in range(F):
        if at:
            outs[at][:piece] = share
            outs[at][piece:] = blocks[at * size : (at + 1) * size]
        else:
            outs[at][...] = blocks[:size]


def pass_kernel(F, piece, *refs):
    got, outs = refs[:F], refs[F:]
    for j, out in enumerate(outs):
        for k in range(1, F):
            out[(k - 1) * piece : k * piece] = got[k][:piece]
        for k in range(F):
            at = (F - 1) * piece + k * BLOCK
            first = (piece if k else 0) + j * BLOCK
            out[at : at + BLOCK] = got[k][first : first + BLOCK]


def first_kernel(C, F, L, place, image, kernels, mine, other, start_out, seen_out, scalars_out, msg):
    c, f = place[0], place[1]
    chips, slots = C // 2, C * F
    height, width = image.shape
    per_facet = height * width // STRIP
    piece = per_facet // C
    size = (F - 1) * piece + F * BLOCK
    tiles, shares = [], []
    for got in (mine, other):
        for q in range(chips):
            shares.append(got[q * size : q * size + (F - 1) * piece].astype(I32))
            tiles.append(got[q * size + (F - 1) * piece : (q + 1) * size].astype(I32))
    blocks = jnp.concatenate(tiles, axis=0)
    out = iota((4 * slots, 1), 0)
    source = (out % slots) * BLOCK + 2 * L * (c & 1) + out // slots
    pick = iota((4 * slots, slots * BLOCK), 1) == source
    seen = jnp.dot(one_hot(pick), floats_of(blocks), preferred_element_type=F32)
    out = iota((3 * slots, 1), 0)
    source = (out % slots) * BLOCK + 4 * L + out // slots
    pick = iota((3 * slots, slots * BLOCK), 1) == source
    whole = joined(jnp.dot(one_hot(pick), halves(blocks), preferred_element_type=F32))
    lane = iota((slots, STRIP), 1)
    scalars = jnp.zeros((slots, STRIP), F32)
    for kind in range(3):
        for ch in range(L):
            of_kind = whole[kind * slots : (kind + 1) * slots]
            value = jnp.sum(jnp.where(lane == c * L + ch, of_kind, 0.0), axis=1, keepdims=True)
            at = L * TERMS + ch if kind == TERMS else ch * TERMS + kind
            scalars = jnp.where(lane == at, value, scalars)
    col = ref_column(scalars, L)
    facet, local = col >> log2(per_facet), col & (per_facet - 1)
    k, d = facet ^ f, (local >> log2(piece)) ^ c
    turn = ((d & 1) * chips + (d >> 1)) * (F - 1) + k - 1
    place_of = jnp.where(k == 0, local, per_facet + turn * piece + (local & (piece - 1)))
    own = jnp.round(tiled_strips(image) * LEVELS)
    levels = jnp.concatenate([own] + [s.astype(F32) + 32768.0 for s in shares], axis=0)
    table = jnp.concatenate(split(levels, 2), axis=1)
    pick = iota((col.shape[0], table.shape[0]), 1) == place_of
    both = jnp.dot(one_hot(pick), table, preferred_element_type=F32)
    est = (both[:, :STRIP] + both[:, STRIP:]) * (1.0 / LEVELS)
    start_out[...] = est
    seen_out[...] = seen.astype(BF16)
    scalars_out[...] = scalars
    encode(measure(est, seen, scalars, kernels, L), col, msg)


def ref_column(scalars, L):
    cols = [scalars[:, i : i + 1] for i in range(L * TERMS)]
    return jnp.concatenate(cols, axis=0).astype(I32)


def measure(est, seen, scalars, kernels, L):
    slots = scalars.shape[0]
    adjoints = []
    for ch in range(L):
        a, b, end = (ch * TERMS + i for i in range(3))
        sky = jnp.concatenate(
            [est[a * slots : b * slots], est[b * slots : end * slots]], axis=1
        ).astype(BF16)
        observed = jnp.concatenate(
            [seen[a * slots : b * slots], seen[b * slots : end * slots]], axis=1
        )
        predicted = jnp.dot(sky, kernels[ch], preferred_element_type=F32)
        live = scalars[:, L * TERMS + ch : L * TERMS + ch + 1].astype(I32)
        lane = iota(predicted.shape, 1) & (VISB - 1)
        residual = jnp.where(lane < live, predicted - observed, 0.0).astype(BF16)
        adjoint = lax.dot_general(
            residual, kernels[ch], (((1,), (1,)), ((), ())), preferred_element_type=F32
        )
        adjoints += [adjoint[:, :STRIP], adjoint[:, STRIP:]]
    return jnp.concatenate(adjoints, axis=0)


def encode(adjoint, col, msg):
    refs = adjoint.shape[0]
    top = jnp.max(jnp.abs(adjoint), axis=(0, 1), keepdims=True)
    exponent = jnp.ceil(jnp.log2(jnp.maximum(top, 1e-30) * (1.0 / 32000.0)))
    code = jnp.round(adjoint * jnp.exp2(-exponent))
    msg[:refs] = code.astype(I32).astype(I16)
    eye = iota((refs, STRIP), 0) == iota((refs, STRIP), 1)
    ids = jnp.sum(jnp.where(eye, col.astype(F32), 0.0), axis=0, keepdims=True)
    row = iota((EXTRA, STRIP), 0)
    extra = jnp.where(row == 0, ids, jnp.where(row == 1, exponent, 0.0))
    msg[refs:] = extra.astype(I32).astype(I16)


def decode(block):
    ids, rows = [], []
    size = STRIP + EXTRA
    for at in range(0, block.shape[0], size):
        extra = block[at + STRIP : at + size].astype(I32)
        ids.append(extra[0:1])
        scale = jnp.exp2(extra[1:2].astype(F32))
        value = block[at : at + STRIP].astype(I32).astype(F32) * scale
        rows.append(jnp.concatenate(split(value, 2), axis=1))
    return jnp.concatenate(ids, axis=1), jnp.concatenate(rows, axis=0)


def summed(ids, values, strips):
    both = jnp.dot(one_hot(ids == strips), values, preferred_element_type=F32)
    return both[:, :STRIP] + both[:, STRIP:]


def part_kernel(L, scalars, block, out):
    out[...] = summed(*decode(block), ref_column(scalars[...], L))


def next_kernel(L, step, scalars_in, seen, kernels, est_in, part, block, msg):
    scalars = scalars_in[...]
    col = ref_column(scalars, L)
    gradient = part[...] + summed(*decode(block), col)
    est = jnp.maximum(est_in[...] - step * gradient - shrinkage, 0.0)
    encode(measure(est, seen[...].astype(F32), scalars, kernels, L), col, msg)


def facet_part_kernel(place, block, out):
    ids, values = decode(block)
    count = out.shape[0]
    chunk = min(256, count)
    for at in range(0, count, chunk):
        out[at : at + chunk] = summed(ids, values, iota((chunk, 1), 0) + (place[1] * count + at))


def settle_kernel(step, place, image, part, block, out):
    ids, values = decode(block)
    height, width = image.shape
    count = part.shape[0]
    per_band = width // STRIP * TILE
    chunk = min(256, count)
    for at in range(0, count, chunk):
        strips = iota((chunk, 1), 0) + (place[1] * count + at)
        gradient = part[at : at + chunk] + summed(ids, values, strips)
        for t in range(0, chunk, TILE):
            r = (at + t) // per_band * TILE
            c = (at + t) % per_band // TILE * STRIP
            old = image[r : r + TILE, c : c + STRIP]
            out[r : r + TILE, c : c + STRIP] = jnp.maximum(
                old - step * gradient[t : t + TILE] - shrinkage, 0.0
            )


def swap(x, axis, k):
    return lax.ppermute(x, axis, [(i, i ^ k) for i in range(lax.axis_size(axis))])


def sparse_device(start_image, visibilities, strip_index, live_counts, uv_kernels):
    C, F = lax.axis_size("chan"), lax.axis_size("facet")
    L = uv_kernels.shape[0]
    refs = C * F * L * TERMS
    per_facet = start_image.size // STRIP
    piece = per_facet // C
    chips = C // 2
    step = float(per_facet * F / (2.5 * C * F * (L * C) * F))
    place = jnp.stack([lax.axis_index("chan"), lax.axis_index("facet")]).astype(I32)
    kernels = uv_kernels[:, 0]

    numbers = jnp.concatenate(
        [strip_index[0].transpose(2, 1, 0).reshape(TERMS * F, L * C), live_counts[0].T], axis=0
    )
    numbers = jnp.pad(numbers, ((0, 16 - numbers.shape[0]), (0, STRIP - numbers.shape[1])))
    seen = visibilities.reshape(L * C * F, 2 * VISB)
    blocks = jax.ShapeDtypeStruct((chips * BLOCK, STRIP), I16)
    both = jax.ShapeDtypeStruct((piece + chips * BLOCK, STRIP), I16)
    packed = call(
        functools.partial(pack_kernel, C, F, L),
        [blocks] + [both] * (F - 1),
        [place, start_image, seen, numbers],
        10**8,
        smem=1,
    )
    got = [packed[0]] + [swap(packed[k], "facet", k) for k in range(1, F)]
    passed = call(
        functools.partial(pass_kernel, F, piece),
        [jax.ShapeDtypeStruct(((F - 1) * piece + F * BLOCK, STRIP), I16)] * chips,
        got,
        10**6,
    )
    mine = jnp.concatenate(
        [passed[0]] + [swap(passed[j], "chan", 2 * j) for j in range(1, chips)], axis=0
    )
    other = swap(mine, "chan", 1)

    at_refs = jax.ShapeDtypeStruct((refs, STRIP), F32)
    message = jax.ShapeDtypeStruct((refs + EXTRA, STRIP), I16)
    facet_strips = jax.ShapeDtypeStruct((per_facet, STRIP), F32)
    est, observed, scalars, msg = call(
        functools.partial(first_kernel, C, F, L),
        [
            at_refs,
            jax.ShapeDtypeStruct((refs, STRIP), BF16),
            jax.ShapeDtypeStruct((C * F, STRIP), F32),
            message,
        ],
        [place, start_image, kernels, mine, other],
        5 * 10**8,
        smem=1,
    )

    image = start_image
    held = None
    for iteration in range(ITERS):
        last = iteration + 1 == ITERS
        near = jnp.concatenate([msg] + [swap(msg, "facet", k) for k in range(1, F)], axis=0)
        if held is not None:
            image = settle(step, place, image, *held)
            near, image = lax.optimization_barrier((near, image))
        mine = jnp.concatenate([near] + [swap(near, "chan", 2 * j) for j in range(1, chips)], axis=0)
        other = swap(mine, "chan", 1)
        if not last:
            (part,) = call(
                functools.partial(part_kernel, L), [at_refs], [scalars, mine], 3 * 10**8
            )
            (msg,) = call(
                functools.partial(next_kernel, L, step),
                [message],
                [scalars, observed, kernels, est, part, other],
                3 * 10**8,
            )
        (part,) = call(facet_part_kernel, [facet_strips], [place, mine], 2 * 10**9, smem=1)
        held = part, other
    return settle(step, place, image, *held)


def settle(step, place, image, part, other):
    (image,) = call(
        functools.partial(settle_kernel, step),
        [jax.ShapeDtypeStruct(image.shape, F32)],
        [place, image, part, other],
        2 * 10**9,
        smem=1,
    )
    return image


def dense_device(start_image, visibilities, strip_index, live_counts, uv_kernels):
    def to_owner(x):
        x = lax.all_to_all(x, "chan", split_axis=1, concat_axis=0, tiled=True)
        return lax.all_to_all(x, "facet", split_axis=2, concat_axis=0, tiled=True)

    observed, picked_ids, live_now = map(to_owner, (visibilities, strip_index, live_counts))
    slot_count = observed.shape[0]
    chan_local, uv_local = uv_kernels.shape[:2]
    slab_rows, facet_width = start_image.shape
    full_width = facet_width * lax.axis_size("facet")
    strip_count = slab_rows * full_width // STRIP
    blocks = slot_count * chan_local * lax.axis_size("chan") * uv_local * lax.axis_size("facet")
    step_size = strip_count / (2.5 * blocks)
    lane_ids = jnp.arange(2 * VISB, dtype=I32) % VISB
    live_mask = lane_ids < live_now[..., None]
    flat_ids = picked_ids.reshape(-1)
    estimate = start_image
    for iteration in range(ITERS):
        full_sky = lax.all_gather(estimate.astype(BF16), "facet", axis=1, tiled=True)
        sky_strips = full_sky.reshape(strip_count, STRIP)
        gathered = sky_strips[picked_ids].reshape(slot_count, chan_local, uv_local, TERMS * STRIP)
        predicted = jnp.einsum("scup,cupq->scuq", gathered, uv_kernels, preferred_element_type=F32)
        residual = jnp.where(live_mask, predicted - observed.astype(F32), 0.0).astype(BF16)
        adjoint = jnp.einsum("scuq,cupq->scup", residual, uv_kernels, preferred_element_type=F32)
        gradient = jnp.zeros((strip_count, STRIP), F32).at[flat_ids].add(adjoint.reshape(-1, STRIP))
        gradient = gradient.reshape(slab_rows, full_width)
        facet_part = lax.psum_scatter(gradient, "facet", scatter_dimension=1, tiled=True)
        facet_sum = lax.psum(facet_part, "chan")
        descent = estimate - step_size * facet_sum
        estimate = jnp.maximum(descent - shrinkage, 0.0)
    return estimate


def on_device(start_image, visibilities, strip_index, live_counts, uv_kernels):
    C, F = lax.axis_size("chan"), lax.axis_size("facet")
    L, uv_local = uv_kernels.shape[:2]
    strips = start_image.size * F // STRIP
    sparse = (
        visibilities.shape[0] == 1
        and uv_local == 1
        and C & (C - 1) == 0
        and F & (F - 1) == 0
        and C >= 4
        and F >= 2
        and C * F * L * TERMS == STRIP
        and 4 * L + TERMS + 1 <= BLOCK
        and (TERMS + 1) * F <= 16
        and L * C <= STRIP
        and strips <= 64 * 256
        and strips & (strips - 1) == 0
        and start_image.shape[0] % (C * TILE) == 0
        and start_image.shape[1] % STRIP == 0
        and start_image.size // STRIP // C % 16 == 0
    )
    run = sparse_device if sparse else dense_device
    return run(start_image, visibilities, strip_index, live_counts, uv_kernels)


def solution(mesh):
    placed = (
        P(None, "facet"),
        P(("chan", "facet"), None, None, None),
        P(("chan", "facet"), None, None, None),
        P(("chan", "facet"), None, None),
        P("chan", "facet", None, None),
    )
    return jax.shard_map(
        on_device, mesh=mesh, in_specs=placed, out_specs=P(None, "facet"), check_vma=False
    )
```

```python
import functools

import jax
import jax.numpy as jnp
from jax import lax
from jax.experimental import pallas as pl
from jax.experimental.pallas import tpu as pltpu
from jax.sharding import PartitionSpec as P

STRIP = 128
VISB = 128
TERMS = 2
ITERS = 2
TILE = 8
EXTRA = 16
BLOCK = 16
LEVELS = 65535.0 / 3.0
LEAST = 119

shrinkage = 0.05
F32, BF16, I32, I16 = jnp.float32, jnp.bfloat16, jnp.int32, jnp.int16
VMEM_LIMIT = 48 * 1024 * 1024


def call(kernel, outs, args, flops, smem=0, hbm=0, scratch=()):
    spaces = [pl.BlockSpec(memory_space=pltpu.SMEM)] * smem
    spaces += [pl.BlockSpec(memory_space=pltpu.HBM)] * hbm
    spaces += [pl.BlockSpec(memory_space=pltpu.VMEM)] * (len(args) - smem - hbm)
    moved = sum(a.size * a.dtype.itemsize for a in list(args) + list(outs))
    args = list(args)
    for i in range(smem, smem + hbm):
        args[i] = pltpu.with_memory_space_constraint(args[i], pltpu.HBM)
    return pl.pallas_call(
        kernel,
        out_shape=list(outs),
        in_specs=spaces,
        out_specs=[pl.BlockSpec(memory_space=pltpu.VMEM)] * len(outs),
        scratch_shapes=list(scratch),
        compiler_params=pltpu.CompilerParams(vmem_limit_bytes=VMEM_LIMIT),
        cost_estimate=pl.CostEstimate(flops=flops, bytes_accessed=moved, transcendentals=0),
    )(*args)


def split(x, parts):
    terms = []
    for _ in range(parts):
        term = x.astype(BF16)
        terms.append(term)
        x = x - term.astype(F32)
    return terms


def one_hot(hit):
    return jnp.where(hit, 1.0, 0.0).astype(BF16)


def iota(shape, dim):
    return lax.broadcasted_iota(I32, shape, dim)


def code_floats(x):
    size = jnp.abs(x)
    power = jnp.maximum(jnp.floor(jnp.log2(jnp.maximum(size, 1e-37))), -LEAST)
    code = (power + LEAST) * 128.0 + jnp.round(size * jnp.exp2(7.0 - power))
    return jnp.where(x < 0, -code, code).astype(I32)


def floats_of(code):
    size = jnp.abs(code)
    power = jnp.maximum((size >> 7) - 1, 0)
    lead = (size - power * 128).astype(F32)
    value = lead * jnp.exp2((power - (LEAST + 7)).astype(F32))
    return jnp.where(code < 0, -value, value).astype(BF16)


def halves(x):
    return jnp.concatenate([(x >> 6).astype(F32), (x & 63).astype(F32)], axis=1).astype(BF16)


def joined(x):
    return x[:, :STRIP] * 64.0 + x[:, STRIP:]


def tiled_strips(rows):
    height, width = rows.shape
    return jnp.concatenate(
        [
            rows[r : r + TILE, c : c + STRIP]
            for r in range(0, height, TILE)
            for c in range(0, width, STRIP)
        ],
        axis=0,
    )


def log2(n):
    return n.bit_length() - 1


def pack_kernel(C, F, L, place, image, seen, terms, counts, *refs):
    outs, (band_in, seen_in, terms_in, counts_in, row_in, sems) = refs[:F], refs[F:]
    c, f = place[0], place[1]
    height, width = image.shape
    band = height // C
    wide = width // STRIP
    per_facet = height * wide
    piece = per_facet // C
    mine = image.at[pl.ds(pl.multiple_of(c * band, TILE), band), :]
    copies = [
        pltpu.make_async_copy(source, target, sems.at[i])
        for i, (source, target) in enumerate(
            ((mine, band_in), (seen, seen_in), (terms, terms_in), (counts, counts_in))
        )
    ]
    for copy in copies:
        copy.start()
    chips = C // 2
    size = chips * BLOCK
    rows = F * size
    row = iota((rows, 1), 0)
    k, j, i = row // size, (row // BLOCK) % chips, row % BLOCK
    channel = ((c >> 1) ^ j) * (2 * L) + (i >> 1)
    is_seen = i < 4 * L
    pick = is_seen & (iota((rows, L * C * F), 1) == channel * F + (k ^ f))
    row_in[...] = jnp.zeros(row_in.shape, I32)
    for copy in copies:
        copy.wait()
    strips = tiled_strips(band_in[...])
    share = (jnp.round(strips * LEVELS) - 32768.0).astype(I32).astype(I16)
    raw = terms_in[...]
    across, column = raw >> log2(F * wide), raw & (F * wide - 1)
    terms_in[...] = (
        (column >> log2(wide)) * per_facet
        + (across >> 3) * (wide * TILE)
        + (column & (wide - 1)) * TILE
        + (across & 7)
    )
    for at in range(F):
        for term in range(TERMS):
            row_in[at * TILE + term : at * TILE + term + 1, : L * C] = terms_in[at ^ f, term : term + 1]
        row_in[at * TILE + TERMS : at * TILE + TERMS + 1, : L * C] = counts_in[pl.ds(at ^ f, 1)]
    by_channel = jnp.concatenate([seen_in[n] for n in range(L * C)], axis=0)
    both = jnp.dot(one_hot(pick), by_channel, preferred_element_type=F32)
    values = code_floats(jnp.where((i & 1) == 0, both[:, :VISB], both[:, VISB:]))
    whole = jnp.concatenate(
        [part for at in range(F) for part in [row_in[at * TILE : (at + 1) * TILE]] * (2 * chips)],
        axis=0,
    )
    blocks = jnp.where(is_seen, values, whole).astype(I16)
    for at in range(F):
        if at:
            outs[at][:piece] = share
            outs[at][piece:] = blocks[at * size : (at + 1) * size]
        else:
            outs[at][...] = blocks[:size]


def pass_kernel(F, piece, *refs):
    got, outs = refs[:F][::-1], refs[F:]
    for j, out in enumerate(outs):
        for k in range(1, F):
            out[(k - 1) * piece : k * piece] = got[k][:piece]
        for k in range(F):
            at = (F - 1) * piece + k * BLOCK
            first = (piece if k else 0) + j * BLOCK
            out[at : at + BLOCK] = got[k][first : first + BLOCK]


def first_kernel(C, F, L, place, image, kernels, mine, other, start_out, seen_out, scalars_out, msg):
    c, f = place[0], place[1]
    chips, slots = C // 2, C * F
    height, width = image.shape
    per_facet = height * width // STRIP
    piece = per_facet // C
    size = (F - 1) * piece + F * BLOCK
    tiles, shares = [], []
    for got in (mine, other):
        for q in range(chips):
            shares.append(got[q * size : q * size + (F - 1) * piece].astype(I32))
            tiles.append(got[q * size + (F - 1) * piece : (q + 1) * size].astype(I32))
    blocks = jnp.concatenate(tiles, axis=0)
    out = iota((4 * slots, 1), 0)
    source = (out % slots) * BLOCK + 2 * L * (c & 1) + out // slots
    pick = iota((4 * slots, slots * BLOCK), 1) == source
    seen = jnp.dot(one_hot(pick), floats_of(blocks), preferred_element_type=F32)
    out = iota((3 * slots, 1), 0)
    source = (out % slots) * BLOCK + 4 * L + out // slots
    pick = iota((3 * slots, slots * BLOCK), 1) == source
    whole = joined(jnp.dot(one_hot(pick), halves(blocks), preferred_element_type=F32))
    lane = iota((slots, STRIP), 1)
    scalars = jnp.zeros((slots, STRIP), F32)
    for kind in range(3):
        for ch in range(L):
            of_kind = whole[kind * slots : (kind + 1) * slots]
            value = jnp.sum(jnp.where(lane == c * L + ch, of_kind, 0.0), axis=1, keepdims=True)
            at = L * TERMS + ch if kind == TERMS else ch * TERMS + kind
            scalars = jnp.where(lane == at, value, scalars)
    col = ref_column(scalars, L)
    facet, local = col >> log2(per_facet), col & (per_facet - 1)
    k, d = facet ^ f, (local >> log2(piece)) ^ c
    turn = ((d & 1) * chips + (d >> 1)) * (F - 1) + k - 1
    place_of = jnp.where(k == 0, local, per_facet + turn * piece + (local & (piece - 1)))
    own = jnp.round(tiled_strips(image) * LEVELS)
    levels = jnp.concatenate([own] + [s.astype(F32) + 32768.0 for s in shares], axis=0)
    table = jnp.concatenate(split(levels, 2), axis=1)
    pick = iota((col.shape[0], table.shape[0]), 1) == place_of
    both = jnp.dot(one_hot(pick), table, preferred_element_type=F32)
    est = (both[:, :STRIP] + both[:, STRIP:]) * (1.0 / LEVELS)
    start_out[...] = est
    seen_out[...] = seen.astype(BF16)
    scalars_out[...] = scalars
    encode(measure(est, seen, scalars, kernels, L), col, msg)


def ref_column(scalars, L):
    cols = [scalars[:, i : i + 1] for i in range(L * TERMS)]
    return jnp.concatenate(cols, axis=0).astype(I32)


def measure(est, seen, scalars, kernels, L):
    slots = scalars.shape[0]
    adjoints = []
    for ch in range(L):
        a, b, end = (ch * TERMS + i for i in range(3))
        sky = jnp.concatenate(
            [est[a * slots : b * slots], est[b * slots : end * slots]], axis=1
        ).astype(BF16)
        observed = jnp.concatenate(
            [seen[a * slots : b * slots], seen[b * slots : end * slots]], axis=1
        )
        predicted = jnp.dot(sky, kernels[ch], preferred_element_type=F32)
        live = scalars[:, L * TERMS + ch : L * TERMS + ch + 1].astype(I32)
        lane = iota(predicted.shape, 1) & (VISB - 1)
        residual = jnp.where(lane < live, predicted - observed, 0.0).astype(BF16)
        adjoint = lax.dot_general(
            residual, kernels[ch], (((1,), (1,)), ((), ())), preferred_element_type=F32
        )
        adjoints += [adjoint[:, :STRIP], adjoint[:, STRIP:]]
    return jnp.concatenate(adjoints, axis=0)


def encode(adjoint, col, msg):
    refs = adjoint.shape[0]
    top = jnp.max(jnp.abs(adjoint), axis=(0, 1), keepdims=True)
    exponent = jnp.ceil(jnp.log2(jnp.maximum(top, 1e-30) * (1.0 / 32000.0)))
    code = jnp.round(adjoint * jnp.exp2(-exponent))
    msg[:refs] = code.astype(I32).astype(I16)
    eye = iota((refs, STRIP), 0) == iota((refs, STRIP), 1)
    ids = jnp.sum(jnp.where(eye, col.astype(F32), 0.0), axis=0, keepdims=True)
    row = iota((EXTRA, STRIP), 0)
    extra = jnp.where(row == 0, ids, jnp.where(row == 1, exponent, 0.0))
    msg[refs:] = extra.astype(I32).astype(I16)


def decode(block):
    ids, rows = [], []
    size = STRIP + EXTRA
    for at in range(0, block.shape[0], size):
        extra = block[at + STRIP : at + size].astype(I32)
        ids.append(extra[0:1])
        scale = jnp.exp2(extra[1:2].astype(F32))
        value = block[at : at + STRIP].astype(I32).astype(F32) * scale
        rows.append(jnp.concatenate(split(value, 2), axis=1))
    return jnp.concatenate(ids, axis=1), jnp.concatenate(rows, axis=0)


def summed(ids, values, strips):
    both = jnp.dot(one_hot(ids == strips), values, preferred_element_type=F32)
    return both[:, :STRIP] + both[:, STRIP:]


def part_kernel(L, scalars, block, out):
    out[...] = summed(*decode(block), ref_column(scalars[...], L))


def next_kernel(L, step, scalars_in, seen, kernels, est_in, part, block, msg):
    scalars = scalars_in[...]
    col = ref_column(scalars, L)
    gradient = part[...] + summed(*decode(block), col)
    est = jnp.maximum(est_in[...] - step * gradient - shrinkage, 0.0)
    encode(measure(est, seen[...].astype(F32), scalars, kernels, L), col, msg)


def facet_part_kernel(place, block, out):
    ids, values = decode(block)
    count = out.shape[0]
    chunk = min(256, count)
    for at in range(0, count, chunk):
        out[at : at + chunk] = summed(ids, values, iota((chunk, 1), 0) + (place[1] * count + at))


def settle_kernel(step, place, image, part, block, out):
    ids, values = decode(block)
    height, width = image.shape
    count = part.shape[0]
    per_band = width // STRIP * TILE
    chunk = min(256, count)
    for at in range(0, count, chunk):
        strips = iota((chunk, 1), 0) + (place[1] * count + at)
        gradient = part[at : at + chunk] + summed(ids, values, strips)
        for t in range(0, chunk, TILE):
            r = (at + t) // per_band * TILE
            c = (at + t) % per_band // TILE * STRIP
            old = image[r : r + TILE, c : c + STRIP]
            out[r : r + TILE, c : c + STRIP] = jnp.maximum(
                old - step * gradient[t : t + TILE] - shrinkage, 0.0
            )


def swap(x, axis, k):
    return lax.ppermute(x, axis, [(i, i ^ k) for i in range(lax.axis_size(axis))])


def sparse_device(start_image, visibilities, strip_index, live_counts, uv_kernels):
    C, F = lax.axis_size("chan"), lax.axis_size("facet")
    L = uv_kernels.shape[0]
    refs = C * F * L * TERMS
    per_facet = start_image.size // STRIP
    piece = per_facet // C
    chips = C // 2
    step = float(per_facet * F / (2.5 * C * F * (L * C) * F))
    place = jnp.stack([lax.axis_index("chan"), lax.axis_index("facet")]).astype(I32)
    kernels = uv_kernels[:, 0]

    blocks = jax.ShapeDtypeStruct((chips * BLOCK, STRIP), I16)
    both = jax.ShapeDtypeStruct((piece + chips * BLOCK, STRIP), I16)
    packed = call(
        functools.partial(pack_kernel, C, F, L),
        [blocks] + [both] * (F - 1),
        [
            place,
            start_image,
            visibilities[0],
            strip_index[0].transpose(1, 2, 0),
            live_counts[0].T,
        ],
        10**8,
        smem=1,
        hbm=4,
        scratch=[
            pltpu.VMEM((start_image.shape[0] // C, start_image.shape[1]), F32),
            pltpu.VMEM(visibilities.shape[1:], BF16),
            pltpu.VMEM((F, TERMS, L * C), I32),
            pltpu.VMEM((F, L * C), I32),
            pltpu.VMEM((F * TILE, STRIP), I32),
            pltpu.SemaphoreType.DMA((4,)),
        ],
    )
    got = [packed[0]] + [swap(packed[k], "facet", k) for k in range(F - 1, 0, -1)][::-1]
    passed = call(
        functools.partial(pass_kernel, F, piece),
        [jax.ShapeDtypeStruct(((F - 1) * piece + F * BLOCK, STRIP), I16)] * chips,
        got[::-1],
        10**6,
    )
    mine = jnp.concatenate(
        [passed[0]] + [swap(passed[j], "chan", 2 * j) for j in range(1, chips)], axis=0
    )
    other = swap(mine, "chan", 1)

    at_refs = jax.ShapeDtypeStruct((refs, STRIP), F32)
    message = jax.ShapeDtypeStruct((refs + EXTRA, STRIP), I16)
    facet_strips = jax.ShapeDtypeStruct((per_facet, STRIP), F32)
    est, observed, scalars, msg = call(
        functools.partial(first_kernel, C, F, L),
        [
            at_refs,
            jax.ShapeDtypeStruct((refs, STRIP), BF16),
            jax.ShapeDtypeStruct((C * F, STRIP), F32),
            message,
        ],
        [place, start_image, kernels, mine, other],
        5 * 10**8,
        smem=1,
    )

    image = start_image
    held = None
    for iteration in range(ITERS):
        last = iteration + 1 == ITERS
        near = jnp.concatenate([msg] + [swap(msg, "facet", k) for k in range(1, F)], axis=0)
        if held is not None:
            image = settle(step, place, image, *held)
            near, image = lax.optimization_barrier((near, image))
        mine = jnp.concatenate([near] + [swap(near, "chan", 2 * j) for j in range(chips - 1, 0, -1)], axis=0)
        other = swap(mine, "chan", 1)
        if not last:
            (part,) = call(
                functools.partial(part_kernel, L), [at_refs], [scalars, mine], 3 * 10**8
            )
            (msg,) = call(
                functools.partial(next_kernel, L, step),
                [message],
                [scalars, observed, kernels, est, part, other],
                3 * 10**8,
            )
        (part,) = call(facet_part_kernel, [facet_strips], [place, mine], 2 * 10**9, smem=1)
        held = part, other
    return settle(step, place, image, *held)


def settle(step, place, image, part, other):
    (image,) = call(
        functools.partial(settle_kernel, step),
        [jax.ShapeDtypeStruct(image.shape, F32)],
        [place, image, part, other],
        2 * 10**9,
        smem=1,
    )
    return image


def dense_device(start_image, visibilities, strip_index, live_counts, uv_kernels):
    def to_owner(x):
        x = lax.all_to_all(x, "chan", split_axis=1, concat_axis=0, tiled=True)
        return lax.all_to_all(x, "facet", split_axis=2, concat_axis=0, tiled=True)

    observed, picked_ids, live_now = map(to_owner, (visibilities, strip_index, live_counts))
    slot_count = observed.shape[0]
    chan_local, uv_local = uv_kernels.shape[:2]
    slab_rows, facet_width = start_image.shape
    full_width = facet_width * lax.axis_size("facet")
    strip_count = slab_rows * full_width // STRIP
    blocks = slot_count * chan_local * lax.axis_size("chan") * uv_local * lax.axis_size("facet")
    step_size = strip_count / (2.5 * blocks)
    lane_ids = jnp.arange(2 * VISB, dtype=I32) % VISB
    live_mask = lane_ids < live_now[..., None]
    flat_ids = picked_ids.reshape(-1)
    estimate = start_image
    for iteration in range(ITERS):
        full_sky = lax.all_gather(estimate.astype(BF16), "facet", axis=1, tiled=True)
        sky_strips = full_sky.reshape(strip_count, STRIP)
        gathered = sky_strips[picked_ids].reshape(slot_count, chan_local, uv_local, TERMS * STRIP)
        predicted = jnp.einsum("scup,cupq->scuq", gathered, uv_kernels, preferred_element_type=F32)
        residual = jnp.where(live_mask, predicted - observed.astype(F32), 0.0).astype(BF16)
        adjoint = jnp.einsum("scuq,cupq->scup", residual, uv_kernels, preferred_element_type=F32)
        gradient = jnp.zeros((strip_count, STRIP), F32).at[flat_ids].add(adjoint.reshape(-1, STRIP))
        gradient = gradient.reshape(slab_rows, full_width)
        facet_part = lax.psum_scatter(gradient, "facet", scatter_dimension=1, tiled=True)
        facet_sum = lax.psum(facet_part, "chan")
        descent = estimate - step_size * facet_sum
        estimate = jnp.maximum(descent - shrinkage, 0.0)
    return estimate


def on_device(start_image, visibilities, strip_index, live_counts, uv_kernels):
    C, F = lax.axis_size("chan"), lax.axis_size("facet")
    L, uv_local = uv_kernels.shape[:2]
    strips = start_image.size * F // STRIP
    sparse = (
        visibilities.shape[0] == 1
        and uv_local == 1
        and C & (C - 1) == 0
        and F & (F - 1) == 0
        and C >= 4
        and F >= 2
        and C * F * L * TERMS == STRIP
        and 4 * L + TERMS + 1 <= BLOCK
        and 4 * L == TILE
        and L * C <= STRIP
        and strips <= 64 * 256
        and strips & (strips - 1) == 0
        and start_image.shape[0] % (C * TILE) == 0
        and start_image.shape[1] % STRIP == 0
        and start_image.size // STRIP // C % 16 == 0
    )
    run = sparse_device if sparse else dense_device
    return run(start_image, visibilities, strip_index, live_counts, uv_kernels)


def solution(mesh):
    placed = (
        P(None, "facet"),
        P(("chan", "facet"), None, None, None),
        P(("chan", "facet"), None, None, None),
        P(("chan", "facet"), None, None),
        P("chan", "facet", None, None),
    )
    return jax.shard_map(
        on_device, mesh=mesh, in_specs=placed, out_specs=P(None, "facet"), check_vma=False
    )
```

```python
import functools

import jax
import jax.numpy as jnp
from jax import lax
from jax.experimental import pallas as pl
from jax.experimental.pallas import tpu as pltpu
from jax.sharding import PartitionSpec as P

STRIP = 128
VISB = 128
TERMS = 2
ITERS = 2
TILE = 8
EXTRA = 16
BLOCK = 16
PART = 64
FINE = 32
FLOOR = 10
LEAST = 119

shrinkage = 0.05
F32, BF16, I32, I16 = jnp.float32, jnp.bfloat16, jnp.int32, jnp.int16
VMEM_LIMIT = 48 * 1024 * 1024


def call(kernel, outs, args, flops, smem=0, hbm=0, scratch=(), scalars=0):
    spaces = [pl.BlockSpec(memory_space=pltpu.SMEM)] * smem
    spaces += [pl.BlockSpec(memory_space=pltpu.HBM)] * hbm
    spaces += [pl.BlockSpec(memory_space=pltpu.VMEM)] * (len(args) - smem - hbm)
    moved = sum(a.size * a.dtype.itemsize for a in list(args) + list(outs))
    args = list(args)
    for i in range(smem, smem + hbm):
        args[i] = pltpu.with_memory_space_constraint(args[i], pltpu.HBM)
    return pl.pallas_call(
        kernel,
        out_shape=list(outs),
        in_specs=spaces,
        out_specs=[pl.BlockSpec(memory_space=pltpu.VMEM)] * (len(outs) - scalars)
        + [pl.BlockSpec(memory_space=pltpu.SMEM)] * scalars,
        scratch_shapes=list(scratch),
        compiler_params=pltpu.CompilerParams(vmem_limit_bytes=VMEM_LIMIT),
        cost_estimate=pl.CostEstimate(flops=flops, bytes_accessed=moved, transcendentals=0),
    )(*args)


def split(x, parts):
    terms = []
    for _ in range(parts):
        term = x.astype(BF16)
        terms.append(term)
        x = x - term.astype(F32)
    return terms


def one_hot(hit):
    return jnp.where(hit, 1.0, 0.0).astype(BF16)


def iota(shape, dim):
    return lax.broadcasted_iota(I32, shape, dim)


def code_floats(x):
    size = jnp.abs(x)
    power = jnp.maximum(jnp.floor(jnp.log2(jnp.maximum(size, 1e-37))), -LEAST)
    code = (power + LEAST) * 128.0 + jnp.round(size * jnp.exp2(7.0 - power))
    return jnp.where(x < 0, -code, code).astype(I32)


def code_levels(x):
    near = x.astype(BF16).astype(F32)
    power = jnp.maximum(jnp.floor(jnp.log2(jnp.maximum(near, 1e-37))), -FLOOR)
    unit = jnp.exp2(power - 7.0)
    lead = jnp.round(near / unit)
    step = jnp.round(((x - lead * unit) / unit + 0.5) * (FINE - 1))
    step = jnp.clip(step, 0.0, FINE - 1)
    code = ((power + FLOOR) * 128.0 + lead) * FINE + step - 32768.0
    return code.astype(I32).astype(I16)


def levels_of(code):
    level = code >> log2(FINE)
    power = jnp.maximum((level >> 7) - 1, 0)
    unit = jnp.exp2((power - (FLOOR + 7)).astype(F32))
    near = ((level - power * 128).astype(F32) * unit).astype(BF16).astype(F32)
    step = (code & (FINE - 1)).astype(F32)
    return near, near + (step * (1.0 / (FINE - 1)) - 0.5) * unit


def floats_of(code):
    size = jnp.abs(code)
    power = jnp.maximum((size >> 7) - 1, 0)
    lead = (size - power * 128).astype(F32)
    value = lead * jnp.exp2((power - (LEAST + 7)).astype(F32))
    return jnp.where(code < 0, -value, value).astype(BF16)


def halves(x):
    return jnp.concatenate([(x >> 6).astype(F32), (x & 63).astype(F32)], axis=1).astype(BF16)


def joined(x):
    return x[:, :STRIP] * 64.0 + x[:, STRIP:]


def tiled_strips(rows):
    height, width = rows.shape
    return jnp.concatenate(
        [
            rows[r : r + TILE, c : c + STRIP]
            for r in range(0, height, TILE)
            for c in range(0, width, STRIP)
        ],
        axis=0,
    )


def log2(n):
    return n.bit_length() - 1


def pack_kernel(C, F, L, place, image, seen, terms, counts, *refs):
    outs, (band_in, seen_in, terms_in, counts_in, row_in, sems) = refs[:F], refs[F:]
    c, f = place[0], place[1]
    height, width = image.shape
    band = height // C
    wide = width // STRIP
    per_facet = height * wide
    piece = per_facet // C
    mine = image.at[pl.ds(pl.multiple_of(c * band, TILE), band), :]
    copies = [
        pltpu.make_async_copy(source, target, sems.at[i])
        for i, (source, target) in enumerate(
            ((mine, band_in), (seen, seen_in), (terms, terms_in), (counts, counts_in))
        )
    ]
    for copy in copies:
        copy.start()
    chips = C // 2
    size = chips * BLOCK
    rows = F * size
    row = iota((rows, 1), 0)
    k, j, i = row // size, (row // BLOCK) % chips, row % BLOCK
    channel = ((c >> 1) ^ j) * (2 * L) + (i >> 1)
    is_seen = i < 4 * L
    pick = is_seen & (iota((rows, L * C * F), 1) == channel * F + (k ^ f))
    row_in[...] = jnp.zeros(row_in.shape, I32)
    for copy in copies:
        copy.wait()
    strips = tiled_strips(band_in[...])
    share = code_levels(strips)
    raw = terms_in[...]
    across, column = raw >> log2(F * wide), raw & (F * wide - 1)
    terms_in[...] = (
        (column >> log2(wide)) * per_facet
        + (across >> 3) * (wide * TILE)
        + (column & (wide - 1)) * TILE
        + (across & 7)
    )
    for at in range(F):
        for term in range(TERMS):
            row_in[at * TILE + term : at * TILE + term + 1, : L * C] = terms_in[at ^ f, term : term + 1]
        row_in[at * TILE + TERMS : at * TILE + TERMS + 1, : L * C] = counts_in[pl.ds(at ^ f, 1)]
    by_channel = jnp.concatenate([seen_in[n] for n in range(L * C)], axis=0)
    both = jnp.dot(one_hot(pick), by_channel, preferred_element_type=F32)
    values = code_floats(jnp.where((i & 1) == 0, both[:, :VISB], both[:, VISB:]))
    whole = jnp.concatenate(
        [part for at in range(F) for part in [row_in[at * TILE : (at + 1) * TILE]] * (2 * chips)],
        axis=0,
    )
    blocks = jnp.where(is_seen, values, whole).astype(I16)
    for at in range(F):
        if at:
            outs[at][:piece] = share
            outs[at][piece:] = blocks[at * size : (at + 1) * size]
        else:
            outs[at][...] = blocks[:size]


def pass_kernel(F, piece, *refs):
    got, outs = refs[:F][::-1], refs[F:]
    for j, out in enumerate(outs):
        for k in range(1, F):
            out[(k - 1) * piece : k * piece] = got[k][:piece]
        for k in range(F):
            at = (F - 1) * piece + k * BLOCK
            first = (piece if k else 0) + j * BLOCK
            out[at : at + BLOCK] = got[k][first : first + BLOCK]


def table_of(levels):
    return jnp.concatenate(split(levels, 2), axis=1)


def shares_of(got, chips, size, used):
    return [got[q * size : q * size + used].astype(I32).astype(F32) + 32768.0 for q in range(chips)]


def sorted_blocks(C, F, L, c, got, first):
    chips, slots = C // 2, C * F
    size = got.shape[0] // chips
    blocks = jnp.concatenate(
        [got[(q + 1) * size - F * BLOCK : (q + 1) * size] for q in range(chips)], axis=0
    ).astype(I32)

    def pick(kinds, start):
        out = iota((kinds * slots, blocks.shape[0]), 0)
        source = (out % slots - first) * BLOCK + start + out // slots
        return one_hot(iota(out.shape, 1) == source)

    seen = jnp.dot(pick(4, 2 * L * (c & 1)), floats_of(blocks), preferred_element_type=F32)
    whole = jnp.dot(pick(3, 4 * L), halves(blocks), preferred_element_type=F32)
    return seen, whole


def ready_kernel(C, F, L, place, image, kernels, mine, table_out, seen_out, whole_out, turned_out):
    height, width = image.shape
    used = (F - 1) * (height * width // STRIP // C)
    shares = shares_of(mine, C // 2, used + F * BLOCK, used)
    own = tiled_strips(image)
    table_out[...] = table_of(jnp.concatenate([own] + shares, axis=0))
    seen_out[...], whole_out[...] = sorted_blocks(C, F, L, place[0], mine, 0)
    for ch in range(L):
        turned_out[ch] = kernels[ch].T


def first_kernel(
    C, F, L, place, known, seen_in, whole_in, kernels, turned, other, start_out, seen_out, refs_out, live_out, msg
):
    c, f = place[0], place[1]
    chips, slots = C // 2, C * F
    size = other.shape[0] // chips
    used = size - F * BLOCK
    per_facet = known.shape[0] - chips * used
    piece = per_facet // C
    seen, whole = sorted_blocks(C, F, L, c, other, slots // 2)
    seen = seen + seen_in[...]
    row, column = iota((2 * STRIP, L * STRIP), 0), iota((2 * STRIP, L * STRIP), 1)
    channel = c * L + column // STRIP
    lanes = jnp.where(row == channel, 64.0, jnp.where(row == channel + STRIP, 1.0, 0.0))
    whole = jnp.dot(
        (whole + whole_in[...]).astype(BF16), lanes.astype(BF16), preferred_element_type=F32
    )
    kinds = [
        whole[kind * slots : (kind + 1) * slots, ch * STRIP : (ch + 1) * STRIP]
        for ch in range(L)
        for kind in range(TERMS + 1)
    ]
    refs = jnp.concatenate([x for i, x in enumerate(kinds) if i % (TERMS + 1) < TERMS], axis=0)
    live = jnp.concatenate(kinds[TERMS :: TERMS + 1], axis=0)
    col = refs.astype(I32)
    facet, local = col >> log2(per_facet), col & (per_facet - 1)
    k, d = facet ^ f, (local >> log2(piece)) ^ c
    turn = ((d & 1) * chips + (d >> 1)) * (F - 1) + k - 1
    place_of = jnp.where(k == 0, local, per_facet + turn * piece + (local & (piece - 1)))
    rest = table_of(jnp.concatenate(shares_of(other, chips, size, used), axis=0))

    def hits(count, start):
        wide = jnp.concatenate([place_of - start] * (count // STRIP), axis=1)
        return one_hot(iota(wide.shape, 1) == wide)

    both = jnp.dot(hits(known.shape[0], 0), known[...], preferred_element_type=F32) + jnp.dot(
        hits(rest.shape[0], known.shape[0]), rest, preferred_element_type=F32
    )
    total = both[:, :STRIP] + both[:, STRIP:]
    near, value = levels_of(jnp.where(k == 0, 0.0, total).astype(I32))
    sky = jnp.where(k == 0, both[:, :STRIP], near)
    start_out[...] = jnp.where(k == 0, total, value)
    seen_out[...] = seen.astype(BF16)
    refs_out[...] = refs
    live_out[...] = live
    encode(measure(sky, seen, live, kernels, turned), refs, msg)


def measure(est, seen, live, kernels, turned):
    L = kernels.shape[0]
    slots = live.shape[0] // L
    adjoints = []
    for ch in range(L):
        a, b, end = (ch * TERMS + i for i in range(3))
        sky = jnp.concatenate(
            [est[a * slots : b * slots], est[b * slots : end * slots]], axis=1
        ).astype(BF16)
        observed = jnp.concatenate(
            [seen[a * slots : b * slots], seen[b * slots : end * slots]], axis=1
        )
        predicted = jnp.dot(sky, kernels[ch], preferred_element_type=F32)
        alive = iota((slots, VISB), 1).astype(F32) < live[ch * slots : (ch + 1) * slots]
        residual = jnp.where(
            jnp.concatenate([alive, alive], axis=1), predicted - observed, 0.0
        ).astype(BF16)
        adjoint = jnp.dot(residual, turned[ch], preferred_element_type=F32)
        adjoints += [adjoint[:, :STRIP], adjoint[:, STRIP:]]
    return jnp.concatenate(adjoints, axis=0)


def as_row(col):
    eye = iota((STRIP, STRIP), 0) == iota((STRIP, STRIP), 1)
    return jnp.sum(jnp.where(eye, col, 0.0), axis=0, keepdims=True)


def scale_of(half):
    return jnp.exp2(half * 0.5).astype(BF16).astype(F32)


def put(msg, code, ids, half):
    msg[: code.shape[0]] = code.astype(I32).astype(I16)
    row = iota((EXTRA, STRIP), 0)
    extra = jnp.where(row == 0, ids, jnp.where(row == 1, half, 0.0))
    msg[code.shape[0] :] = extra.astype(I32).astype(I16)


def encode(adjoint, refs, msg):
    top = jnp.max(jnp.abs(adjoint), axis=1, keepdims=True)
    half = jnp.ceil(2.0 * jnp.log2(jnp.maximum(top, 1e-30) * (1.0 / 32500.0)))
    code = jnp.round(adjoint * (1.0 / scale_of(half)))
    row = as_row(half)
    put(msg, code, as_row(refs), row)
    return code, row


def sort_kernel(F, per_facet, place, refs, pick_out, numbers_out):
    f = place[1]
    ids = as_row(refs[...]).astype(I32)
    turn = iota((TILE, STRIP), 0)
    wanted = ((ids >> log2(per_facet)) == (turn ^ f)) & (turn < F)
    before = one_hot(iota((STRIP, STRIP), 0) < iota((STRIP, STRIP), 1))
    rank = jnp.dot(one_hot(wanted), before, preferred_element_type=F32)
    rank = jnp.where(wanted, rank, -1.0)
    slot = iota((PART, 1), 0).astype(F32)
    pick = jnp.concatenate([one_hot(rank[k : k + 1] == slot) for k in range(F)], axis=0)
    pick_out[...] = pick
    kinds = jnp.where(turn == 0, ids >> 6, jnp.where(turn == 1, ids & 63, 1))
    found = lax.dot_general(
        kinds.astype(F32).astype(BF16), pick, (((1,), (1,)), ((), ())), preferred_element_type=F32
    )
    found = jnp.where(found[2:3] > 0, found[0:1] * 64.0 + found[1:2], -1.0)
    for k in range(F):
        numbers_out[k * EXTRA : (k + 1) * EXTRA] = in_both_halves(found, k)


def in_both_halves(rows, k):
    at = k * PART // STRIP * STRIP
    pair = jnp.broadcast_to(rows[:, at : at + STRIP], (EXTRA, STRIP))
    low = iota((EXTRA, STRIP), 1) < PART
    return jnp.where(low == (k % 2 == 0), pair, pltpu.roll(pair, PART, 1))


def join_kernel(*refs):
    got, out = refs[:-1], refs[-1]
    F = len(got)
    rows = got[0].shape[0] - EXTRA
    number_rows = F * rows // STRIP
    row, lane = iota((EXTRA, STRIP), 0), iota((EXTRA, STRIP), 1)
    extra = jnp.zeros((EXTRA, STRIP), I32)
    for k in range(F):
        out[k * rows : (k + 1) * rows] = got[k][:rows]
        here = got[k][rows:].astype(I32)
        first, at = k * rows % STRIP, k * rows // STRIP
        own = (lane >= first) & (lane < first + rows)
        extra = jnp.where(own & (row == at), here[0:1], extra)
        extra = jnp.where(own & (row == number_rows + at), here[1:2], extra)
    out[F * rows :] = extra.astype(I16)


def decode(F, block, chips):
    ids, scales, values = [], [], []
    size = block.shape[0] // chips
    rows = size - EXTRA
    number_rows = rows // STRIP
    for at in range(0, block.shape[0], size):
        extra = block[at + rows : at + size].astype(I32)
        ids += [extra[j : j + 1] for j in range(number_rows)]
        scales += [extra[j : j + 1] for j in range(number_rows, 2 * number_rows)]
        values.append(table_of(block[at : at + rows].astype(I32).astype(F32)))
    scale = scale_of(jnp.concatenate(scales, axis=1).astype(F32))
    return ids, scale, jnp.concatenate(values, axis=0)


def summed(decoded, strips):
    ids, scale, values = decoded
    wide = strips if len(ids) * STRIP == strips.shape[1] else jnp.concatenate([strips] * len(ids), axis=1)
    hit = jnp.concatenate(ids, axis=1) == wide
    both = jnp.dot(jnp.where(hit, scale, 0.0).astype(BF16), values, preferred_element_type=F32)
    return both[:, :STRIP] + both[:, STRIP:]


def crowd_of(ids, F, per_facet):
    facets = jnp.concatenate(ids, axis=0) >> log2(per_facet)
    hits = jnp.concatenate([one_hot(facets == f) for f in range(F)], axis=0)
    ones = jnp.ones((STRIP, STRIP), BF16)
    counts = jnp.dot(hits, ones, preferred_element_type=F32)
    return jnp.max(counts, axis=0, keepdims=True)


def part_kernel(F, chips, refs, block, out):
    out[...] = summed(decode(F, block, chips), refs[...].astype(I32))


def next_kernel(
    F, chips, step, refs, live, seen, kernels, turned, est_in, part, block, pick, numbers, msg, *msgs
):
    gradient = part[...] + summed(decode(F, block, chips), refs[...].astype(I32))
    est = jnp.maximum(est_in[...] - step * gradient - shrinkage, 0.0)
    adjoint = measure(est, seen[...].astype(F32), live[...], kernels, turned)
    code, half = encode(adjoint, refs[...], msg)
    both = jnp.dot(pick[...], table_of(code), preferred_element_type=F32)
    rows = both[:, :STRIP] + both[:, STRIP:]
    halves_of = lax.dot_general(
        jnp.broadcast_to(half, (TILE, STRIP)).astype(BF16),
        pick[...],
        (((1,), (1,)), ((), ())),
        preferred_element_type=F32,
    )[0:1]
    for k, short in enumerate(msgs):
        put(
            short,
            rows[k * PART : (k + 1) * PART],
            numbers[k * EXTRA : (k + 1) * EXTRA],
            in_both_halves(halves_of, k),
        )


def facet_part_kernel(F, chips, place, block, out, *crowd):
    decoded = decode(F, block, chips)
    count = out.shape[0]
    out[...] = summed(decoded, iota((count, STRIP), 0) + place[1] * count)
    for most in crowd:
        most[...] = jnp.broadcast_to(crowd_of(decoded[0], F, count), most.shape)


def settle_kernel(F, chips, step, place, image, part, block, *refs):
    decoded = decode(F, block, chips)
    height, width = image.shape
    count = part.shape[0]
    if len(refs) == 3:
        crowd, out, most = refs
        most[0] = jnp.max(jnp.maximum(crowd[0:1], crowd_of(decoded[0], F, count))).astype(I32)
    else:
        (out,) = refs
    per_band = width // STRIP * TILE
    chunk = min(256, count)
    for at in range(0, count, chunk):
        strips = iota((chunk, STRIP), 0) + (place[1] * count + at)
        gradient = part[at : at + chunk] + summed(decoded, strips)
        for t in range(0, chunk, TILE):
            r = (at + t) // per_band * TILE
            c = (at + t) % per_band // TILE * STRIP
            old = image[r : r + TILE, c : c + STRIP]
            out[r : r + TILE, c : c + STRIP] = jnp.maximum(
                old - step * gradient[t : t + TILE] - shrinkage, 0.0
            )


def swap(x, axis, k):
    return lax.ppermute(x, axis, [(i, i ^ k) for i in range(lax.axis_size(axis))])


def sparse_device(start_image, visibilities, strip_index, live_counts, uv_kernels):
    C, F = lax.axis_size("chan"), lax.axis_size("facet")
    L = uv_kernels.shape[0]
    refs = C * F * L * TERMS
    per_facet = start_image.size // STRIP
    piece = per_facet // C
    chips = C // 2
    step = float(per_facet * F / (2.5 * C * F * (L * C) * F))
    place = jnp.stack([lax.axis_index("chan"), lax.axis_index("facet")]).astype(I32)
    kernels = uv_kernels[:, 0]

    blocks = jax.ShapeDtypeStruct((chips * BLOCK, STRIP), I16)
    both = jax.ShapeDtypeStruct((piece + chips * BLOCK, STRIP), I16)
    packed = call(
        functools.partial(pack_kernel, C, F, L),
        [blocks] + [both] * (F - 1),
        [
            place,
            start_image,
            visibilities[0],
            strip_index[0].transpose(1, 2, 0),
            live_counts[0].T,
        ],
        10**8,
        smem=1,
        hbm=4,
        scratch=[
            pltpu.VMEM((start_image.shape[0] // C, start_image.shape[1]), F32),
            pltpu.VMEM(visibilities.shape[1:], BF16),
            pltpu.VMEM((F, TERMS, L * C), I32),
            pltpu.VMEM((F, L * C), I32),
            pltpu.VMEM((F * TILE, STRIP), I32),
            pltpu.SemaphoreType.DMA((4,)),
        ],
    )
    got = [packed[0]] + [swap(packed[k], "facet", k) for k in range(F - 1, 0, -1)][::-1]
    passed = call(
        functools.partial(pass_kernel, F, piece),
        [jax.ShapeDtypeStruct(((F - 1) * piece + F * BLOCK, STRIP), I16)] * chips,
        got[::-1],
        10**6,
    )
    mine = jnp.concatenate(
        [passed[0]] + [swap(passed[j], "chan", 2 * j) for j in range(1, chips)], axis=0
    )
    other = swap(mine, "chan", 1)

    at_refs = jax.ShapeDtypeStruct((refs, STRIP), F32)
    message = jax.ShapeDtypeStruct((refs + EXTRA, STRIP), I16)
    short = jax.ShapeDtypeStruct((PART + EXTRA, STRIP), I16)
    facet_strips = jax.ShapeDtypeStruct((per_facet, STRIP), F32)
    known, seen_part, whole_part, turned = call(
        functools.partial(ready_kernel, C, F, L),
        [
            jax.ShapeDtypeStruct((per_facet + chips * (F - 1) * piece, 2 * STRIP), BF16),
            at_refs,
            jax.ShapeDtypeStruct(((TERMS + 1) * C * F, 2 * STRIP), F32),
            jax.ShapeDtypeStruct(kernels.shape, BF16),
        ],
        [place, start_image, kernels, mine],
        10**8,
        smem=1,
    )
    est, observed, at, live, msg = call(
        functools.partial(first_kernel, C, F, L),
        [
            at_refs,
            jax.ShapeDtypeStruct((refs, STRIP), BF16),
            at_refs,
            jax.ShapeDtypeStruct((L * C * F, STRIP), F32),
            message,
        ],
        [place, known, seen_part, whole_part, kernels, turned, other],
        5 * 10**8,
        smem=1,
    )

    def along_facet(msgs):
        got = [msgs[0]] + [swap(msgs[k], "facet", k) for k in range(1, F)]
        rows = got[0].shape[0] - EXTRA
        return call(
            join_kernel, [jax.ShapeDtypeStruct((F * rows + EXTRA, STRIP), I16)], got, 10**6
        )[0]

    def around_chan(near):
        around = [swap(near, "chan", 2 * j) for j in range(chips - 1, 0, -1)]
        return jnp.concatenate([near] + around, axis=0)

    def along_chan(near):
        mine = around_chan(near)
        return mine, swap(mine, "chan", 1)

    def facet_part(mine, *crowd):
        return call(
            functools.partial(facet_part_kernel, F, chips),
            [facet_strips, *crowd],
            [place, mine],
            2 * 10**9,
            smem=1,
        )

    settle = functools.partial(settle_kernel, F, chips, step)
    whole = jax.ShapeDtypeStruct(start_image.shape, F32)

    near = along_facet([msg] * F)
    pick, numbers = call(
        functools.partial(sort_kernel, F, per_facet),
        [
            jax.ShapeDtypeStruct((F * PART, refs), BF16),
            jax.ShapeDtypeStruct((F * EXTRA, STRIP), F32),
        ],
        [place, at],
        10**8,
        smem=1,
    )
    near, pick, numbers = lax.optimization_barrier((near, pick, numbers))
    mine, other = along_chan(near)
    (part,) = call(
        functools.partial(part_kernel, F, chips), [at_refs], [at, mine], 3 * 10**8
    )
    msg, *msgs = call(
        functools.partial(next_kernel, F, chips, step),
        [message] + [short] * F,
        [at, live, observed, kernels, turned, est, part, other, pick, numbers],
        3 * 10**8,
    )
    msg, mine, *msgs = lax.optimization_barrier((msg, mine, *msgs))
    near = along_facet(msgs)
    part, crowd = facet_part(mine, jax.ShapeDtypeStruct((TILE, STRIP), F32))
    near, part, crowd = lax.optimization_barrier((near, part, crowd))
    around = around_chan(near)
    image, crowd = call(
        settle,
        [whole, jax.ShapeDtypeStruct((1,), I32)],
        [place, start_image, part, other, crowd],
        2 * 10**9,
        smem=1,
        scalars=1,
    )
    crowded = crowd[0] > PART
    around, image, crowded = lax.optimization_barrier((around, image, crowded))

    other = swap(around, "chan", 1)
    (part,) = facet_part(around)

    def in_full():
        mine, other = along_chan(along_facet([msg] * F))
        (part,) = facet_part(mine)
        (rest,) = facet_part(other)
        return part + rest, jnp.zeros((chips * (F * PART + EXTRA), STRIP), I16)

    part, other = lax.cond(crowded, in_full, lambda: (part, other))
    return call(
        settle,
        [whole],
        [place, image, part, other],
        2 * 10**9,
        smem=1,
    )[0]


def dense_device(start_image, visibilities, strip_index, live_counts, uv_kernels):
    def to_owner(x):
        x = lax.all_to_all(x, "chan", split_axis=1, concat_axis=0, tiled=True)
        return lax.all_to_all(x, "facet", split_axis=2, concat_axis=0, tiled=True)

    observed, picked_ids, live_now = map(to_owner, (visibilities, strip_index, live_counts))
    slot_count = observed.shape[0]
    chan_local, uv_local = uv_kernels.shape[:2]
    slab_rows, facet_width = start_image.shape
    full_width = facet_width * lax.axis_size("facet")
    strip_count = slab_rows * full_width // STRIP
    blocks = slot_count * chan_local * lax.axis_size("chan") * uv_local * lax.axis_size("facet")
    step_size = strip_count / (2.5 * blocks)
    lane_ids = jnp.arange(2 * VISB, dtype=I32) % VISB
    live_mask = lane_ids < live_now[..., None]
    flat_ids = picked_ids.reshape(-1)
    estimate = start_image
    for iteration in range(ITERS):
        full_sky = lax.all_gather(estimate.astype(BF16), "facet", axis=1, tiled=True)
        sky_strips = full_sky.reshape(strip_count, STRIP)
        gathered = sky_strips[picked_ids].reshape(slot_count, chan_local, uv_local, TERMS * STRIP)
        predicted = jnp.einsum("scup,cupq->scuq", gathered, uv_kernels, preferred_element_type=F32)
        residual = jnp.where(live_mask, predicted - observed.astype(F32), 0.0).astype(BF16)
        adjoint = jnp.einsum("scuq,cupq->scup", residual, uv_kernels, preferred_element_type=F32)
        gradient = jnp.zeros((strip_count, STRIP), F32).at[flat_ids].add(adjoint.reshape(-1, STRIP))
        gradient = gradient.reshape(slab_rows, full_width)
        facet_part = lax.psum_scatter(gradient, "facet", scatter_dimension=1, tiled=True)
        facet_sum = lax.psum(facet_part, "chan")
        descent = estimate - step_size * facet_sum
        estimate = jnp.maximum(descent - shrinkage, 0.0)
    return estimate


def on_device(start_image, visibilities, strip_index, live_counts, uv_kernels):
    C, F = lax.axis_size("chan"), lax.axis_size("facet")
    L, uv_local = uv_kernels.shape[:2]
    strips = start_image.size * F // STRIP
    sparse = (
        visibilities.shape[0] == 1
        and uv_local == 1
        and C & (C - 1) == 0
        and F & (F - 1) == 0
        and C >= 4
        and ITERS == 2
        and F >= 2
        and F <= TILE and F * PART % STRIP == 0
        and C * F * L * TERMS == STRIP
        and 4 * L + TERMS + 1 <= BLOCK
        and 4 * L == TILE
        and L * C <= STRIP
        and strips <= 64 * 256
        and strips & (strips - 1) == 0
        and start_image.shape[0] % (C * TILE) == 0
        and start_image.shape[1] % STRIP == 0
        and start_image.size // STRIP // C % 16 == 0
    )
    run = sparse_device if sparse else dense_device
    return run(start_image, visibilities, strip_index, live_counts, uv_kernels)


def solution(mesh):
    placed = (
        P(None, "facet"),
        P(("chan", "facet"), None, None, None),
        P(("chan", "facet"), None, None, None),
        P(("chan", "facet"), None, None),
        P("chan", "facet", None, None),
    )
    return jax.shard_map(
        on_device, mesh=mesh, in_specs=placed, out_specs=P(None, "facet"), check_vma=False
    )
```

```python
import functools

import jax
import jax.numpy as jnp
from jax import lax
from jax.experimental import pallas as pl
from jax.experimental.pallas import tpu as pltpu
from jax.sharding import PartitionSpec as P

STRIP = 128
VISB = 128
TERMS = 2
ITERS = 2
TILE = 8
EXTRA = 16
BLOCK = 16
PART = 64
FINE = 32
FLOOR = 10
LEAST = 119

shrinkage = 0.05
F32, BF16, I32, I16 = jnp.float32, jnp.bfloat16, jnp.int32, jnp.int16
VMEM_LIMIT = 48 * 1024 * 1024


def call(kernel, outs, args, flops, smem=0, hbm=0, scratch=(), scalars=0):
    spaces = [pl.BlockSpec(memory_space=pltpu.SMEM)] * smem
    spaces += [pl.BlockSpec(memory_space=pltpu.HBM)] * hbm
    spaces += [pl.BlockSpec(memory_space=pltpu.VMEM)] * (len(args) - smem - hbm)
    moved = sum(a.size * a.dtype.itemsize for a in list(args) + list(outs))
    args = list(args)
    for i in range(smem, smem + hbm):
        args[i] = pltpu.with_memory_space_constraint(args[i], pltpu.HBM)
    return pl.pallas_call(
        kernel,
        out_shape=list(outs),
        in_specs=spaces,
        out_specs=[pl.BlockSpec(memory_space=pltpu.VMEM)] * (len(outs) - scalars)
        + [pl.BlockSpec(memory_space=pltpu.SMEM)] * scalars,
        scratch_shapes=list(scratch),
        compiler_params=pltpu.CompilerParams(vmem_limit_bytes=VMEM_LIMIT),
        cost_estimate=pl.CostEstimate(flops=flops, bytes_accessed=moved, transcendentals=0),
    )(*args)


def split(x, parts):
    terms = []
    for _ in range(parts):
        term = x.astype(BF16)
        terms.append(term)
        x = x - term.astype(F32)
    return terms


def one_hot(hit):
    return jnp.where(hit, 1.0, 0.0).astype(BF16)


def iota(shape, dim):
    return lax.broadcasted_iota(I32, shape, dim)


def code_floats(x):
    size = jnp.abs(x)
    power = jnp.maximum(jnp.floor(jnp.log2(jnp.maximum(size, 1e-37))), -LEAST)
    code = (power + LEAST) * 128.0 + jnp.round(size * jnp.exp2(7.0 - power))
    return jnp.where(x < 0, -code, code).astype(I32)


def code_levels(x):
    near = x.astype(BF16).astype(F32)
    power = jnp.maximum(jnp.floor(jnp.log2(jnp.maximum(near, 1e-37))), -FLOOR)
    unit = jnp.exp2(power - 7.0)
    lead = jnp.round(near / unit)
    step = jnp.round(((x - lead * unit) / unit + 0.5) * (FINE - 1))
    step = jnp.clip(step, 0.0, FINE - 1)
    code = ((power + FLOOR) * 128.0 + lead) * FINE + step - 32768.0
    return code.astype(I32).astype(I16)


def levels_of(code):
    level = code >> log2(FINE)
    power = jnp.maximum((level >> 7) - 1, 0)
    unit = jnp.exp2((power - (FLOOR + 7)).astype(F32))
    near = ((level - power * 128).astype(F32) * unit).astype(BF16).astype(F32)
    step = (code & (FINE - 1)).astype(F32)
    return near, near + (step * (1.0 / (FINE - 1)) - 0.5) * unit


def floats_of(code):
    size = jnp.abs(code)
    power = jnp.maximum((size >> 7) - 1, 0)
    lead = (size - power * 128).astype(F32)
    value = lead * jnp.exp2((power - (LEAST + 7)).astype(F32))
    return jnp.where(code < 0, -value, value).astype(BF16)


def halves(x):
    return jnp.concatenate([(x >> 6).astype(F32), (x & 63).astype(F32)], axis=1).astype(BF16)


def joined(x):
    return x[:, :STRIP] * 64.0 + x[:, STRIP:]


def tiled_strips(rows):
    height, width = rows.shape
    return jnp.concatenate(
        [
            rows[r : r + TILE, c : c + STRIP]
            for r in range(0, height, TILE)
            for c in range(0, width, STRIP)
        ],
        axis=0,
    )


def log2(n):
    return n.bit_length() - 1


def pack_kernel(C, F, L, place, image, seen, terms, counts, *refs):
    outs, (band_in, seen_in, terms_in, counts_in, row_in, sems) = refs[:F], refs[F:]
    c, f = place[0], place[1]
    height, width = image.shape
    band = height // C
    wide = width // STRIP
    per_facet = height * wide
    piece = per_facet // C
    mine = image.at[pl.ds(pl.multiple_of(c * band, TILE), band), :]
    copies = [
        pltpu.make_async_copy(source, target, sems.at[i])
        for i, (source, target) in enumerate(
            ((mine, band_in), (seen, seen_in), (terms, terms_in), (counts, counts_in))
        )
    ]
    for copy in copies:
        copy.start()
    chips = C // 2
    size = chips * BLOCK
    rows = F * size
    row = iota((rows, 1), 0)
    k, j, i = row // size, (row // BLOCK) % chips, row % BLOCK
    channel = ((c >> 1) ^ j) * (2 * L) + (i >> 1)
    is_seen = i < 4 * L
    pick = is_seen & (iota((rows, L * C * F), 1) == channel * F + (k ^ f))
    row_in[...] = jnp.zeros(row_in.shape, I32)
    for copy in copies:
        copy.wait()
    strips = tiled_strips(band_in[...])
    share = code_levels(strips)
    raw = terms_in[...]
    across, column = raw >> log2(F * wide), raw & (F * wide - 1)
    terms_in[...] = (
        (column >> log2(wide)) * per_facet
        + (across >> 3) * (wide * TILE)
        + (column & (wide - 1)) * TILE
        + (across & 7)
    )
    for at in range(F):
        for term in range(TERMS):
            row_in[at * TILE + term : at * TILE + term + 1, : L * C] = terms_in[at ^ f, term : term + 1]
        row_in[at * TILE + TERMS : at * TILE + TERMS + 1, : L * C] = counts_in[pl.ds(at ^ f, 1)]
    by_channel = jnp.concatenate([seen_in[n] for n in range(L * C)], axis=0)
    both = jnp.dot(one_hot(pick), by_channel, preferred_element_type=F32)
    values = code_floats(jnp.where((i & 1) == 0, both[:, :VISB], both[:, VISB:]))
    whole = jnp.concatenate(
        [part for at in range(F) for part in [row_in[at * TILE : (at + 1) * TILE]] * (2 * chips)],
        axis=0,
    )
    blocks = jnp.where(is_seen, values, whole).astype(I16)
    for at in range(F):
        if at:
            outs[at][:piece] = share
            outs[at][piece:] = blocks[at * size : (at + 1) * size]
        else:
            outs[at][...] = blocks[:size]


def pass_kernel(F, piece, *refs):
    got, outs = refs[:F][::-1], refs[F:]
    for j, out in enumerate(outs):
        for k in range(1, F):
            out[(k - 1) * piece : k * piece] = got[k][:piece]
        for k in range(F):
            at = (F - 1) * piece + k * BLOCK
            first = (piece if k else 0) + j * BLOCK
            out[at : at + BLOCK] = got[k][first : first + BLOCK]


def table_of(levels):
    return jnp.concatenate(split(levels, 2), axis=1)


def shares_of(got, chips, size, used):
    return [got[q * size : q * size + used].astype(I32).astype(F32) + 32768.0 for q in range(chips)]


def sorted_blocks(C, F, L, c, got, first):
    chips, slots = C // 2, C * F
    size = got.shape[0] // chips
    blocks = jnp.concatenate(
        [got[(q + 1) * size - F * BLOCK : (q + 1) * size] for q in range(chips)], axis=0
    ).astype(I32)

    def pick(kinds, start):
        out = iota((kinds * slots, blocks.shape[0]), 0)
        source = (out % slots - first) * BLOCK + start + out // slots
        return one_hot(iota(out.shape, 1) == source)

    seen = jnp.dot(pick(4, 2 * L * (c & 1)), floats_of(blocks), preferred_element_type=F32)
    whole = jnp.dot(pick(3, 4 * L), halves(blocks), preferred_element_type=F32)
    return seen, whole


def ready_kernel(C, F, L, place, image, kernels, mine, table_out, seen_out, whole_out, turned_out):
    height, width = image.shape
    used = (F - 1) * (height * width // STRIP // C)
    shares = shares_of(mine, C // 2, used + F * BLOCK, used)
    own = tiled_strips(image)
    table_out[...] = table_of(jnp.concatenate([own] + shares, axis=0))
    seen_out[...], whole_out[...] = sorted_blocks(C, F, L, place[0], mine, 0)
    for ch in range(L):
        turned_out[ch] = kernels[ch].T


def first_kernel(
    C, F, L, place, known, seen_in, whole_in, kernels, turned, other, start_out, seen_out, refs_out, live_out, msg
):
    c, f = place[0], place[1]
    chips, slots = C // 2, C * F
    size = other.shape[0] // chips
    used = size - F * BLOCK
    per_facet = known.shape[0] - chips * used
    piece = per_facet // C
    seen, whole = sorted_blocks(C, F, L, c, other, slots // 2)
    seen = seen + seen_in[...]
    row, column = iota((2 * STRIP, L * STRIP), 0), iota((2 * STRIP, L * STRIP), 1)
    channel = c * L + column // STRIP
    lanes = jnp.where(row == channel, 64.0, jnp.where(row == channel + STRIP, 1.0, 0.0))
    whole = jnp.dot(
        (whole + whole_in[...]).astype(BF16), lanes.astype(BF16), preferred_element_type=F32
    )
    kinds = [
        whole[kind * slots : (kind + 1) * slots, ch * STRIP : (ch + 1) * STRIP]
        for ch in range(L)
        for kind in range(TERMS + 1)
    ]
    refs = jnp.concatenate([x for i, x in enumerate(kinds) if i % (TERMS + 1) < TERMS], axis=0)
    live = jnp.concatenate(kinds[TERMS :: TERMS + 1], axis=0)
    col = refs.astype(I32)
    facet, local = col >> log2(per_facet), col & (per_facet - 1)
    k, d = facet ^ f, (local >> log2(piece)) ^ c
    turn = ((d & 1) * chips + (d >> 1)) * (F - 1) + k - 1
    place_of = jnp.where(k == 0, local, per_facet + turn * piece + (local & (piece - 1)))
    rest = table_of(jnp.concatenate(shares_of(other, chips, size, used), axis=0))

    def hits(count, start):
        wide = jnp.concatenate([place_of - start] * (count // STRIP), axis=1)
        return one_hot(iota(wide.shape, 1) == wide)

    both = jnp.dot(hits(known.shape[0], 0), known[...], preferred_element_type=F32) + jnp.dot(
        hits(rest.shape[0], known.shape[0]), rest, preferred_element_type=F32
    )
    total = both[:, :STRIP] + both[:, STRIP:]
    near, value = levels_of(jnp.where(k == 0, 0.0, total).astype(I32))
    sky = jnp.where(k == 0, both[:, :STRIP], near)
    start_out[...] = jnp.where(k == 0, total, value)
    seen_out[...] = seen.astype(BF16)
    refs_out[...] = refs
    live_out[...] = live
    encode(measure(sky, seen, live, kernels, turned), refs, msg)


def measure(est, seen, live, kernels, turned):
    L = kernels.shape[0]
    slots = live.shape[0] // L
    adjoints = []
    for ch in range(L):
        a, b, end = (ch * TERMS + i for i in range(3))
        sky = jnp.concatenate(
            [est[a * slots : b * slots], est[b * slots : end * slots]], axis=1
        ).astype(BF16)
        observed = jnp.concatenate(
            [seen[a * slots : b * slots], seen[b * slots : end * slots]], axis=1
        )
        predicted = jnp.dot(sky, kernels[ch], preferred_element_type=F32)
        alive = iota((slots, VISB), 1).astype(F32) < live[ch * slots : (ch + 1) * slots]
        residual = jnp.where(
            jnp.concatenate([alive, alive], axis=1), predicted - observed, 0.0
        ).astype(BF16)
        adjoint = jnp.dot(residual, turned[ch], preferred_element_type=F32)
        adjoints += [adjoint[:, :STRIP], adjoint[:, STRIP:]]
    return jnp.concatenate(adjoints, axis=0)


def as_row(col):
    eye = iota((STRIP, STRIP), 0) == iota((STRIP, STRIP), 1)
    return jnp.sum(jnp.where(eye, col, 0.0), axis=0, keepdims=True)


def scale_of(half):
    return jnp.exp2(half * 0.5).astype(BF16).astype(F32)


def put(msg, code, ids, half):
    msg[: code.shape[0]] = code.astype(I32).astype(I16)
    row = iota((EXTRA, STRIP), 0)
    extra = jnp.where(row == 0, ids, jnp.where(row == 1, half, 0.0))
    msg[code.shape[0] :] = extra.astype(I32).astype(I16)


def encode(adjoint, refs, msg):
    top = jnp.max(jnp.abs(adjoint), axis=1, keepdims=True)
    half = jnp.ceil(2.0 * jnp.log2(jnp.maximum(top, 1e-30) * (1.0 / 32500.0)))
    code = jnp.round(adjoint * (1.0 / scale_of(half)))
    row = as_row(half)
    put(msg, code, as_row(refs), row)
    return code, row


def sort_kernel(F, per_facet, place, refs, pick_out, numbers_out):
    f = place[1]
    ids = as_row(refs[...]).astype(I32)
    turn = iota((TILE, STRIP), 0)
    wanted = ((ids >> log2(per_facet)) == (turn ^ f)) & (turn < F)
    before = one_hot(iota((STRIP, STRIP), 0) < iota((STRIP, STRIP), 1))
    rank = jnp.dot(one_hot(wanted), before, preferred_element_type=F32)
    rank = jnp.where(wanted, rank, -1.0)
    slot = iota((PART, 1), 0).astype(F32)
    pick = jnp.concatenate([one_hot(rank[k : k + 1] == slot) for k in range(F)], axis=0)
    pick_out[...] = pick
    kinds = jnp.where(turn == 0, ids >> 6, jnp.where(turn == 1, ids & 63, 1))
    found = lax.dot_general(
        kinds.astype(F32).astype(BF16), pick, (((1,), (1,)), ((), ())), preferred_element_type=F32
    )
    found = jnp.where(found[2:3] > 0, found[0:1] * 64.0 + found[1:2], -1.0)
    for k in range(F):
        numbers_out[k * EXTRA : (k + 1) * EXTRA] = in_both_halves(found, k)


def in_both_halves(rows, k):
    at = k * PART // STRIP * STRIP
    pair = jnp.broadcast_to(rows[:, at : at + STRIP], (EXTRA, STRIP))
    low = iota((EXTRA, STRIP), 1) < PART
    return jnp.where(low == (k % 2 == 0), pair, pltpu.roll(pair, PART, 1))


def join_kernel(*refs):
    got, out = refs[:-1], refs[-1]
    F = len(got)
    rows = got[0].shape[0] - EXTRA
    number_rows = F * rows // STRIP
    row, lane = iota((EXTRA, STRIP), 0), iota((EXTRA, STRIP), 1)
    extra = jnp.zeros((EXTRA, STRIP), I32)
    for k in range(F):
        out[k * rows : (k + 1) * rows] = got[k][:rows]
        here = got[k][rows:].astype(I32)
        first, at = k * rows % STRIP, k * rows // STRIP
        own = (lane >= first) & (lane < first + rows)
        extra = jnp.where(own & (row == at), here[0:1], extra)
        extra = jnp.where(own & (row == number_rows + at), here[1:2], extra)
    out[F * rows :] = extra.astype(I16)


def decode(F, block, chips):
    ids, scales, values = [], [], []
    size = block.shape[0] // chips
    rows = size - EXTRA
    number_rows = rows // STRIP
    for at in range(0, block.shape[0], size):
        extra = block[at + rows : at + size].astype(I32)
        ids += [extra[j : j + 1] for j in range(number_rows)]
        scales += [extra[j : j + 1] for j in range(number_rows, 2 * number_rows)]
        values.append(table_of(block[at : at + rows].astype(I32).astype(F32)))
    scale = scale_of(jnp.concatenate(scales, axis=1).astype(F32))
    return ids, scale, jnp.concatenate(values, axis=0)


def summed(decoded, strips):
    ids, scale, values = decoded
    wide = strips if len(ids) * STRIP == strips.shape[1] else jnp.concatenate([strips] * len(ids), axis=1)
    hit = jnp.concatenate(ids, axis=1) == wide
    both = jnp.dot(jnp.where(hit, scale, 0.0).astype(BF16), values, preferred_element_type=F32)
    return both[:, :STRIP] + both[:, STRIP:]


def crowd_of(ids, F, per_facet):
    facets = jnp.concatenate(ids, axis=0) >> log2(per_facet)
    hits = jnp.concatenate([one_hot(facets == f) for f in range(F)], axis=0)
    ones = jnp.ones((STRIP, STRIP), BF16)
    counts = jnp.dot(hits, ones, preferred_element_type=F32)
    return jnp.max(counts, axis=0, keepdims=True)


def part_kernel(F, chips, refs, other_refs, block, out, other_out):
    strips = jnp.concatenate([refs[...], other_refs[...]], axis=0).astype(I32)
    total = summed(decode(F, block, chips), strips)
    out[...] = total[: refs.shape[0]]
    other_out[...] = total[refs.shape[0] :]


def next_kernel(
    step, refs, live, seen, kernels, turned, est_in, part, rest, pick, numbers, msg, *msgs
):
    gradient = part[...] + rest[...]
    est = jnp.maximum(est_in[...] - step * gradient - shrinkage, 0.0)
    adjoint = measure(est, seen[...].astype(F32), live[...], kernels, turned)
    code, half = encode(adjoint, refs[...], msg)
    both = jnp.dot(pick[...], table_of(code), preferred_element_type=F32)
    rows = both[:, :STRIP] + both[:, STRIP:]
    halves_of = lax.dot_general(
        jnp.broadcast_to(half, (TILE, STRIP)).astype(BF16),
        pick[...],
        (((1,), (1,)), ((), ())),
        preferred_element_type=F32,
    )[0:1]
    for k, short in enumerate(msgs):
        put(
            short,
            rows[k * PART : (k + 1) * PART],
            numbers[k * EXTRA : (k + 1) * EXTRA],
            in_both_halves(halves_of, k),
        )


def facet_part_kernel(F, chips, place, block, out, *crowd):
    decoded = decode(F, block, chips)
    count = out.shape[0]
    out[...] = summed(decoded, iota((count, STRIP), 0) + place[1] * count)
    for most in crowd:
        most[...] = jnp.broadcast_to(crowd_of(decoded[0], F, count), most.shape)


def settle_kernel(F, chips, step, place, image, part, block, *refs):
    decoded = decode(F, block, chips)
    height, width = image.shape
    count = part.shape[0]
    if len(refs) == 3:
        crowd, out, most = refs
        most[0] = jnp.max(jnp.maximum(crowd[0:1], crowd_of(decoded[0], F, count))).astype(I32)
    else:
        (out,) = refs
    per_band = width // STRIP * TILE
    chunk = min(256, count)
    for at in range(0, count, chunk):
        strips = iota((chunk, STRIP), 0) + (place[1] * count + at)
        gradient = part[at : at + chunk] + summed(decoded, strips)
        for t in range(0, chunk, TILE):
            r = (at + t) // per_band * TILE
            c = (at + t) % per_band // TILE * STRIP
            old = image[r : r + TILE, c : c + STRIP]
            out[r : r + TILE, c : c + STRIP] = jnp.maximum(
                old - step * gradient[t : t + TILE] - shrinkage, 0.0
            )


def swap(x, along_chan, along_facet=0):
    C, F = lax.axis_size("chan"), lax.axis_size("facet")
    pairs = [
        (c * F + f, (c ^ along_chan) * F + (f ^ along_facet)) for c in range(C) for f in range(F)
    ]
    return lax.ppermute(x, ("chan", "facet"), pairs)


def sparse_device(start_image, visibilities, strip_index, live_counts, uv_kernels):
    C, F = lax.axis_size("chan"), lax.axis_size("facet")
    L = uv_kernels.shape[0]
    refs = C * F * L * TERMS
    per_facet = start_image.size // STRIP
    piece = per_facet // C
    chips = C // 2
    step = float(per_facet * F / (2.5 * C * F * (L * C) * F))
    place = jnp.stack([lax.axis_index("chan"), lax.axis_index("facet")]).astype(I32)
    kernels = uv_kernels[:, 0]

    blocks = jax.ShapeDtypeStruct((chips * BLOCK, STRIP), I16)
    both = jax.ShapeDtypeStruct((piece + chips * BLOCK, STRIP), I16)
    packed = call(
        functools.partial(pack_kernel, C, F, L),
        [blocks] + [both] * (F - 1),
        [
            place,
            start_image,
            visibilities[0],
            strip_index[0].transpose(1, 2, 0),
            live_counts[0].T,
        ],
        10**8,
        smem=1,
        hbm=4,
        scratch=[
            pltpu.VMEM((start_image.shape[0] // C, start_image.shape[1]), F32),
            pltpu.VMEM(visibilities.shape[1:], BF16),
            pltpu.VMEM((F, TERMS, L * C), I32),
            pltpu.VMEM((F, L * C), I32),
            pltpu.VMEM((F * TILE, STRIP), I32),
            pltpu.SemaphoreType.DMA((4,)),
        ],
    )
    got = [packed[0]] + [swap(packed[k], 0, k) for k in range(F - 1, 0, -1)][::-1]
    passed = call(
        functools.partial(pass_kernel, F, piece),
        [jax.ShapeDtypeStruct(((F - 1) * piece + F * BLOCK, STRIP), I16)] * chips,
        got[::-1],
        10**6,
    )
    mine = jnp.concatenate(
        [passed[0]] + [swap(passed[j], 2 * j) for j in range(1, chips)], axis=0
    )
    other = swap(mine, 1)

    at_refs = jax.ShapeDtypeStruct((refs, STRIP), F32)
    message = jax.ShapeDtypeStruct((refs + EXTRA, STRIP), I16)
    short = jax.ShapeDtypeStruct((PART + EXTRA, STRIP), I16)
    facet_strips = jax.ShapeDtypeStruct((per_facet, STRIP), F32)
    known, seen_part, whole_part, turned = call(
        functools.partial(ready_kernel, C, F, L),
        [
            jax.ShapeDtypeStruct((per_facet + chips * (F - 1) * piece, 2 * STRIP), BF16),
            at_refs,
            jax.ShapeDtypeStruct(((TERMS + 1) * C * F, 2 * STRIP), F32),
            jax.ShapeDtypeStruct(kernels.shape, BF16),
        ],
        [place, start_image, kernels, mine],
        10**8,
        smem=1,
    )
    est, observed, at, live, msg = call(
        functools.partial(first_kernel, C, F, L),
        [
            at_refs,
            jax.ShapeDtypeStruct((refs, STRIP), BF16),
            at_refs,
            jax.ShapeDtypeStruct((L * C * F, STRIP), F32),
            message,
        ],
        [place, known, seen_part, whole_part, kernels, turned, other],
        5 * 10**8,
        smem=1,
    )

    def along_facet(msgs, cross=0):
        got = [msgs[0]] + [swap(msgs[k], cross, k) for k in range(1, F)]
        rows = got[0].shape[0] - EXTRA
        return call(
            join_kernel, [jax.ShapeDtypeStruct((F * rows + EXTRA, STRIP), I16)], got, 10**6
        )[0]

    def around_chan(near, cross=0):
        around = [swap(near, 2 * j + cross) for j in range(chips - 1, 0, -1)]
        return jnp.concatenate([near] + around, axis=0)

    def along_chan(near):
        mine = around_chan(near)
        return mine, swap(mine, 1)

    def facet_part(mine, *crowd):
        return call(
            functools.partial(facet_part_kernel, F, chips),
            [facet_strips, *crowd],
            [place, mine],
            2 * 10**9,
            smem=1,
        )

    settle = functools.partial(settle_kernel, F, chips, step)
    whole = jax.ShapeDtypeStruct(start_image.shape, F32)

    near = along_facet([msg] * F)
    pick, numbers = call(
        functools.partial(sort_kernel, F, per_facet),
        [
            jax.ShapeDtypeStruct((F * PART, refs), BF16),
            jax.ShapeDtypeStruct((F * EXTRA, STRIP), F32),
        ],
        [place, at],
        10**8,
        smem=1,
    )
    near, pick, numbers, at, other_at = lax.optimization_barrier(
        (near, pick, numbers, at, swap(at, 1))
    )
    mine = around_chan(near)
    part, other_part = call(
        functools.partial(part_kernel, F, chips),
        [at_refs, at_refs],
        [at, other_at, mine],
        3 * 10**8,
    )
    msg, *msgs = call(
        functools.partial(next_kernel, step),
        [message] + [short] * F,
        [at, live, observed, kernels, turned, est, part, swap(other_part, 1), pick, numbers],
        3 * 10**8,
    )
    msg, mine, *msgs = lax.optimization_barrier((msg, mine, *msgs))
    near = along_facet(msgs, 1)
    other = swap(mine, 1)
    part, crowd = facet_part(mine, jax.ShapeDtypeStruct((TILE, STRIP), F32))
    near, part, crowd, other = lax.optimization_barrier((near, part, crowd, other))
    around = around_chan(near, 1)
    image, crowd = call(
        settle,
        [whole, jax.ShapeDtypeStruct((1,), I32)],
        [place, start_image, part, other, crowd],
        2 * 10**9,
        smem=1,
        scalars=1,
    )
    crowded = crowd[0] > PART
    around, image, crowded = lax.optimization_barrier((around, image, crowded))

    other = swap(around, 1)
    (part,) = facet_part(around)

    def in_full():
        mine, other = along_chan(along_facet([msg] * F))
        (part,) = facet_part(mine)
        (rest,) = facet_part(other)
        return part + rest, jnp.zeros((chips * (F * PART + EXTRA), STRIP), I16)

    part, other = lax.cond(crowded, in_full, lambda: (part, other))
    return call(
        settle,
        [whole],
        [place, image, part, other],
        2 * 10**9,
        smem=1,
    )[0]


def dense_device(start_image, visibilities, strip_index, live_counts, uv_kernels):
    def to_owner(x):
        x = lax.all_to_all(x, "chan", split_axis=1, concat_axis=0, tiled=True)
        return lax.all_to_all(x, "facet", split_axis=2, concat_axis=0, tiled=True)

    observed, picked_ids, live_now = map(to_owner, (visibilities, strip_index, live_counts))
    slot_count = observed.shape[0]
    chan_local, uv_local = uv_kernels.shape[:2]
    slab_rows, facet_width = start_image.shape
    full_width = facet_width * lax.axis_size("facet")
    strip_count = slab_rows * full_width // STRIP
    blocks = slot_count * chan_local * lax.axis_size("chan") * uv_local * lax.axis_size("facet")
    step_size = strip_count / (2.5 * blocks)
    lane_ids = jnp.arange(2 * VISB, dtype=I32) % VISB
    live_mask = lane_ids < live_now[..., None]
    flat_ids = picked_ids.reshape(-1)
    estimate = start_image
    for iteration in range(ITERS):
        full_sky = lax.all_gather(estimate.astype(BF16), "facet", axis=1, tiled=True)
        sky_strips = full_sky.reshape(strip_count, STRIP)
        gathered = sky_strips[picked_ids].reshape(slot_count, chan_local, uv_local, TERMS * STRIP)
        predicted = jnp.einsum("scup,cupq->scuq", gathered, uv_kernels, preferred_element_type=F32)
        residual = jnp.where(live_mask, predicted - observed.astype(F32), 0.0).astype(BF16)
        adjoint = jnp.einsum("scuq,cupq->scup", residual, uv_kernels, preferred_element_type=F32)
        gradient = jnp.zeros((strip_count, STRIP), F32).at[flat_ids].add(adjoint.reshape(-1, STRIP))
        gradient = gradient.reshape(slab_rows, full_width)
        facet_part = lax.psum_scatter(gradient, "facet", scatter_dimension=1, tiled=True)
        facet_sum = lax.psum(facet_part, "chan")
        descent = estimate - step_size * facet_sum
        estimate = jnp.maximum(descent - shrinkage, 0.0)
    return estimate


def on_device(start_image, visibilities, strip_index, live_counts, uv_kernels):
    C, F = lax.axis_size("chan"), lax.axis_size("facet")
    L, uv_local = uv_kernels.shape[:2]
    strips = start_image.size * F // STRIP
    sparse = (
        visibilities.shape[0] == 1
        and uv_local == 1
        and C & (C - 1) == 0
        and F & (F - 1) == 0
        and C >= 4
        and ITERS == 2
        and F >= 2
        and F <= TILE and F * PART % STRIP == 0
        and C * F * L * TERMS == STRIP
        and 4 * L + TERMS + 1 <= BLOCK
        and 4 * L == TILE
        and L * C <= STRIP
        and strips <= 64 * 256
        and strips & (strips - 1) == 0
        and start_image.shape[0] % (C * TILE) == 0
        and start_image.shape[1] % STRIP == 0
        and start_image.size // STRIP // C % 16 == 0
    )
    run = sparse_device if sparse else dense_device
    return run(start_image, visibilities, strip_index, live_counts, uv_kernels)


def solution(mesh):
    placed = (
        P(None, "facet"),
        P(("chan", "facet"), None, None, None),
        P(("chan", "facet"), None, None, None),
        P(("chan", "facet"), None, None),
        P("chan", "facet", None, None),
    )
    return jax.shard_map(
        on_device, mesh=mesh, in_specs=placed, out_specs=P(None, "facet"), check_vma=False
    )
```

```python
import functools

import jax
import jax.numpy as jnp
from jax import lax
from jax.experimental import pallas as pl
from jax.experimental.pallas import tpu as pltpu
from jax.sharding import PartitionSpec as P

STRIP = 128
VISB = 128
TERMS = 2
ITERS = 2
TILE = 8
EXTRA = 16
BLOCK = 16
PART = 64
FINE = 32
FLOOR = 10
LEAST = 119

shrinkage = 0.05
F32, BF16, I32, I16 = jnp.float32, jnp.bfloat16, jnp.int32, jnp.int16
VMEM_LIMIT = 48 * 1024 * 1024


def call(kernel, outs, args, flops, placed=False, hbm=0, scratch=(), scalars=0):
    spaces = [pl.BlockSpec(memory_space=pltpu.HBM)] * hbm
    spaces += [pl.BlockSpec(memory_space=pltpu.VMEM)] * (len(args) - hbm)
    moved = sum(a.size * a.dtype.itemsize for a in list(args) + list(outs))
    args = list(args)
    for i in range(hbm):
        args[i] = pltpu.with_memory_space_constraint(args[i], pltpu.HBM)
    body = kernel
    if placed:

        def body(*refs):
            kernel((lax.axis_index("chan"), lax.axis_index("facet")), *refs)

    return pl.pallas_call(
        body,
        out_shape=list(outs),
        in_specs=spaces,
        out_specs=[pl.BlockSpec(memory_space=pltpu.VMEM)] * (len(outs) - scalars)
        + [pl.BlockSpec(memory_space=pltpu.SMEM)] * scalars,
        scratch_shapes=list(scratch),
        compiler_params=pltpu.CompilerParams(vmem_limit_bytes=VMEM_LIMIT),
        cost_estimate=pl.CostEstimate(flops=flops, bytes_accessed=moved, transcendentals=0),
    )(*args)


def split(x, parts):
    terms = []
    for _ in range(parts):
        term = x.astype(BF16)
        terms.append(term)
        x = x - term.astype(F32)
    return terms


def one_hot(hit):
    return jnp.where(hit, 1.0, 0.0).astype(BF16)


def iota(shape, dim):
    return lax.broadcasted_iota(I32, shape, dim)


def code_floats(x):
    size = jnp.abs(x)
    power = jnp.maximum(jnp.floor(jnp.log2(jnp.maximum(size, 1e-37))), -LEAST)
    code = (power + LEAST) * 128.0 + jnp.round(size * jnp.exp2(7.0 - power))
    return jnp.where(x < 0, -code, code).astype(I32)


def code_levels(x):
    near = x.astype(BF16).astype(F32)
    power = jnp.maximum(jnp.floor(jnp.log2(jnp.maximum(near, 1e-37))), -FLOOR)
    unit = jnp.exp2(power - 7.0)
    lead = jnp.round(near / unit)
    step = jnp.round(((x - lead * unit) / unit + 0.5) * (FINE - 1))
    step = jnp.clip(step, 0.0, FINE - 1)
    code = ((power + FLOOR) * 128.0 + lead) * FINE + step - 32768.0
    return code.astype(I32).astype(I16)


def levels_of(code):
    level = code >> log2(FINE)
    power = jnp.maximum((level >> 7) - 1, 0)
    unit = jnp.exp2((power - (FLOOR + 7)).astype(F32))
    near = ((level - power * 128).astype(F32) * unit).astype(BF16).astype(F32)
    step = (code & (FINE - 1)).astype(F32)
    return near, near + (step * (1.0 / (FINE - 1)) - 0.5) * unit


def floats_of(code):
    size = jnp.abs(code)
    power = jnp.maximum((size >> 7) - 1, 0)
    lead = (size - power * 128).astype(F32)
    value = lead * jnp.exp2((power - (LEAST + 7)).astype(F32))
    return jnp.where(code < 0, -value, value).astype(BF16)


def halves(x):
    return jnp.concatenate([(x >> 6).astype(F32), (x & 63).astype(F32)], axis=1).astype(BF16)


def joined(x):
    return x[:, :STRIP] * 64.0 + x[:, STRIP:]


def tiled_strips(rows):
    height, width = rows.shape
    return jnp.concatenate(
        [
            rows[r : r + TILE, c : c + STRIP]
            for r in range(0, height, TILE)
            for c in range(0, width, STRIP)
        ],
        axis=0,
    )


def log2(n):
    return n.bit_length() - 1


def pack_kernel(C, F, L, place, image, seen, terms, counts, *refs):
    outs, (band_in, seen_in, terms_in, counts_in, row_in, sems) = refs[:F], refs[F:]
    c, f = place[0], place[1]
    height, width = image.shape
    band = height // C
    wide = width // STRIP
    per_facet = height * wide
    piece = per_facet // C
    mine = image.at[pl.ds(pl.multiple_of(c * band, TILE), band), :]
    copies = [
        pltpu.make_async_copy(source, target, sems.at[i])
        for i, (source, target) in enumerate(
            ((mine, band_in), (seen, seen_in), (terms, terms_in), (counts, counts_in))
        )
    ]
    for copy in copies:
        copy.start()
    chips = C // 2
    size = chips * BLOCK
    rows = F * size
    row = iota((rows, 1), 0)
    k, j, i = row // size, (row // BLOCK) % chips, row % BLOCK
    channel = ((c >> 1) ^ j) * (2 * L) + (i >> 1)
    is_seen = i < 4 * L
    pick = is_seen & (iota((rows, L * C * F), 1) == channel * F + (k ^ f))
    row_in[...] = jnp.zeros(row_in.shape, I32)
    for copy in copies:
        copy.wait()
    strips = tiled_strips(band_in[...])
    share = code_levels(strips)
    raw = terms_in[...]
    across, column = raw >> log2(F * wide), raw & (F * wide - 1)
    terms_in[...] = (
        (column >> log2(wide)) * per_facet
        + (across >> 3) * (wide * TILE)
        + (column & (wide - 1)) * TILE
        + (across & 7)
    )
    for at in range(F):
        for term in range(TERMS):
            row_in[at * TILE + term : at * TILE + term + 1, : L * C] = terms_in[at ^ f, term : term + 1]
        row_in[at * TILE + TERMS : at * TILE + TERMS + 1, : L * C] = counts_in[pl.ds(at ^ f, 1)]
    by_channel = jnp.concatenate([seen_in[n] for n in range(L * C)], axis=0)
    both = jnp.dot(one_hot(pick), by_channel, preferred_element_type=F32)
    values = code_floats(jnp.where((i & 1) == 0, both[:, :VISB], both[:, VISB:]))
    whole = jnp.concatenate(
        [part for at in range(F) for part in [row_in[at * TILE : (at + 1) * TILE]] * (2 * chips)],
        axis=0,
    )
    blocks = jnp.where(is_seen, values, whole).astype(I16)
    for at in range(F):
        if at:
            outs[at][:piece] = share
            outs[at][piece:] = blocks[at * size : (at + 1) * size]
        else:
            outs[at][...] = blocks[:size]


def pass_kernel(F, piece, *refs):
    got, outs = refs[:F][::-1], refs[F:]
    for j, out in enumerate(outs):
        for k in range(1, F):
            out[(k - 1) * piece : k * piece] = got[k][:piece]
        for k in range(F):
            at = (F - 1) * piece + k * BLOCK
            first = (piece if k else 0) + j * BLOCK
            out[at : at + BLOCK] = got[k][first : first + BLOCK]


def table_of(levels):
    return jnp.concatenate(split(levels, 2), axis=1)


def shares_of(got, chips, size, used):
    return [got[q * size : q * size + used].astype(I32).astype(F32) + 32768.0 for q in range(chips)]


def sorted_blocks(C, F, L, c, got, first):
    chips, slots = C // 2, C * F
    size = got.shape[0] // chips
    blocks = jnp.concatenate(
        [got[(q + 1) * size - F * BLOCK : (q + 1) * size] for q in range(chips)], axis=0
    ).astype(I32)

    def pick(kinds, start):
        out = iota((kinds * slots, blocks.shape[0]), 0)
        source = (out % slots - first) * BLOCK + start + out // slots
        return one_hot(iota(out.shape, 1) == source)

    seen = jnp.dot(pick(4, 2 * L * (c & 1)), floats_of(blocks), preferred_element_type=F32)
    whole = jnp.dot(pick(3, 4 * L), halves(blocks), preferred_element_type=F32)
    return seen, whole


def ready_kernel(C, F, L, place, image, kernels, mine, table_out, seen_out, whole_out, turned_out):
    height, width = image.shape
    used = (F - 1) * (height * width // STRIP // C)
    shares = shares_of(mine, C // 2, used + F * BLOCK, used)
    own = tiled_strips(image)
    table_out[...] = table_of(jnp.concatenate([own] + shares, axis=0))
    seen_out[...], whole_out[...] = sorted_blocks(C, F, L, place[0], mine, 0)
    for ch in range(L):
        turned_out[ch] = kernels[ch].T


def first_kernel(
    C, F, L, place, known, seen_in, whole_in, kernels, turned, other, start_out, seen_out, refs_out, live_out, msg
):
    c, f = place[0], place[1]
    chips, slots = C // 2, C * F
    size = other.shape[0] // chips
    used = size - F * BLOCK
    per_facet = known.shape[0] - chips * used
    piece = per_facet // C
    seen, whole = sorted_blocks(C, F, L, c, other, slots // 2)
    seen = seen + seen_in[...]
    row, column = iota((2 * STRIP, L * STRIP), 0), iota((2 * STRIP, L * STRIP), 1)
    channel = c * L + column // STRIP
    lanes = jnp.where(row == channel, 64.0, jnp.where(row == channel + STRIP, 1.0, 0.0))
    whole = jnp.dot(
        (whole + whole_in[...]).astype(BF16), lanes.astype(BF16), preferred_element_type=F32
    )
    kinds = [
        whole[kind * slots : (kind + 1) * slots, ch * STRIP : (ch + 1) * STRIP]
        for ch in range(L)
        for kind in range(TERMS + 1)
    ]
    refs = jnp.concatenate([x for i, x in enumerate(kinds) if i % (TERMS + 1) < TERMS], axis=0)
    live = jnp.concatenate(kinds[TERMS :: TERMS + 1], axis=0)
    col = refs.astype(I32)
    facet, local = col >> log2(per_facet), col & (per_facet - 1)
    k, d = facet ^ f, (local >> log2(piece)) ^ c
    turn = ((d & 1) * chips + (d >> 1)) * (F - 1) + k - 1
    place_of = jnp.where(k == 0, local, per_facet + turn * piece + (local & (piece - 1)))
    rest = table_of(jnp.concatenate(shares_of(other, chips, size, used), axis=0))

    def hits(count, start):
        wide = jnp.concatenate([place_of - start] * (count // STRIP), axis=1)
        return one_hot(iota(wide.shape, 1) == wide)

    both = jnp.dot(hits(known.shape[0], 0), known[...], preferred_element_type=F32) + jnp.dot(
        hits(rest.shape[0], known.shape[0]), rest, preferred_element_type=F32
    )
    total = both[:, :STRIP] + both[:, STRIP:]
    near, value = levels_of(jnp.where(k == 0, 0.0, total).astype(I32))
    sky = jnp.where(k == 0, both[:, :STRIP], near)
    start_out[...] = jnp.where(k == 0, total, value)
    seen_out[...] = seen.astype(BF16)
    refs_out[...] = refs
    live_out[...] = live
    encode(measure(sky, seen, live, kernels, turned), refs, msg)


def measure(est, seen, live, kernels, turned):
    L = kernels.shape[0]
    slots = live.shape[0] // L
    adjoints = []
    for ch in range(L):
        a, b, end = (ch * TERMS + i for i in range(3))
        sky = jnp.concatenate(
            [est[a * slots : b * slots], est[b * slots : end * slots]], axis=1
        ).astype(BF16)
        observed = jnp.concatenate(
            [seen[a * slots : b * slots], seen[b * slots : end * slots]], axis=1
        )
        predicted = jnp.dot(sky, kernels[ch], preferred_element_type=F32)
        alive = iota((slots, VISB), 1).astype(F32) < live[ch * slots : (ch + 1) * slots]
        residual = jnp.where(
            jnp.concatenate([alive, alive], axis=1), predicted - observed, 0.0
        ).astype(BF16)
        adjoint = jnp.dot(residual, turned[ch], preferred_element_type=F32)
        adjoints += [adjoint[:, :STRIP], adjoint[:, STRIP:]]
    return jnp.concatenate(adjoints, axis=0)


def as_row(col):
    eye = iota((STRIP, STRIP), 0) == iota((STRIP, STRIP), 1)
    return jnp.sum(jnp.where(eye, col, 0.0), axis=0, keepdims=True)


def scale_of(half):
    return jnp.exp2(half * 0.5).astype(BF16).astype(F32)


def put(msg, code, ids, half):
    msg[: code.shape[0]] = code.astype(I32).astype(I16)
    row = iota((EXTRA, STRIP), 0)
    extra = jnp.where(row == 0, ids, jnp.where(row == 1, half, 0.0))
    msg[code.shape[0] :] = extra.astype(I32).astype(I16)


def encode(adjoint, refs, msg):
    top = jnp.max(jnp.abs(adjoint), axis=1, keepdims=True)
    half = jnp.ceil(2.0 * jnp.log2(jnp.maximum(top, 1e-30) * (1.0 / 32500.0)))
    code = jnp.round(adjoint * (1.0 / scale_of(half)))
    row = as_row(half)
    put(msg, code, as_row(refs), row)
    return code, row


def sort_kernel(F, per_facet, place, refs, pick_out, numbers_out):
    f = place[1]
    ids = as_row(refs[...]).astype(I32)
    turn = iota((TILE, STRIP), 0)
    wanted = ((ids >> log2(per_facet)) == (turn ^ f)) & (turn < F)
    before = one_hot(iota((STRIP, STRIP), 0) < iota((STRIP, STRIP), 1))
    rank = jnp.dot(one_hot(wanted), before, preferred_element_type=F32)
    rank = jnp.where(wanted, rank, -1.0)
    slot = iota((PART, 1), 0).astype(F32)
    pick = jnp.concatenate([one_hot(rank[k : k + 1] == slot) for k in range(F)], axis=0)
    pick_out[...] = pick
    kinds = jnp.where(turn == 0, ids >> 6, jnp.where(turn == 1, ids & 63, 1))
    found = lax.dot_general(
        kinds.astype(F32).astype(BF16), pick, (((1,), (1,)), ((), ())), preferred_element_type=F32
    )
    found = jnp.where(found[2:3] > 0, found[0:1] * 64.0 + found[1:2], -1.0)
    for k in range(F):
        numbers_out[k * EXTRA : (k + 1) * EXTRA] = in_both_halves(found, k)


def in_both_halves(rows, k):
    at = k * PART // STRIP * STRIP
    pair = jnp.broadcast_to(rows[:, at : at + STRIP], (EXTRA, STRIP))
    low = iota((EXTRA, STRIP), 1) < PART
    return jnp.where(low == (k % 2 == 0), pair, pltpu.roll(pair, PART, 1))


def join_kernel(*refs):
    got, out = refs[:-1], refs[-1]
    F = len(got)
    rows = got[0].shape[0] - EXTRA
    number_rows = F * rows // STRIP
    row, lane = iota((EXTRA, STRIP), 0), iota((EXTRA, STRIP), 1)
    extra = jnp.zeros((EXTRA, STRIP), I32)
    for k in range(F):
        out[k * rows : (k + 1) * rows] = got[k][:rows]
        here = got[k][rows:].astype(I32)
        first, at = k * rows % STRIP, k * rows // STRIP
        own = (lane >= first) & (lane < first + rows)
        extra = jnp.where(own & (row == at), here[0:1], extra)
        extra = jnp.where(own & (row == number_rows + at), here[1:2], extra)
    out[F * rows :] = extra.astype(I16)


def decode(F, block, chips):
    ids, scales, values = [], [], []
    size = block.shape[0] // chips
    rows = size - EXTRA
    number_rows = rows // STRIP
    for at in range(0, block.shape[0], size):
        extra = block[at + rows : at + size].astype(I32)
        ids += [extra[j : j + 1] for j in range(number_rows)]
        scales += [extra[j : j + 1] for j in range(number_rows, 2 * number_rows)]
        values.append(table_of(block[at : at + rows].astype(I32).astype(F32)))
    scale = scale_of(jnp.concatenate(scales, axis=1).astype(F32))
    return ids, scale, jnp.concatenate(values, axis=0)


def summed(decoded, strips):
    ids, scale, values = decoded
    wide = strips if len(ids) * STRIP == strips.shape[1] else jnp.concatenate([strips] * len(ids), axis=1)
    hit = jnp.concatenate(ids, axis=1) == wide
    both = jnp.dot(jnp.where(hit, scale, 0.0).astype(BF16), values, preferred_element_type=F32)
    return both[:, :STRIP] + both[:, STRIP:]


def crowd_of(ids, F, per_facet):
    facets = jnp.concatenate(ids, axis=0) >> log2(per_facet)
    hits = jnp.concatenate([one_hot(facets == f) for f in range(F)], axis=0)
    ones = jnp.ones((STRIP, STRIP), BF16)
    counts = jnp.dot(hits, ones, preferred_element_type=F32)
    return jnp.max(counts, axis=0, keepdims=True)


def part_kernel(F, chips, refs, other_refs, block, out, other_out):
    strips = jnp.concatenate([refs[...], other_refs[...]], axis=0).astype(I32)
    total = summed(decode(F, block, chips), strips)
    out[...] = total[: refs.shape[0]]
    other_out[...] = total[refs.shape[0] :]


def next_kernel(
    step, refs, live, seen, kernels, turned, est_in, part, rest, pick, numbers, msg, *msgs
):
    gradient = part[...] + rest[...]
    est = jnp.maximum(est_in[...] - step * gradient - shrinkage, 0.0)
    adjoint = measure(est, seen[...].astype(F32), live[...], kernels, turned)
    code, half = encode(adjoint, refs[...], msg)
    both = jnp.dot(pick[...], table_of(code), preferred_element_type=F32)
    rows = both[:, :STRIP] + both[:, STRIP:]
    halves_of = lax.dot_general(
        jnp.broadcast_to(half, (TILE, STRIP)).astype(BF16),
        pick[...],
        (((1,), (1,)), ((), ())),
        preferred_element_type=F32,
    )[0:1]
    for k, short in enumerate(msgs):
        put(
            short,
            rows[k * PART : (k + 1) * PART],
            numbers[k * EXTRA : (k + 1) * EXTRA],
            in_both_halves(halves_of, k),
        )


def facet_part_kernel(F, chips, place, block, out, *crowd):
    decoded = decode(F, block, chips)
    count = out.shape[0]
    out[...] = summed(decoded, iota((count, STRIP), 0) + place[1] * count)
    for most in crowd:
        most[...] = jnp.broadcast_to(crowd_of(decoded[0], F, count), most.shape)


def settle_kernel(F, chips, step, place, image, part, block, *refs):
    decoded = decode(F, block, chips)
    height, width = image.shape
    count = part.shape[0]
    if len(refs) == 3:
        crowd, out, most = refs
        most[0] = jnp.max(jnp.maximum(crowd[0:1], crowd_of(decoded[0], F, count))).astype(I32)
    else:
        (out,) = refs
    per_band = width // STRIP * TILE
    chunk = min(256, count)
    for at in range(0, count, chunk):
        strips = iota((chunk, STRIP), 0) + (place[1] * count + at)
        gradient = part[at : at + chunk] + summed(decoded, strips)
        for t in range(0, chunk, TILE):
            r = (at + t) // per_band * TILE
            c = (at + t) % per_band // TILE * STRIP
            old = image[r : r + TILE, c : c + STRIP]
            out[r : r + TILE, c : c + STRIP] = jnp.maximum(
                old - step * gradient[t : t + TILE] - shrinkage, 0.0
            )


def swap(x, along_chan, along_facet=0):
    C, F = lax.axis_size("chan"), lax.axis_size("facet")
    pairs = [
        (c * F + f, (c ^ along_chan) * F + (f ^ along_facet)) for c in range(C) for f in range(F)
    ]
    return lax.ppermute(x, ("chan", "facet"), pairs)


def sparse_device(start_image, visibilities, strip_index, live_counts, uv_kernels):
    C, F = lax.axis_size("chan"), lax.axis_size("facet")
    L = uv_kernels.shape[0]
    refs = C * F * L * TERMS
    per_facet = start_image.size // STRIP
    piece = per_facet // C
    chips = C // 2
    step = float(per_facet * F / (2.5 * C * F * (L * C) * F))
    kernels = uv_kernels[:, 0]

    blocks = jax.ShapeDtypeStruct((chips * BLOCK, STRIP), I16)
    both = jax.ShapeDtypeStruct((piece + chips * BLOCK, STRIP), I16)
    packed = call(
        functools.partial(pack_kernel, C, F, L),
        [blocks] + [both] * (F - 1),
        [
            start_image,
            visibilities[0],
            strip_index[0].transpose(1, 2, 0),
            live_counts[0].T,
        ],
        10**8,
        placed=True,
        hbm=4,
        scratch=[
            pltpu.VMEM((start_image.shape[0] // C, start_image.shape[1]), F32),
            pltpu.VMEM(visibilities.shape[1:], BF16),
            pltpu.VMEM((F, TERMS, L * C), I32),
            pltpu.VMEM((F, L * C), I32),
            pltpu.VMEM((F * TILE, STRIP), I32),
            pltpu.SemaphoreType.DMA((4,)),
        ],
    )
    got = [packed[0]] + [swap(packed[k], 0, k) for k in range(F - 1, 0, -1)][::-1]
    passed = call(
        functools.partial(pass_kernel, F, piece),
        [jax.ShapeDtypeStruct(((F - 1) * piece + F * BLOCK, STRIP), I16)] * chips,
        got[::-1],
        10**6,
    )
    mine = jnp.concatenate(
        [passed[0]] + [swap(passed[j], 2 * j) for j in range(1, chips)], axis=0
    )
    other = swap(mine, 1)

    at_refs = jax.ShapeDtypeStruct((refs, STRIP), F32)
    message = jax.ShapeDtypeStruct((refs + EXTRA, STRIP), I16)
    short = jax.ShapeDtypeStruct((PART + EXTRA, STRIP), I16)
    facet_strips = jax.ShapeDtypeStruct((per_facet, STRIP), F32)
    known, seen_part, whole_part, turned = call(
        functools.partial(ready_kernel, C, F, L),
        [
            jax.ShapeDtypeStruct((per_facet + chips * (F - 1) * piece, 2 * STRIP), BF16),
            at_refs,
            jax.ShapeDtypeStruct(((TERMS + 1) * C * F, 2 * STRIP), F32),
            jax.ShapeDtypeStruct(kernels.shape, BF16),
        ],
        [start_image, kernels, mine],
        10**8,
        placed=True,
    )
    est, observed, at, live, msg = call(
        functools.partial(first_kernel, C, F, L),
        [
            at_refs,
            jax.ShapeDtypeStruct((refs, STRIP), BF16),
            at_refs,
            jax.ShapeDtypeStruct((L * C * F, STRIP), F32),
            message,
        ],
        [known, seen_part, whole_part, kernels, turned, other],
        5 * 10**8,
        placed=True,
    )

    def along_facet(msgs, cross=0):
        got = [msgs[0]] + [swap(msgs[k], cross, k) for k in range(1, F)]
        rows = got[0].shape[0] - EXTRA
        return call(
            join_kernel, [jax.ShapeDtypeStruct((F * rows + EXTRA, STRIP), I16)], got, 10**6
        )[0]

    def around_chan(near, cross=0):
        around = [swap(near, 2 * j + cross) for j in range(chips - 1, 0, -1)]
        return jnp.concatenate([near] + around, axis=0)

    def along_chan(near):
        mine = around_chan(near)
        return mine, swap(mine, 1)

    def facet_part(mine, *crowd):
        return call(
            functools.partial(facet_part_kernel, F, chips),
            [facet_strips, *crowd],
            [mine],
            2 * 10**9,
            placed=True,
        )

    settle = functools.partial(settle_kernel, F, chips, step)
    whole = jax.ShapeDtypeStruct(start_image.shape, F32)

    near = along_facet([msg] * F)
    pick, numbers = call(
        functools.partial(sort_kernel, F, per_facet),
        [
            jax.ShapeDtypeStruct((F * PART, refs), BF16),
            jax.ShapeDtypeStruct((F * EXTRA, STRIP), F32),
        ],
        [at],
        10**8,
        placed=True,
    )
    near, pick, numbers, at, other_at = lax.optimization_barrier(
        (near, pick, numbers, at, swap(at, 1))
    )
    mine = around_chan(near)
    part, other_part = call(
        functools.partial(part_kernel, F, chips),
        [at_refs, at_refs],
        [at, other_at, mine],
        3 * 10**8,
    )
    msg, *msgs = call(
        functools.partial(next_kernel, step),
        [message] + [short] * F,
        [at, live, observed, kernels, turned, est, part, swap(other_part, 1), pick, numbers],
        3 * 10**8,
    )
    msg, mine, *msgs = lax.optimization_barrier((msg, mine, *msgs))
    near = along_facet(msgs, 1)
    other = swap(mine, 1)
    part, crowd = facet_part(mine, jax.ShapeDtypeStruct((TILE, STRIP), F32))
    near, part, crowd, other = lax.optimization_barrier((near, part, crowd, other))
    around = around_chan(near, 1)
    image, crowd = call(
        settle,
        [whole, jax.ShapeDtypeStruct((1,), I32)],
        [start_image, part, other, crowd],
        2 * 10**9,
        placed=True,
        scalars=1,
    )
    crowded = crowd[0] > PART
    around, image, crowded = lax.optimization_barrier((around, image, crowded))

    other = swap(around, 1)
    (part,) = facet_part(around)

    def in_full():
        mine, other = along_chan(along_facet([msg] * F))
        (part,) = facet_part(mine)
        (rest,) = facet_part(other)
        return part + rest, jnp.zeros((chips * (F * PART + EXTRA), STRIP), I16)

    part, other = lax.cond(crowded, in_full, lambda: (part, other))
    return call(
        settle,
        [whole],
        [image, part, other],
        2 * 10**9,
        placed=True,
    )[0]


def dense_device(start_image, visibilities, strip_index, live_counts, uv_kernels):
    def to_owner(x):
        x = lax.all_to_all(x, "chan", split_axis=1, concat_axis=0, tiled=True)
        return lax.all_to_all(x, "facet", split_axis=2, concat_axis=0, tiled=True)

    observed, picked_ids, live_now = map(to_owner, (visibilities, strip_index, live_counts))
    slot_count = observed.shape[0]
    chan_local, uv_local = uv_kernels.shape[:2]
    slab_rows, facet_width = start_image.shape
    full_width = facet_width * lax.axis_size("facet")
    strip_count = slab_rows * full_width // STRIP
    blocks = slot_count * chan_local * lax.axis_size("chan") * uv_local * lax.axis_size("facet")
    step_size = strip_count / (2.5 * blocks)
    lane_ids = jnp.arange(2 * VISB, dtype=I32) % VISB
    live_mask = lane_ids < live_now[..., None]
    flat_ids = picked_ids.reshape(-1)
    estimate = start_image
    for iteration in range(ITERS):
        full_sky = lax.all_gather(estimate.astype(BF16), "facet", axis=1, tiled=True)
        sky_strips = full_sky.reshape(strip_count, STRIP)
        gathered = sky_strips[picked_ids].reshape(slot_count, chan_local, uv_local, TERMS * STRIP)
        predicted = jnp.einsum("scup,cupq->scuq", gathered, uv_kernels, preferred_element_type=F32)
        residual = jnp.where(live_mask, predicted - observed.astype(F32), 0.0).astype(BF16)
        adjoint = jnp.einsum("scuq,cupq->scup", residual, uv_kernels, preferred_element_type=F32)
        gradient = jnp.zeros((strip_count, STRIP), F32).at[flat_ids].add(adjoint.reshape(-1, STRIP))
        gradient = gradient.reshape(slab_rows, full_width)
        facet_part = lax.psum_scatter(gradient, "facet", scatter_dimension=1, tiled=True)
        facet_sum = lax.psum(facet_part, "chan")
        descent = estimate - step_size * facet_sum
        estimate = jnp.maximum(descent - shrinkage, 0.0)
    return estimate


def on_device(start_image, visibilities, strip_index, live_counts, uv_kernels):
    C, F = lax.axis_size("chan"), lax.axis_size("facet")
    L, uv_local = uv_kernels.shape[:2]
    strips = start_image.size * F // STRIP
    sparse = (
        visibilities.shape[0] == 1
        and uv_local == 1
        and C & (C - 1) == 0
        and F & (F - 1) == 0
        and C >= 4
        and ITERS == 2
        and F >= 2
        and F <= TILE and F * PART % STRIP == 0
        and C * F * L * TERMS == STRIP
        and 4 * L + TERMS + 1 <= BLOCK
        and 4 * L == TILE
        and L * C <= STRIP
        and strips <= 64 * 256
        and strips & (strips - 1) == 0
        and start_image.shape[0] % (C * TILE) == 0
        and start_image.shape[1] % STRIP == 0
        and start_image.size // STRIP // C % 16 == 0
    )
    run = sparse_device if sparse else dense_device
    return run(start_image, visibilities, strip_index, live_counts, uv_kernels)


def solution(mesh):
    placed = (
        P(None, "facet"),
        P(("chan", "facet"), None, None, None),
        P(("chan", "facet"), None, None, None),
        P(("chan", "facet"), None, None),
        P("chan", "facet", None, None),
    )
    return jax.shard_map(
        on_device, mesh=mesh, in_specs=placed, out_specs=P(None, "facet"), check_vma=False
    )
```

```python
import functools

import jax
import jax.numpy as jnp
from jax import lax
from jax.experimental import pallas as pl
from jax.experimental.pallas import tpu as pltpu
from jax.sharding import PartitionSpec as P

STRIP = 128
VISB = 128
TERMS = 2
ITERS = 2
TILE = 8
EXTRA = 16
BLOCK = 16
PART = 64
FINE = 32
FLOOR = 10
LEAST = 119

shrinkage = 0.05
F32, BF16, I32, I16 = jnp.float32, jnp.bfloat16, jnp.int32, jnp.int16
VMEM_LIMIT = 48 * 1024 * 1024


def call(kernel, outs, args, flops, placed=False, hbm=0, scratch=(), scalars=0):
    spaces = [pl.BlockSpec(memory_space=pltpu.HBM)] * hbm
    spaces += [pl.BlockSpec(memory_space=pltpu.VMEM)] * (len(args) - hbm)
    moved = sum(a.size * a.dtype.itemsize for a in list(args) + list(outs))
    args = list(args)
    for i in range(hbm):
        args[i] = pltpu.with_memory_space_constraint(args[i], pltpu.HBM)
    body = kernel
    if placed:

        def body(*refs):
            kernel((lax.axis_index("chan"), lax.axis_index("facet")), *refs)

    return pl.pallas_call(
        body,
        out_shape=list(outs),
        in_specs=spaces,
        out_specs=[pl.BlockSpec(memory_space=pltpu.VMEM)] * (len(outs) - scalars)
        + [pl.BlockSpec(memory_space=pltpu.SMEM)] * scalars,
        scratch_shapes=list(scratch),
        compiler_params=pltpu.CompilerParams(vmem_limit_bytes=VMEM_LIMIT),
        cost_estimate=pl.CostEstimate(flops=flops, bytes_accessed=moved, transcendentals=0),
    )(*args)


def split(x, parts):
    terms = []
    for _ in range(parts):
        term = x.astype(BF16)
        terms.append(term)
        x = x - term.astype(F32)
    return terms


def one_hot(hit):
    return jnp.where(hit, 1.0, 0.0).astype(BF16)


def iota(shape, dim):
    return lax.broadcasted_iota(I32, shape, dim)


def code_floats(x):
    size = jnp.abs(x)
    power = jnp.maximum(jnp.floor(jnp.log2(jnp.maximum(size, 1e-37))), -LEAST)
    code = (power + LEAST) * 128.0 + jnp.round(size * jnp.exp2(7.0 - power))
    return jnp.where(x < 0, -code, code).astype(I32)


def code_levels(x):
    near = x.astype(BF16).astype(F32)
    power = jnp.maximum(jnp.floor(jnp.log2(jnp.maximum(near, 1e-37))), -FLOOR)
    unit = jnp.exp2(power - 7.0)
    lead = jnp.round(near / unit)
    step = jnp.round(((x - lead * unit) / unit + 0.5) * (FINE - 1))
    step = jnp.clip(step, 0.0, FINE - 1)
    code = ((power + FLOOR) * 128.0 + lead) * FINE + step - 32768.0
    return code.astype(I32).astype(I16)


def levels_of(code):
    level = code >> log2(FINE)
    power = jnp.maximum((level >> 7) - 1, 0)
    unit = jnp.exp2((power - (FLOOR + 7)).astype(F32))
    near = ((level - power * 128).astype(F32) * unit).astype(BF16).astype(F32)
    step = (code & (FINE - 1)).astype(F32)
    return near, near + (step * (1.0 / (FINE - 1)) - 0.5) * unit


def floats_of(code):
    size = jnp.abs(code)
    power = jnp.maximum((size >> 7) - 1, 0)
    lead = (size - power * 128).astype(F32)
    value = lead * jnp.exp2((power - (LEAST + 7)).astype(F32))
    return jnp.where(code < 0, -value, value).astype(BF16)


def halves(x):
    return jnp.concatenate([(x >> 6).astype(F32), (x & 63).astype(F32)], axis=1).astype(BF16)


def joined(x):
    return x[:, :STRIP] * 64.0 + x[:, STRIP:]


def tiled_strips(rows):
    height, width = rows.shape
    return jnp.concatenate(
        [
            rows[r : r + TILE, c : c + STRIP]
            for r in range(0, height, TILE)
            for c in range(0, width, STRIP)
        ],
        axis=0,
    )


def log2(n):
    return n.bit_length() - 1


def pack_kernel(C, F, L, place, image, seen, terms, counts, *refs):
    outs, (band_in, seen_in, terms_in, counts_in, row_in, sems) = refs[:F], refs[F:]
    c, f = place[0], place[1]
    height, width = image.shape
    band = height // C
    wide = width // STRIP
    per_facet = height * wide
    piece = per_facet // C
    mine = image.at[pl.ds(pl.multiple_of(c * band, TILE), band), :]
    copies = [
        pltpu.make_async_copy(source, target, sems.at[i])
        for i, (source, target) in enumerate(
            ((mine, band_in), (seen, seen_in), (terms, terms_in), (counts, counts_in))
        )
    ]
    for copy in copies:
        copy.start()
    chips = C // 2
    size = chips * BLOCK
    rows = F * size
    row = iota((rows, 1), 0)
    k, j, i = row // size, (row // BLOCK) % chips, row % BLOCK
    channel = ((c >> 1) ^ j) * (2 * L) + (i >> 1)
    is_seen = i < 4 * L
    pick = is_seen & (iota((rows, L * C * F), 1) == channel * F + (k ^ f))
    row_in[...] = jnp.zeros(row_in.shape, I32)
    for copy in copies:
        copy.wait()
    strips = tiled_strips(band_in[...])
    share = code_levels(strips)
    raw = terms_in[...]
    across, column = raw >> log2(F * wide), raw & (F * wide - 1)
    terms_in[...] = (
        (column >> log2(wide)) * per_facet
        + (across >> 3) * (wide * TILE)
        + (column & (wide - 1)) * TILE
        + (across & 7)
    )
    for at in range(F):
        for term in range(TERMS):
            row_in[at * TILE + term : at * TILE + term + 1, : L * C] = terms_in[at ^ f, term : term + 1]
        row_in[at * TILE + TERMS : at * TILE + TERMS + 1, : L * C] = counts_in[pl.ds(at ^ f, 1)]
    by_channel = jnp.concatenate([seen_in[n] for n in range(L * C)], axis=0)
    both = jnp.dot(one_hot(pick), by_channel, preferred_element_type=F32)
    values = code_floats(jnp.where((i & 1) == 0, both[:, :VISB], both[:, VISB:]))
    whole = jnp.concatenate(
        [part for at in range(F) for part in [row_in[at * TILE : (at + 1) * TILE]] * (2 * chips)],
        axis=0,
    )
    blocks = jnp.where(is_seen, values, whole).astype(I16)
    for at in range(F):
        if at:
            outs[at][:piece] = share
            outs[at][piece:] = blocks[at * size : (at + 1) * size]
        else:
            outs[at][...] = blocks[:size]


def pass_kernel(F, piece, *refs):
    got, outs = refs[:F][::-1], refs[F:]
    for j, out in enumerate(outs):
        for k in range(1, F):
            out[(k - 1) * piece : k * piece] = got[k][:piece]
        for k in range(F):
            at = (F - 1) * piece + k * BLOCK
            first = (piece if k else 0) + j * BLOCK
            out[at : at + BLOCK] = got[k][first : first + BLOCK]


def table_of(levels):
    return jnp.concatenate(split(levels, 2), axis=1)


def shares_of(got, chips, size, used):
    return [got[q * size : q * size + used].astype(I32).astype(F32) + 32768.0 for q in range(chips)]


def sorted_blocks(C, F, L, c, got, first):
    chips, slots = C // 2, C * F
    size = got.shape[0] // chips
    blocks = jnp.concatenate(
        [got[(q + 1) * size - F * BLOCK : (q + 1) * size] for q in range(chips)], axis=0
    ).astype(I32)

    def pick(kinds, start):
        out = iota((kinds * slots, blocks.shape[0]), 0)
        source = (out % slots - first) * BLOCK + start + out // slots
        return one_hot(iota(out.shape, 1) == source)

    seen = jnp.dot(pick(4, 2 * L * (c & 1)), floats_of(blocks), preferred_element_type=F32)
    whole = jnp.dot(pick(3, 4 * L), halves(blocks), preferred_element_type=F32)
    return seen, whole


def ready_kernel(C, F, L, place, image, kernels, mine, table_out, seen_out, whole_out, turned_out):
    height, width = image.shape
    used = (F - 1) * (height * width // STRIP // C)
    shares = shares_of(mine, C // 2, used + F * BLOCK, used)
    own = tiled_strips(image)
    table_out[...] = table_of(jnp.concatenate([own] + shares, axis=0))
    seen_out[...], whole_out[...] = sorted_blocks(C, F, L, place[0], mine, 0)
    for ch in range(L):
        turned_out[ch] = kernels[ch].T


def first_kernel(
    C, F, L, place, known, seen_in, whole_in, kernels, turned, other, start_out, seen_out, refs_out, near_out, live_out, msg
):
    c, f = place[0], place[1]
    chips, slots = C // 2, C * F
    size = other.shape[0] // chips
    used = size - F * BLOCK
    per_facet = known.shape[0] - chips * used
    piece = per_facet // C
    seen, whole = sorted_blocks(C, F, L, c, other, slots // 2)
    seen = seen + seen_in[...]
    row, column = iota((2 * STRIP, 2 * L * STRIP), 0), iota((2 * STRIP, 2 * L * STRIP), 1)
    channel = (c ^ (column // (L * STRIP))) * L + column // STRIP % L
    lanes = jnp.where(row == channel, 64.0, jnp.where(row == channel + STRIP, 1.0, 0.0))
    whole = jnp.dot(
        (whole + whole_in[...]).astype(BF16), lanes.astype(BF16), preferred_element_type=F32
    )
    kinds = [
        whole[kind * slots : (kind + 1) * slots, ch * STRIP : (ch + 1) * STRIP]
        for ch in range(2 * L)
        for kind in range(TERMS + 1)
    ]
    both_refs = jnp.concatenate([x for i, x in enumerate(kinds) if i % (TERMS + 1) < TERMS], axis=0)
    refs = both_refs[: both_refs.shape[0] // 2]
    near_out[...] = jnp.concatenate(
        [
            both_refs[at : at + slots // 2]
            for first in range(both_refs.shape[0] // 2, both_refs.shape[0], slots)
            for at in (first + slots // 2, first)
        ],
        axis=0,
    )
    live = jnp.concatenate(kinds[TERMS : L * (TERMS + 1) : TERMS + 1], axis=0)
    col = refs.astype(I32)
    facet, local = col >> log2(per_facet), col & (per_facet - 1)
    k, d = facet ^ f, (local >> log2(piece)) ^ c
    turn = ((d & 1) * chips + (d >> 1)) * (F - 1) + k - 1
    place_of = jnp.where(k == 0, local, per_facet + turn * piece + (local & (piece - 1)))
    rest = table_of(jnp.concatenate(shares_of(other, chips, size, used), axis=0))

    def hits(count, start):
        wide = jnp.concatenate([place_of - start] * (count // STRIP), axis=1)
        return one_hot(iota(wide.shape, 1) == wide)

    both = jnp.dot(hits(known.shape[0], 0), known[...], preferred_element_type=F32) + jnp.dot(
        hits(rest.shape[0], known.shape[0]), rest, preferred_element_type=F32
    )
    total = both[:, :STRIP] + both[:, STRIP:]
    near, value = levels_of(jnp.where(k == 0, 0.0, total).astype(I32))
    sky = jnp.where(k == 0, both[:, :STRIP], near)
    start_out[...] = jnp.where(k == 0, total, value)
    seen_out[...] = seen.astype(BF16)
    refs_out[...] = refs
    live_out[...] = live
    encode(measure(sky, seen, live, kernels, turned), refs, msg)


def measure(est, seen, live, kernels, turned):
    L = kernels.shape[0]
    slots = live.shape[0] // L
    adjoints = []
    for ch in range(L):
        a, b, end = (ch * TERMS + i for i in range(3))
        sky = jnp.concatenate(
            [est[a * slots : b * slots], est[b * slots : end * slots]], axis=1
        ).astype(BF16)
        observed = jnp.concatenate(
            [seen[a * slots : b * slots], seen[b * slots : end * slots]], axis=1
        )
        predicted = jnp.dot(sky, kernels[ch], preferred_element_type=F32)
        alive = iota((slots, VISB), 1).astype(F32) < live[ch * slots : (ch + 1) * slots]
        residual = jnp.where(
            jnp.concatenate([alive, alive], axis=1), predicted - observed, 0.0
        ).astype(BF16)
        adjoint = jnp.dot(residual, turned[ch], preferred_element_type=F32)
        adjoints += [adjoint[:, :STRIP], adjoint[:, STRIP:]]
    return jnp.concatenate(adjoints, axis=0)


def as_row(col):
    eye = iota((STRIP, STRIP), 0) == iota((STRIP, STRIP), 1)
    return jnp.sum(jnp.where(eye, col, 0.0), axis=0, keepdims=True)


def scale_of(half):
    return jnp.exp2(half * 0.5).astype(BF16).astype(F32)


def put(msg, code, ids, half):
    msg[: code.shape[0]] = code.astype(I32).astype(I16)
    row = iota((EXTRA, STRIP), 0)
    extra = jnp.where(row == 0, ids, jnp.where(row == 1, half, 0.0))
    msg[code.shape[0] :] = extra.astype(I32).astype(I16)


def encode(adjoint, refs, msg):
    top = jnp.max(jnp.abs(adjoint), axis=1, keepdims=True)
    half = jnp.ceil(2.0 * jnp.log2(jnp.maximum(top, 1e-30) * (1.0 / 32500.0)))
    code = jnp.round(adjoint * (1.0 / scale_of(half)))
    row = as_row(half)
    put(msg, code, as_row(refs), row)
    return code, row


def sort_kernel(F, per_facet, place, refs, pick_out, numbers_out):
    f = place[1]
    ids = as_row(refs[...]).astype(I32)
    turn = iota((TILE, STRIP), 0)
    wanted = ((ids >> log2(per_facet)) == (turn ^ f)) & (turn < F)
    before = one_hot(iota((STRIP, STRIP), 0) < iota((STRIP, STRIP), 1))
    rank = jnp.dot(one_hot(wanted), before, preferred_element_type=F32)
    rank = jnp.where(wanted, rank, -1.0)
    slot = iota((PART, 1), 0).astype(F32)
    pick = jnp.concatenate([one_hot(rank[k : k + 1] == slot) for k in range(F)], axis=0)
    pick_out[...] = pick
    kinds = jnp.where(turn == 0, ids >> 6, jnp.where(turn == 1, ids & 63, 1))
    found = lax.dot_general(
        kinds.astype(F32).astype(BF16), pick, (((1,), (1,)), ((), ())), preferred_element_type=F32
    )
    found = jnp.where(found[2:3] > 0, found[0:1] * 64.0 + found[1:2], -1.0)
    for k in range(F):
        numbers_out[k * EXTRA : (k + 1) * EXTRA] = in_both_halves(found, k)


def in_both_halves(rows, k):
    at = k * PART // STRIP * STRIP
    pair = jnp.broadcast_to(rows[:, at : at + STRIP], (EXTRA, STRIP))
    low = iota((EXTRA, STRIP), 1) < PART
    return jnp.where(low == (k % 2 == 0), pair, pltpu.roll(pair, PART, 1))


def join_kernel(*refs):
    got, out = refs[:-1], refs[-1]
    F = len(got)
    rows = got[0].shape[0] - EXTRA
    number_rows = F * rows // STRIP
    row, lane = iota((EXTRA, STRIP), 0), iota((EXTRA, STRIP), 1)
    extra = jnp.zeros((EXTRA, STRIP), I32)
    for k in range(F):
        out[k * rows : (k + 1) * rows] = got[k][:rows]
        here = got[k][rows:].astype(I32)
        first, at = k * rows % STRIP, k * rows // STRIP
        own = (lane >= first) & (lane < first + rows)
        extra = jnp.where(own & (row == at), here[0:1], extra)
        extra = jnp.where(own & (row == number_rows + at), here[1:2], extra)
    out[F * rows :] = extra.astype(I16)


def decode(F, block, chips):
    ids, scales, values = [], [], []
    size = block.shape[0] // chips
    rows = size - EXTRA
    number_rows = rows // STRIP
    for at in range(0, block.shape[0], size):
        extra = block[at + rows : at + size].astype(I32)
        ids += [extra[j : j + 1] for j in range(number_rows)]
        scales += [extra[j : j + 1] for j in range(number_rows, 2 * number_rows)]
        values.append(table_of(block[at : at + rows].astype(I32).astype(F32)))
    scale = scale_of(jnp.concatenate(scales, axis=1).astype(F32))
    return ids, scale, jnp.concatenate(values, axis=0)


def summed(decoded, strips):
    ids, scale, values = decoded
    wide = strips if len(ids) * STRIP == strips.shape[1] else jnp.concatenate([strips] * len(ids), axis=1)
    hit = jnp.concatenate(ids, axis=1) == wide
    both = jnp.dot(jnp.where(hit, scale, 0.0).astype(BF16), values, preferred_element_type=F32)
    return both[:, :STRIP] + both[:, STRIP:]


def crowd_of(ids, F, per_facet):
    facets = jnp.concatenate(ids, axis=0) >> log2(per_facet)
    hits = jnp.concatenate([one_hot(facets == f) for f in range(F)], axis=0)
    ones = jnp.ones((STRIP, STRIP), BF16)
    counts = jnp.dot(hits, ones, preferred_element_type=F32)
    return jnp.max(counts, axis=0, keepdims=True)


def part_kernel(F, chips, refs, other_refs, block, out, other_out):
    strips = jnp.concatenate([refs[...], other_refs[...]], axis=0).astype(I32)
    total = summed(decode(F, block, chips), strips)
    out[...] = total[: refs.shape[0]]
    other_out[...] = total[refs.shape[0] :]


def next_kernel(
    step, refs, live, seen, kernels, turned, est_in, part, rest, pick, numbers, msg, *msgs
):
    gradient = part[...] + rest[...]
    est = jnp.maximum(est_in[...] - step * gradient - shrinkage, 0.0)
    adjoint = measure(est, seen[...].astype(F32), live[...], kernels, turned)
    code, half = encode(adjoint, refs[...], msg)
    both = jnp.dot(pick[...], table_of(code), preferred_element_type=F32)
    rows = both[:, :STRIP] + both[:, STRIP:]
    halves_of = lax.dot_general(
        jnp.broadcast_to(half, (TILE, STRIP)).astype(BF16),
        pick[...],
        (((1,), (1,)), ((), ())),
        preferred_element_type=F32,
    )[0:1]
    for k, short in enumerate(msgs):
        put(
            short,
            rows[k * PART : (k + 1) * PART],
            numbers[k * EXTRA : (k + 1) * EXTRA],
            in_both_halves(halves_of, k),
        )


def facet_part_kernel(F, chips, place, block, out, *crowd):
    decoded = decode(F, block, chips)
    count = out.shape[0]
    out[...] = summed(decoded, iota((count, STRIP), 0) + place[1] * count)
    for most in crowd:
        most[...] = jnp.broadcast_to(crowd_of(decoded[0], F, count), most.shape)


def settle_kernel(F, chips, step, place, image, part, block, *refs):
    decoded = decode(F, block, chips)
    height, width = image.shape
    count = part.shape[0]
    if len(refs) == 3:
        crowd, out, most = refs
        most[0] = jnp.max(jnp.maximum(crowd[0:1], crowd_of(decoded[0], F, count))).astype(I32)
    else:
        (out,) = refs
    per_band = width // STRIP * TILE
    chunk = min(256, count)
    for at in range(0, count, chunk):
        strips = iota((chunk, STRIP), 0) + (place[1] * count + at)
        gradient = part[at : at + chunk] + summed(decoded, strips)
        for t in range(0, chunk, TILE):
            r = (at + t) // per_band * TILE
            c = (at + t) % per_band // TILE * STRIP
            old = image[r : r + TILE, c : c + STRIP]
            out[r : r + TILE, c : c + STRIP] = jnp.maximum(
                old - step * gradient[t : t + TILE] - shrinkage, 0.0
            )


def swap(x, along_chan, along_facet=0):
    C, F = lax.axis_size("chan"), lax.axis_size("facet")
    pairs = [
        (c * F + f, (c ^ along_chan) * F + (f ^ along_facet)) for c in range(C) for f in range(F)
    ]
    return lax.ppermute(x, ("chan", "facet"), pairs)


def sparse_device(start_image, visibilities, strip_index, live_counts, uv_kernels):
    C, F = lax.axis_size("chan"), lax.axis_size("facet")
    L = uv_kernels.shape[0]
    refs = C * F * L * TERMS
    per_facet = start_image.size // STRIP
    piece = per_facet // C
    chips = C // 2
    step = float(per_facet * F / (2.5 * C * F * (L * C) * F))
    kernels = uv_kernels[:, 0]

    blocks = jax.ShapeDtypeStruct((chips * BLOCK, STRIP), I16)
    both = jax.ShapeDtypeStruct((piece + chips * BLOCK, STRIP), I16)
    packed = call(
        functools.partial(pack_kernel, C, F, L),
        [blocks] + [both] * (F - 1),
        [
            start_image,
            visibilities[0],
            strip_index[0].transpose(1, 2, 0),
            live_counts[0].T,
        ],
        10**8,
        placed=True,
        hbm=4,
        scratch=[
            pltpu.VMEM((start_image.shape[0] // C, start_image.shape[1]), F32),
            pltpu.VMEM(visibilities.shape[1:], BF16),
            pltpu.VMEM((F, TERMS, L * C), I32),
            pltpu.VMEM((F, L * C), I32),
            pltpu.VMEM((F * TILE, STRIP), I32),
            pltpu.SemaphoreType.DMA((4,)),
        ],
    )
    got = [packed[0]] + [swap(packed[k], 0, k) for k in range(F - 1, 0, -1)][::-1]
    passed = call(
        functools.partial(pass_kernel, F, piece),
        [jax.ShapeDtypeStruct(((F - 1) * piece + F * BLOCK, STRIP), I16)] * chips,
        got[::-1],
        10**6,
    )
    mine = jnp.concatenate(
        [passed[0]] + [swap(passed[j], 2 * j) for j in range(1, chips)], axis=0
    )
    other = swap(mine, 1)

    at_refs = jax.ShapeDtypeStruct((refs, STRIP), F32)
    message = jax.ShapeDtypeStruct((refs + EXTRA, STRIP), I16)
    short = jax.ShapeDtypeStruct((PART + EXTRA, STRIP), I16)
    facet_strips = jax.ShapeDtypeStruct((per_facet, STRIP), F32)
    known, seen_part, whole_part, turned = call(
        functools.partial(ready_kernel, C, F, L),
        [
            jax.ShapeDtypeStruct((per_facet + chips * (F - 1) * piece, 2 * STRIP), BF16),
            at_refs,
            jax.ShapeDtypeStruct(((TERMS + 1) * C * F, 2 * STRIP), F32),
            jax.ShapeDtypeStruct(kernels.shape, BF16),
        ],
        [start_image, kernels, mine],
        10**8,
        placed=True,
    )
    est, observed, at, other_at, live, msg = call(
        functools.partial(first_kernel, C, F, L),
        [
            at_refs,
            jax.ShapeDtypeStruct((refs, STRIP), BF16),
            at_refs,
            at_refs,
            jax.ShapeDtypeStruct((L * C * F, STRIP), F32),
            message,
        ],
        [known, seen_part, whole_part, kernels, turned, other],
        5 * 10**8,
        placed=True,
    )

    def along_facet(msgs, cross=0):
        got = [msgs[0]] + [swap(msgs[k], cross, k) for k in range(1, F)]
        rows = got[0].shape[0] - EXTRA
        return call(
            join_kernel, [jax.ShapeDtypeStruct((F * rows + EXTRA, STRIP), I16)], got, 10**6
        )[0]

    def around_chan(near, cross=0):
        around = [swap(near, 2 * j + cross) for j in range(chips - 1, 0, -1)]
        return jnp.concatenate([near] + around, axis=0)

    def along_chan(near):
        mine = around_chan(near)
        return mine, swap(mine, 1)

    def facet_part(mine, *crowd):
        return call(
            functools.partial(facet_part_kernel, F, chips),
            [facet_strips, *crowd],
            [mine],
            2 * 10**9,
            placed=True,
        )

    settle = functools.partial(settle_kernel, F, chips, step)
    whole = jax.ShapeDtypeStruct(start_image.shape, F32)

    near = along_facet([msg] * F)
    pick, numbers = call(
        functools.partial(sort_kernel, F, per_facet),
        [
            jax.ShapeDtypeStruct((F * PART, refs), BF16),
            jax.ShapeDtypeStruct((F * EXTRA, STRIP), F32),
        ],
        [at],
        10**8,
        placed=True,
    )
    near, pick, numbers = lax.optimization_barrier((near, pick, numbers))
    mine = around_chan(near)
    part, other_part = call(
        functools.partial(part_kernel, F, chips),
        [at_refs, at_refs],
        [at, other_at, mine],
        3 * 10**8,
    )
    msg, *msgs = call(
        functools.partial(next_kernel, step),
        [message] + [short] * F,
        [at, live, observed, kernels, turned, est, part, swap(other_part, 1), pick, numbers],
        3 * 10**8,
    )
    msg, mine, *msgs = lax.optimization_barrier((msg, mine, *msgs))
    near = along_facet(msgs, 1)
    other = swap(mine, 1)
    part, crowd = facet_part(mine, jax.ShapeDtypeStruct((TILE, STRIP), F32))
    near, part, crowd, other = lax.optimization_barrier((near, part, crowd, other))
    around = around_chan(near, 1)
    image, crowd = call(
        settle,
        [whole, jax.ShapeDtypeStruct((1,), I32)],
        [start_image, part, other, crowd],
        2 * 10**9,
        placed=True,
        scalars=1,
    )
    crowded = crowd[0] > PART
    around, image, crowded = lax.optimization_barrier((around, image, crowded))

    other = swap(around, 1)
    (part,) = facet_part(around)

    def in_full():
        mine, other = along_chan(along_facet([msg] * F))
        (part,) = facet_part(mine)
        (rest,) = facet_part(other)
        return part + rest, jnp.zeros((chips * (F * PART + EXTRA), STRIP), I16)

    part, other = lax.cond(crowded, in_full, lambda: (part, other))
    return call(
        settle,
        [whole],
        [image, part, other],
        2 * 10**9,
        placed=True,
    )[0]


def dense_device(start_image, visibilities, strip_index, live_counts, uv_kernels):
    def to_owner(x):
        x = lax.all_to_all(x, "chan", split_axis=1, concat_axis=0, tiled=True)
        return lax.all_to_all(x, "facet", split_axis=2, concat_axis=0, tiled=True)

    observed, picked_ids, live_now = map(to_owner, (visibilities, strip_index, live_counts))
    slot_count = observed.shape[0]
    chan_local, uv_local = uv_kernels.shape[:2]
    slab_rows, facet_width = start_image.shape
    full_width = facet_width * lax.axis_size("facet")
    strip_count = slab_rows * full_width // STRIP
    blocks = slot_count * chan_local * lax.axis_size("chan") * uv_local * lax.axis_size("facet")
    step_size = strip_count / (2.5 * blocks)
    lane_ids = jnp.arange(2 * VISB, dtype=I32) % VISB
    live_mask = lane_ids < live_now[..., None]
    flat_ids = picked_ids.reshape(-1)
    estimate = start_image
    for iteration in range(ITERS):
        full_sky = lax.all_gather(estimate.astype(BF16), "facet", axis=1, tiled=True)
        sky_strips = full_sky.reshape(strip_count, STRIP)
        gathered = sky_strips[picked_ids].reshape(slot_count, chan_local, uv_local, TERMS * STRIP)
        predicted = jnp.einsum("scup,cupq->scuq", gathered, uv_kernels, preferred_element_type=F32)
        residual = jnp.where(live_mask, predicted - observed.astype(F32), 0.0).astype(BF16)
        adjoint = jnp.einsum("scuq,cupq->scup", residual, uv_kernels, preferred_element_type=F32)
        gradient = jnp.zeros((strip_count, STRIP), F32).at[flat_ids].add(adjoint.reshape(-1, STRIP))
        gradient = gradient.reshape(slab_rows, full_width)
        facet_part = lax.psum_scatter(gradient, "facet", scatter_dimension=1, tiled=True)
        facet_sum = lax.psum(facet_part, "chan")
        descent = estimate - step_size * facet_sum
        estimate = jnp.maximum(descent - shrinkage, 0.0)
    return estimate


def on_device(start_image, visibilities, strip_index, live_counts, uv_kernels):
    C, F = lax.axis_size("chan"), lax.axis_size("facet")
    L, uv_local = uv_kernels.shape[:2]
    strips = start_image.size * F // STRIP
    sparse = (
        visibilities.shape[0] == 1
        and uv_local == 1
        and C & (C - 1) == 0
        and F & (F - 1) == 0
        and C >= 4
        and ITERS == 2
        and F >= 2
        and F <= TILE and F * PART % STRIP == 0
        and C * F * L * TERMS == STRIP
        and 4 * L + TERMS + 1 <= BLOCK
        and 4 * L == TILE
        and L * C <= STRIP
        and strips <= 64 * 256
        and strips & (strips - 1) == 0
        and start_image.shape[0] % (C * TILE) == 0
        and start_image.shape[1] % STRIP == 0
        and start_image.size // STRIP // C % 16 == 0
    )
    run = sparse_device if sparse else dense_device
    return run(start_image, visibilities, strip_index, live_counts, uv_kernels)


def solution(mesh):
    placed = (
        P(None, "facet"),
        P(("chan", "facet"), None, None, None),
        P(("chan", "facet"), None, None, None),
        P(("chan", "facet"), None, None),
        P("chan", "facet", None, None),
    )
    return jax.shard_map(
        on_device, mesh=mesh, in_specs=placed, out_specs=P(None, "facet"), check_vma=False
    )
```

```python
import functools

import jax
import jax.numpy as jnp
from jax import lax
from jax.experimental import pallas as pl
from jax.experimental.pallas import tpu as pltpu
from jax.sharding import PartitionSpec as P

STRIP = 128
VISB = 128
TERMS = 2
ITERS = 2
TILE = 8
EXTRA = 16
BLOCK = 16
PART = 64
FINE = 32
FLOOR = 10
LEAST = 119

shrinkage = 0.05
F32, BF16, I32, I16 = jnp.float32, jnp.bfloat16, jnp.int32, jnp.int16
VMEM_LIMIT = 48 * 1024 * 1024


def call(kernel, outs, args, flops, placed=False, hbm=0, scratch=(), scalars=0):
    spaces = [pl.BlockSpec(memory_space=pltpu.HBM)] * hbm
    spaces += [pl.BlockSpec(memory_space=pltpu.VMEM)] * (len(args) - hbm)
    moved = sum(a.size * a.dtype.itemsize for a in list(args) + list(outs))
    args = list(args)
    for i in range(hbm):
        args[i] = pltpu.with_memory_space_constraint(args[i], pltpu.HBM)
    body = kernel
    if placed:

        def body(*refs):
            kernel((lax.axis_index("chan"), lax.axis_index("facet")), *refs)

    return pl.pallas_call(
        body,
        out_shape=list(outs),
        in_specs=spaces,
        out_specs=[pl.BlockSpec(memory_space=pltpu.VMEM)] * (len(outs) - scalars)
        + [pl.BlockSpec(memory_space=pltpu.SMEM)] * scalars,
        scratch_shapes=list(scratch),
        compiler_params=pltpu.CompilerParams(vmem_limit_bytes=VMEM_LIMIT),
        cost_estimate=pl.CostEstimate(flops=flops, bytes_accessed=moved, transcendentals=0),
    )(*args)


def split(x, parts):
    terms = []
    for _ in range(parts):
        term = x.astype(BF16)
        terms.append(term)
        x = x - term.astype(F32)
    return terms


def one_hot(hit):
    return jnp.where(hit, 1.0, 0.0).astype(BF16)


def iota(shape, dim):
    return lax.broadcasted_iota(I32, shape, dim)


def code_floats(x):
    size = jnp.abs(x)
    power = jnp.maximum(jnp.floor(jnp.log2(jnp.maximum(size, 1e-37))), -LEAST)
    code = (power + LEAST) * 128.0 + jnp.round(size * jnp.exp2(7.0 - power))
    return jnp.where(x < 0, -code, code).astype(I32)


def code_levels(x):
    near = x.astype(BF16).astype(F32)
    power = jnp.maximum(jnp.floor(jnp.log2(jnp.maximum(near, 1e-37))), -FLOOR)
    unit = jnp.exp2(power - 7.0)
    lead = jnp.round(near / unit)
    step = jnp.round(((x - lead * unit) / unit + 0.5) * (FINE - 1))
    step = jnp.clip(step, 0.0, FINE - 1)
    code = ((power + FLOOR) * 128.0 + lead) * FINE + step - 32768.0
    return code.astype(I32).astype(I16)


def levels_of(code):
    level = code >> log2(FINE)
    power = jnp.maximum((level >> 7) - 1, 0)
    unit = jnp.exp2((power - (FLOOR + 7)).astype(F32))
    near = ((level - power * 128).astype(F32) * unit).astype(BF16).astype(F32)
    step = (code & (FINE - 1)).astype(F32)
    return near, near + (step * (1.0 / (FINE - 1)) - 0.5) * unit


def floats_of(code):
    size = jnp.abs(code)
    power = jnp.maximum((size >> 7) - 1, 0)
    lead = (size - power * 128).astype(F32)
    value = lead * jnp.exp2((power - (LEAST + 7)).astype(F32))
    return jnp.where(code < 0, -value, value).astype(BF16)


def halves(x):
    return jnp.concatenate([(x >> 6).astype(F32), (x & 63).astype(F32)], axis=1).astype(BF16)


def joined(x):
    return x[:, :STRIP] * 64.0 + x[:, STRIP:]


def tiled_strips(rows):
    height, width = rows.shape
    return jnp.concatenate(
        [
            rows[r : r + TILE, c : c + STRIP]
            for r in range(0, height, TILE)
            for c in range(0, width, STRIP)
        ],
        axis=0,
    )


def log2(n):
    return n.bit_length() - 1


def pack_kernel(C, F, L, place, image, seen, terms, counts, *refs):
    outs, (band_in, seen_in, terms_in, counts_in, row_in, sems) = refs[:F], refs[F:]
    c, f = place[0], place[1]
    height, width = image.shape
    band = height // C
    wide = width // STRIP
    per_facet = height * wide
    piece = per_facet // C
    mine = image.at[pl.ds(pl.multiple_of(c * band, TILE), band), :]
    copies = [
        pltpu.make_async_copy(source, target, sems.at[i])
        for i, (source, target) in enumerate(
            ((mine, band_in), (seen, seen_in), (terms, terms_in), (counts, counts_in))
        )
    ]
    for copy in copies:
        copy.start()
    chips = C // 2
    size = chips * BLOCK
    rows = F * size
    row = iota((rows, 1), 0)
    k, j, i = row // size, (row // BLOCK) % chips, row % BLOCK
    channel = ((c >> 1) ^ j) * (2 * L) + (i >> 1)
    is_seen = i < 4 * L
    pick = is_seen & (iota((rows, L * C * F), 1) == channel * F + (k ^ f))
    row_in[...] = jnp.zeros(row_in.shape, I32)
    for copy in copies:
        copy.wait()
    strips = tiled_strips(band_in[...])
    share = code_levels(strips)
    raw = terms_in[...]
    across, column = raw >> log2(F * wide), raw & (F * wide - 1)
    terms_in[...] = (
        (column >> log2(wide)) * per_facet
        + (across >> 3) * (wide * TILE)
        + (column & (wide - 1)) * TILE
        + (across & 7)
    )
    for at in range(F):
        for term in range(TERMS):
            row_in[at * TILE + term : at * TILE + term + 1, : L * C] = terms_in[at ^ f, term : term + 1]
        row_in[at * TILE + TERMS : at * TILE + TERMS + 1, : L * C] = counts_in[pl.ds(at ^ f, 1)]
    by_channel = jnp.concatenate([seen_in[n] for n in range(L * C)], axis=0)
    both = jnp.dot(one_hot(pick), by_channel, preferred_element_type=F32)
    values = code_floats(jnp.where((i & 1) == 0, both[:, :VISB], both[:, VISB:]))
    whole = jnp.concatenate(
        [part for at in range(F) for part in [row_in[at * TILE : (at + 1) * TILE]] * (2 * chips)],
        axis=0,
    )
    blocks = jnp.where(is_seen, values, whole).astype(I16)
    for at in range(F):
        if at:
            outs[at][:piece] = share
            outs[at][piece:] = blocks[at * size : (at + 1) * size]
        else:
            outs[at][...] = blocks[:size]


def pass_kernel(F, piece, *refs):
    got, outs = refs[:F][::-1], refs[F:]
    for j, out in enumerate(outs):
        for k in range(1, F):
            out[(k - 1) * piece : k * piece] = got[k][:piece]
        for k in range(F):
            at = (F - 1) * piece + k * BLOCK
            first = (piece if k else 0) + j * BLOCK
            out[at : at + BLOCK] = got[k][first : first + BLOCK]


def table_of(levels):
    return jnp.concatenate(split(levels, 2), axis=1)


def shares_of(got, chips, size, used):
    return [got[q * size : q * size + used].astype(I32).astype(F32) + 32768.0 for q in range(chips)]


def sorted_blocks(C, F, L, c, got, first):
    chips, slots = C // 2, C * F
    size = got.shape[0] // chips
    blocks = jnp.concatenate(
        [got[(q + 1) * size - F * BLOCK : (q + 1) * size] for q in range(chips)], axis=0
    ).astype(I32)

    def pick(kinds, start):
        out = iota((kinds * slots, blocks.shape[0]), 0)
        source = (out % slots - first) * BLOCK + start + out // slots
        return one_hot(iota(out.shape, 1) == source)

    seen = jnp.dot(pick(4, 2 * L * (c & 1)), floats_of(blocks), preferred_element_type=F32)
    whole = jnp.dot(pick(3, 4 * L), halves(blocks), preferred_element_type=F32)
    return seen, whole


def ready_kernel(C, F, L, place, image, kernels, mine, table_out, seen_out, whole_out, turned_out):
    height, width = image.shape
    used = (F - 1) * (height * width // STRIP // C)
    shares = shares_of(mine, C // 2, used + F * BLOCK, used)
    own = tiled_strips(image)
    table_out[...] = table_of(jnp.concatenate([own] + shares, axis=0))
    seen_out[...], whole_out[...] = sorted_blocks(C, F, L, place[0], mine, 0)
    for ch in range(L):
        turned_out[ch] = kernels[ch].T


def first_kernel(
    C, F, L, place, known, seen_in, whole_in, kernels, turned, other, start_out, seen_out, refs_out, near_out, live_out, msg
):
    c, f = place[0], place[1]
    chips, slots = C // 2, C * F
    size = other.shape[0] // chips
    used = size - F * BLOCK
    per_facet = known.shape[0] - chips * used
    piece = per_facet // C
    seen, whole = sorted_blocks(C, F, L, c, other, slots // 2)
    seen = seen + seen_in[...]
    row, column = iota((2 * STRIP, 2 * L * STRIP), 0), iota((2 * STRIP, 2 * L * STRIP), 1)
    channel = (c ^ (column // (L * STRIP))) * L + column // STRIP % L
    lanes = jnp.where(row == channel, 64.0, jnp.where(row == channel + STRIP, 1.0, 0.0))
    whole = jnp.dot(
        (whole + whole_in[...]).astype(BF16), lanes.astype(BF16), preferred_element_type=F32
    )
    kinds = [
        whole[kind * slots : (kind + 1) * slots, ch * STRIP : (ch + 1) * STRIP]
        for ch in range(2 * L)
        for kind in range(TERMS + 1)
    ]
    both_refs = jnp.concatenate([x for i, x in enumerate(kinds) if i % (TERMS + 1) < TERMS], axis=0)
    refs = both_refs[: both_refs.shape[0] // 2]
    near_out[...] = jnp.concatenate(
        [
            both_refs[at : at + slots // 2]
            for first in range(both_refs.shape[0] // 2, both_refs.shape[0], slots)
            for at in (first + slots // 2, first)
        ],
        axis=0,
    )
    live = jnp.concatenate(kinds[TERMS : L * (TERMS + 1) : TERMS + 1], axis=0)
    col = refs.astype(I32)
    facet, local = col >> log2(per_facet), col & (per_facet - 1)
    k, d = facet ^ f, (local >> log2(piece)) ^ c
    block = (chips - (d >> 1)) & (chips - 1)
    turn = ((d & 1) * chips + block) * (F - 1) + k - 1
    place_of = jnp.where(k == 0, local, per_facet + turn * piece + (local & (piece - 1)))
    rest = table_of(jnp.concatenate(shares_of(other, chips, size, used), axis=0))

    def hits(count, start):
        wide = jnp.concatenate([place_of - start] * (count // STRIP), axis=1)
        return one_hot(iota(wide.shape, 1) == wide)

    both = jnp.dot(hits(known.shape[0], 0), known[...], preferred_element_type=F32) + jnp.dot(
        hits(rest.shape[0], known.shape[0]), rest, preferred_element_type=F32
    )
    total = both[:, :STRIP] + both[:, STRIP:]
    near, value = levels_of(jnp.where(k == 0, 0.0, total).astype(I32))
    sky = jnp.where(k == 0, both[:, :STRIP], near)
    start_out[...] = jnp.where(k == 0, total, value)
    seen_out[...] = seen.astype(BF16)
    refs_out[...] = refs
    live_out[...] = live
    encode(measure(sky, seen, live, kernels, turned), refs, msg)


def measure(est, seen, live, kernels, turned):
    L = kernels.shape[0]
    slots = live.shape[0] // L
    adjoints = []
    for ch in range(L):
        a, b, end = (ch * TERMS + i for i in range(3))
        sky = jnp.concatenate(
            [est[a * slots : b * slots], est[b * slots : end * slots]], axis=1
        ).astype(BF16)
        observed = jnp.concatenate(
            [seen[a * slots : b * slots], seen[b * slots : end * slots]], axis=1
        )
        predicted = jnp.dot(sky, kernels[ch], preferred_element_type=F32)
        alive = iota((slots, VISB), 1).astype(F32) < live[ch * slots : (ch + 1) * slots]
        residual = jnp.where(
            jnp.concatenate([alive, alive], axis=1), predicted - observed, 0.0
        ).astype(BF16)
        adjoint = jnp.dot(residual, turned[ch], preferred_element_type=F32)
        adjoints += [adjoint[:, :STRIP], adjoint[:, STRIP:]]
    return jnp.concatenate(adjoints, axis=0)


def as_row(col):
    eye = iota((STRIP, STRIP), 0) == iota((STRIP, STRIP), 1)
    return jnp.sum(jnp.where(eye, col, 0.0), axis=0, keepdims=True)


def scale_of(half):
    return jnp.exp2(half * 0.5).astype(BF16).astype(F32)


def put(msg, code, ids, half):
    msg[: code.shape[0]] = code.astype(I32).astype(I16)
    row = iota((EXTRA, STRIP), 0)
    extra = jnp.where(row == 0, ids, jnp.where(row == 1, half, 0.0))
    msg[code.shape[0] :] = extra.astype(I32).astype(I16)


def encode(adjoint, refs, msg):
    top = jnp.max(jnp.abs(adjoint), axis=1, keepdims=True)
    half = jnp.ceil(2.0 * jnp.log2(jnp.maximum(top, 1e-30) * (1.0 / 32500.0)))
    code = jnp.round(adjoint * (1.0 / scale_of(half)))
    row = as_row(half)
    put(msg, code, as_row(refs), row)
    return code, row


def sort_kernel(F, per_facet, place, refs, pick_out, numbers_out):
    f = place[1]
    ids = as_row(refs[...]).astype(I32)
    turn = iota((TILE, STRIP), 0)
    wanted = ((ids >> log2(per_facet)) == (turn ^ f)) & (turn < F)
    before = one_hot(iota((STRIP, STRIP), 0) < iota((STRIP, STRIP), 1))
    rank = jnp.dot(one_hot(wanted), before, preferred_element_type=F32)
    rank = jnp.where(wanted, rank, -1.0)
    slot = iota((PART, 1), 0).astype(F32)
    pick = jnp.concatenate([one_hot(rank[k : k + 1] == slot) for k in range(F)], axis=0)
    pick_out[...] = pick
    kinds = jnp.where(turn == 0, ids >> 6, jnp.where(turn == 1, ids & 63, 1))
    found = lax.dot_general(
        kinds.astype(F32).astype(BF16), pick, (((1,), (1,)), ((), ())), preferred_element_type=F32
    )
    found = jnp.where(found[2:3] > 0, found[0:1] * 64.0 + found[1:2], -1.0)
    for k in range(F):
        numbers_out[k * EXTRA : (k + 1) * EXTRA] = in_both_halves(found, k)


def in_both_halves(rows, k):
    at = k * PART // STRIP * STRIP
    pair = jnp.broadcast_to(rows[:, at : at + STRIP], (EXTRA, STRIP))
    low = iota((EXTRA, STRIP), 1) < PART
    return jnp.where(low == (k % 2 == 0), pair, pltpu.roll(pair, PART, 1))


def join_kernel(*refs):
    got, out = refs[:-1], refs[-1]
    F = len(got)
    rows = got[0].shape[0] - EXTRA
    number_rows = F * rows // STRIP
    row, lane = iota((EXTRA, STRIP), 0), iota((EXTRA, STRIP), 1)
    extra = jnp.zeros((EXTRA, STRIP), I32)
    for k in range(F):
        out[k * rows : (k + 1) * rows] = got[k][:rows]
        here = got[k][rows:].astype(I32)
        first, at = k * rows % STRIP, k * rows // STRIP
        own = (lane >= first) & (lane < first + rows)
        extra = jnp.where(own & (row == at), here[0:1], extra)
        extra = jnp.where(own & (row == number_rows + at), here[1:2], extra)
    out[F * rows :] = extra.astype(I16)


def decode(F, block, chips):
    ids, scales, values = [], [], []
    size = block.shape[0] // chips
    rows = size - EXTRA
    number_rows = rows // STRIP
    for at in range(0, block.shape[0], size):
        extra = block[at + rows : at + size].astype(I32)
        ids += [extra[j : j + 1] for j in range(number_rows)]
        scales += [extra[j : j + 1] for j in range(number_rows, 2 * number_rows)]
        values.append(table_of(block[at : at + rows].astype(I32).astype(F32)))
    scale = scale_of(jnp.concatenate(scales, axis=1).astype(F32))
    return ids, scale, jnp.concatenate(values, axis=0)


def summed(decoded, strips):
    ids, scale, values = decoded
    wide = strips if len(ids) * STRIP == strips.shape[1] else jnp.concatenate([strips] * len(ids), axis=1)
    hit = jnp.concatenate(ids, axis=1) == wide
    both = jnp.dot(jnp.where(hit, scale, 0.0).astype(BF16), values, preferred_element_type=F32)
    return both[:, :STRIP] + both[:, STRIP:]


def crowd_of(ids, F, per_facet):
    facets = jnp.concatenate(ids, axis=0) >> log2(per_facet)
    hits = jnp.concatenate([one_hot(facets == f) for f in range(F)], axis=0)
    ones = jnp.ones((STRIP, STRIP), BF16)
    counts = jnp.dot(hits, ones, preferred_element_type=F32)
    return jnp.max(counts, axis=0, keepdims=True)


def part_kernel(F, chips, refs, other_refs, block, out, other_out):
    strips = jnp.concatenate([refs[...], other_refs[...]], axis=0).astype(I32)
    total = summed(decode(F, block, chips), strips)
    out[...] = total[: refs.shape[0]]
    other_out[...] = total[refs.shape[0] :]


def next_kernel(
    step, refs, live, seen, kernels, turned, est_in, part, rest, pick, numbers, msg, *msgs
):
    gradient = part[...] + rest[...]
    est = jnp.maximum(est_in[...] - step * gradient - shrinkage, 0.0)
    adjoint = measure(est, seen[...].astype(F32), live[...], kernels, turned)
    code, half = encode(adjoint, refs[...], msg)
    both = jnp.dot(pick[...], table_of(code), preferred_element_type=F32)
    rows = both[:, :STRIP] + both[:, STRIP:]
    halves_of = lax.dot_general(
        jnp.broadcast_to(half, (TILE, STRIP)).astype(BF16),
        pick[...],
        (((1,), (1,)), ((), ())),
        preferred_element_type=F32,
    )[0:1]
    for k, short in enumerate(msgs):
        put(
            short,
            rows[k * PART : (k + 1) * PART],
            numbers[k * EXTRA : (k + 1) * EXTRA],
            in_both_halves(halves_of, k),
        )


def facet_part_kernel(F, chips, place, block, out, *crowd):
    decoded = decode(F, block, chips)
    count = out.shape[0]
    out[...] = summed(decoded, iota((count, STRIP), 0) + place[1] * count)
    for most in crowd:
        most[...] = jnp.broadcast_to(crowd_of(decoded[0], F, count), most.shape)


def settle_kernel(F, chips, step, place, image, part, block, *refs):
    decoded = decode(F, block, chips)
    height, width = image.shape
    count = part.shape[0]
    if len(refs) == 3:
        crowd, out, most = refs
        most[0] = jnp.max(jnp.maximum(crowd[0:1], crowd_of(decoded[0], F, count))).astype(I32)
    else:
        (out,) = refs
    per_band = width // STRIP * TILE
    chunk = min(256, count)
    for at in range(0, count, chunk):
        strips = iota((chunk, STRIP), 0) + (place[1] * count + at)
        gradient = part[at : at + chunk] + summed(decoded, strips)
        for t in range(0, chunk, TILE):
            r = (at + t) // per_band * TILE
            c = (at + t) % per_band // TILE * STRIP
            old = image[r : r + TILE, c : c + STRIP]
            out[r : r + TILE, c : c + STRIP] = jnp.maximum(
                old - step * gradient[t : t + TILE] - shrinkage, 0.0
            )


def swap(x, along_chan, along_facet=0):
    C, F = lax.axis_size("chan"), lax.axis_size("facet")
    pairs = [
        (c * F + f, (c ^ along_chan) * F + (f ^ along_facet)) for c in range(C) for f in range(F)
    ]
    return lax.ppermute(x, ("chan", "facet"), pairs)


def sparse_device(start_image, visibilities, strip_index, live_counts, uv_kernels):
    C, F = lax.axis_size("chan"), lax.axis_size("facet")
    L = uv_kernels.shape[0]
    refs = C * F * L * TERMS
    per_facet = start_image.size // STRIP
    piece = per_facet // C
    chips = C // 2
    step = float(per_facet * F / (2.5 * C * F * (L * C) * F))
    kernels = uv_kernels[:, 0]

    blocks = jax.ShapeDtypeStruct((chips * BLOCK, STRIP), I16)
    both = jax.ShapeDtypeStruct((piece + chips * BLOCK, STRIP), I16)
    packed = call(
        functools.partial(pack_kernel, C, F, L),
        [blocks] + [both] * (F - 1),
        [
            start_image,
            visibilities[0],
            strip_index[0].transpose(1, 2, 0),
            live_counts[0].T,
        ],
        10**8,
        placed=True,
        hbm=4,
        scratch=[
            pltpu.VMEM((start_image.shape[0] // C, start_image.shape[1]), F32),
            pltpu.VMEM(visibilities.shape[1:], BF16),
            pltpu.VMEM((F, TERMS, L * C), I32),
            pltpu.VMEM((F, L * C), I32),
            pltpu.VMEM((F * TILE, STRIP), I32),
            pltpu.SemaphoreType.DMA((4,)),
        ],
    )
    got = [packed[0]] + [swap(packed[k], 0, k) for k in range(F - 1, 0, -1)][::-1]
    passed = call(
        functools.partial(pass_kernel, F, piece),
        [jax.ShapeDtypeStruct(((F - 1) * piece + F * BLOCK, STRIP), I16)] * chips,
        got[::-1],
        10**6,
    )
    mine = jnp.concatenate(
        [passed[0]] + [swap(passed[j], 2 * j) for j in range(chips - 1, 0, -1)], axis=0
    )
    other = swap(mine, 1)

    at_refs = jax.ShapeDtypeStruct((refs, STRIP), F32)
    message = jax.ShapeDtypeStruct((refs + EXTRA, STRIP), I16)
    short = jax.ShapeDtypeStruct((PART + EXTRA, STRIP), I16)
    facet_strips = jax.ShapeDtypeStruct((per_facet, STRIP), F32)
    known, seen_part, whole_part, turned = call(
        functools.partial(ready_kernel, C, F, L),
        [
            jax.ShapeDtypeStruct((per_facet + chips * (F - 1) * piece, 2 * STRIP), BF16),
            at_refs,
            jax.ShapeDtypeStruct(((TERMS + 1) * C * F, 2 * STRIP), F32),
            jax.ShapeDtypeStruct(kernels.shape, BF16),
        ],
        [start_image, kernels, mine],
        10**8,
        placed=True,
    )
    est, observed, at, other_at, live, msg = call(
        functools.partial(first_kernel, C, F, L),
        [
            at_refs,
            jax.ShapeDtypeStruct((refs, STRIP), BF16),
            at_refs,
            at_refs,
            jax.ShapeDtypeStruct((L * C * F, STRIP), F32),
            message,
        ],
        [known, seen_part, whole_part, kernels, turned, other],
        5 * 10**8,
        placed=True,
    )

    def along_facet(msgs, cross=0):
        got = [msgs[0]] + [swap(msgs[k], cross, k) for k in range(F - 1, 0, -1)][::-1]
        rows = got[0].shape[0] - EXTRA
        return call(
            join_kernel, [jax.ShapeDtypeStruct((F * rows + EXTRA, STRIP), I16)], got, 10**6
        )[0]

    def around_chan(near, cross=0):
        around = [swap(near, 2 * j + cross) for j in range(chips - 1, 0, -1)]
        return jnp.concatenate([near] + around, axis=0)

    def along_chan(near):
        mine = around_chan(near)
        return mine, swap(mine, 1)

    def facet_part(mine, *crowd):
        return call(
            functools.partial(facet_part_kernel, F, chips),
            [facet_strips, *crowd],
            [mine],
            2 * 10**9,
            placed=True,
        )

    settle = functools.partial(settle_kernel, F, chips, step)
    whole = jax.ShapeDtypeStruct(start_image.shape, F32)

    near = along_facet([msg] * F)
    pick, numbers = call(
        functools.partial(sort_kernel, F, per_facet),
        [
            jax.ShapeDtypeStruct((F * PART, refs), BF16),
            jax.ShapeDtypeStruct((F * EXTRA, STRIP), F32),
        ],
        [at],
        10**8,
        placed=True,
    )
    near, pick, numbers = lax.optimization_barrier((near, pick, numbers))
    mine = around_chan(near)
    part, other_part = call(
        functools.partial(part_kernel, F, chips),
        [at_refs, at_refs],
        [at, other_at, mine],
        3 * 10**8,
    )
    msg, *msgs = call(
        functools.partial(next_kernel, step),
        [message] + [short] * F,
        [at, live, observed, kernels, turned, est, part, swap(other_part, 1), pick, numbers],
        3 * 10**8,
    )
    msg, mine, *msgs = lax.optimization_barrier((msg, mine, *msgs))
    near = along_facet(msgs, 1)
    other = swap(mine, 1)
    part, crowd = facet_part(mine, jax.ShapeDtypeStruct((TILE, STRIP), F32))
    near, part, crowd, other = lax.optimization_barrier((near, part, crowd, other))
    around = around_chan(near, 1)
    image, crowd = call(
        settle,
        [whole, jax.ShapeDtypeStruct((1,), I32)],
        [start_image, part, other, crowd],
        2 * 10**9,
        placed=True,
        scalars=1,
    )
    crowded = crowd[0] > PART
    around, image, crowded = lax.optimization_barrier((around, image, crowded))

    other = swap(around, 1)
    (part,) = facet_part(around)

    def in_full():
        mine, other = along_chan(along_facet([msg] * F))
        (part,) = facet_part(mine)
        (rest,) = facet_part(other)
        return part + rest, jnp.zeros((chips * (F * PART + EXTRA), STRIP), I16)

    part, other = lax.cond(crowded, in_full, lambda: (part, other))
    return call(
        settle,
        [whole],
        [image, part, other],
        2 * 10**9,
        placed=True,
    )[0]


def dense_device(start_image, visibilities, strip_index, live_counts, uv_kernels):
    def to_owner(x):
        x = lax.all_to_all(x, "chan", split_axis=1, concat_axis=0, tiled=True)
        return lax.all_to_all(x, "facet", split_axis=2, concat_axis=0, tiled=True)

    observed, picked_ids, live_now = map(to_owner, (visibilities, strip_index, live_counts))
    slot_count = observed.shape[0]
    chan_local, uv_local = uv_kernels.shape[:2]
    slab_rows, facet_width = start_image.shape
    full_width = facet_width * lax.axis_size("facet")
    strip_count = slab_rows * full_width // STRIP
    blocks = slot_count * chan_local * lax.axis_size("chan") * uv_local * lax.axis_size("facet")
    step_size = strip_count / (2.5 * blocks)
    lane_ids = jnp.arange(2 * VISB, dtype=I32) % VISB
    live_mask = lane_ids < live_now[..., None]
    flat_ids = picked_ids.reshape(-1)
    estimate = start_image
    for iteration in range(ITERS):
        full_sky = lax.all_gather(estimate.astype(BF16), "facet", axis=1, tiled=True)
        sky_strips = full_sky.reshape(strip_count, STRIP)
        gathered = sky_strips[picked_ids].reshape(slot_count, chan_local, uv_local, TERMS * STRIP)
        predicted = jnp.einsum("scup,cupq->scuq", gathered, uv_kernels, preferred_element_type=F32)
        residual = jnp.where(live_mask, predicted - observed.astype(F32), 0.0).astype(BF16)
        adjoint = jnp.einsum("scuq,cupq->scup", residual, uv_kernels, preferred_element_type=F32)
        gradient = jnp.zeros((strip_count, STRIP), F32).at[flat_ids].add(adjoint.reshape(-1, STRIP))
        gradient = gradient.reshape(slab_rows, full_width)
        facet_part = lax.psum_scatter(gradient, "facet", scatter_dimension=1, tiled=True)
        facet_sum = lax.psum(facet_part, "chan")
        descent = estimate - step_size * facet_sum
        estimate = jnp.maximum(descent - shrinkage, 0.0)
    return estimate


def on_device(start_image, visibilities, strip_index, live_counts, uv_kernels):
    C, F = lax.axis_size("chan"), lax.axis_size("facet")
    L, uv_local = uv_kernels.shape[:2]
    strips = start_image.size * F // STRIP
    sparse = (
        visibilities.shape[0] == 1
        and uv_local == 1
        and C & (C - 1) == 0
        and F & (F - 1) == 0
        and C >= 4
        and ITERS == 2
        and F >= 2
        and F <= TILE and F * PART % STRIP == 0
        and C * F * L * TERMS == STRIP
        and 4 * L + TERMS + 1 <= BLOCK
        and 4 * L == TILE
        and L * C <= STRIP
        and strips <= 64 * 256
        and strips & (strips - 1) == 0
        and start_image.shape[0] % (C * TILE) == 0
        and start_image.shape[1] % STRIP == 0
        and start_image.size // STRIP // C % 16 == 0
    )
    run = sparse_device if sparse else dense_device
    return run(start_image, visibilities, strip_index, live_counts, uv_kernels)


def solution(mesh):
    placed = (
        P(None, "facet"),
        P(("chan", "facet"), None, None, None),
        P(("chan", "facet"), None, None, None),
        P(("chan", "facet"), None, None),
        P("chan", "facet", None, None),
    )
    return jax.shard_map(
        on_device, mesh=mesh, in_specs=placed, out_specs=P(None, "facet"), check_vma=False
    )
```

```python
import functools

import jax
import jax.numpy as jnp
from jax import lax
from jax.experimental import pallas as pl
from jax.experimental.pallas import tpu as pltpu
from jax.sharding import PartitionSpec as P

STRIP = 128
VISB = 128
TERMS = 2
ITERS = 2
TILE = 8
EXTRA = 16
BLOCK = 16
PART = 64
FINE = 32
FLOOR = 10
LEAST = 119

shrinkage = 0.05
F32, BF16, I32, I16 = jnp.float32, jnp.bfloat16, jnp.int32, jnp.int16
VMEM_LIMIT = 48 * 1024 * 1024


def call(kernel, outs, args, flops, placed=False, hbm=0, scratch=(), scalars=0):
    spaces = [pl.BlockSpec(memory_space=pltpu.HBM)] * hbm
    spaces += [pl.BlockSpec(memory_space=pltpu.VMEM)] * (len(args) - hbm)
    moved = sum(a.size * a.dtype.itemsize for a in list(args) + list(outs))
    args = list(args)
    for i in range(hbm):
        args[i] = pltpu.with_memory_space_constraint(args[i], pltpu.HBM)
    body = kernel
    if placed:

        def body(*refs):
            kernel((lax.axis_index("chan"), lax.axis_index("facet")), *refs)

    return pl.pallas_call(
        body,
        out_shape=list(outs),
        in_specs=spaces,
        out_specs=[pl.BlockSpec(memory_space=pltpu.VMEM)] * (len(outs) - scalars)
        + [pl.BlockSpec(memory_space=pltpu.SMEM)] * scalars,
        scratch_shapes=list(scratch),
        compiler_params=pltpu.CompilerParams(vmem_limit_bytes=VMEM_LIMIT),
        cost_estimate=pl.CostEstimate(flops=flops, bytes_accessed=moved, transcendentals=0),
    )(*args)


def split(x, parts):
    terms = []
    for _ in range(parts):
        term = x.astype(BF16)
        terms.append(term)
        x = x - term.astype(F32)
    return terms


def one_hot(hit):
    return jnp.where(hit, 1.0, 0.0).astype(BF16)


def iota(shape, dim):
    return lax.broadcasted_iota(I32, shape, dim)


def code_floats(x):
    size = jnp.abs(x)
    power = jnp.maximum(jnp.floor(jnp.log2(jnp.maximum(size, 1e-37))), -LEAST)
    code = (power + LEAST) * 128.0 + jnp.round(size * jnp.exp2(7.0 - power))
    return jnp.where(x < 0, -code, code).astype(I32)


def code_levels(x):
    near = x.astype(BF16).astype(F32)
    power = jnp.maximum(jnp.floor(jnp.log2(jnp.maximum(near, 1e-37))), -FLOOR)
    unit = jnp.exp2(power - 7.0)
    lead = jnp.round(near / unit)
    step = jnp.round(((x - lead * unit) / unit + 0.5) * (FINE - 1))
    step = jnp.clip(step, 0.0, FINE - 1)
    code = ((power + FLOOR) * 128.0 + lead) * FINE + step - 32768.0
    return code.astype(I32).astype(I16)


def levels_of(code):
    level = code >> log2(FINE)
    power = jnp.maximum((level >> 7) - 1, 0)
    unit = jnp.exp2((power - (FLOOR + 7)).astype(F32))
    near = ((level - power * 128).astype(F32) * unit).astype(BF16).astype(F32)
    step = (code & (FINE - 1)).astype(F32)
    return near, near + (step * (1.0 / (FINE - 1)) - 0.5) * unit


def floats_of(code):
    size = jnp.abs(code)
    power = jnp.maximum((size >> 7) - 1, 0)
    lead = (size - power * 128).astype(F32)
    value = lead * jnp.exp2((power - (LEAST + 7)).astype(F32))
    return jnp.where(code < 0, -value, value).astype(BF16)


def halves(x):
    return jnp.concatenate([(x >> 6).astype(F32), (x & 63).astype(F32)], axis=1).astype(BF16)


def joined(x):
    return x[:, :STRIP] * 64.0 + x[:, STRIP:]


def tiled_strips(rows):
    height, width = rows.shape
    return jnp.concatenate(
        [
            rows[r : r + TILE, c : c + STRIP]
            for r in range(0, height, TILE)
            for c in range(0, width, STRIP)
        ],
        axis=0,
    )


def log2(n):
    return n.bit_length() - 1


def pack_kernel(C, F, L, place, image, seen, terms, counts, *refs):
    outs, (band_in, seen_in, terms_in, counts_in, row_in, sems) = refs[:F], refs[F:]
    c, f = place[0], place[1]
    height, width = image.shape
    band = height // C
    wide = width // STRIP
    per_facet = height * wide
    piece = per_facet // C
    mine = image.at[pl.ds(pl.multiple_of(c * band, TILE), band), :]
    copies = [
        pltpu.make_async_copy(source, target, sems.at[i])
        for i, (source, target) in enumerate(
            ((mine, band_in), (seen, seen_in), (terms, terms_in), (counts, counts_in))
        )
    ]
    for copy in copies:
        copy.start()
    chips = C // 2
    size = chips * BLOCK
    rows = F * size
    row = iota((rows, 1), 0)
    k, j, i = row // size, (row // BLOCK) % chips, row % BLOCK
    channel = ((c >> 1) ^ j) * (2 * L) + (i >> 1)
    is_seen = i < 4 * L
    pick = is_seen & (iota((rows, L * C * F), 1) == channel * F + (k ^ f))
    row_in[...] = jnp.zeros(row_in.shape, I32)
    for copy in copies:
        copy.wait()
    strips = tiled_strips(band_in[...])
    share = code_levels(strips)
    raw = terms_in[...]
    across, column = raw >> log2(F * wide), raw & (F * wide - 1)
    terms_in[...] = (
        (column >> log2(wide)) * per_facet
        + (across >> 3) * (wide * TILE)
        + (column & (wide - 1)) * TILE
        + (across & 7)
    )
    for at in range(F):
        for term in range(TERMS):
            row_in[at * TILE + term : at * TILE + term + 1, : L * C] = terms_in[at ^ f, term : term + 1]
        row_in[at * TILE + TERMS : at * TILE + TERMS + 1, : L * C] = counts_in[pl.ds(at ^ f, 1)]
    by_channel = jnp.concatenate([seen_in[n] for n in range(L * C)], axis=0)
    both = jnp.dot(one_hot(pick), by_channel, preferred_element_type=F32)
    values = code_floats(jnp.where((i & 1) == 0, both[:, :VISB], both[:, VISB:]))
    whole = jnp.concatenate(
        [part for at in range(F) for part in [row_in[at * TILE : (at + 1) * TILE]] * (2 * chips)],
        axis=0,
    )
    blocks = jnp.where(is_seen, values, whole).astype(I16)
    for at in range(F):
        if at:
            outs[at][:piece] = share
            outs[at][piece:] = blocks[at * size : (at + 1) * size]
        else:
            outs[at][...] = blocks[:size]


def pass_kernel(F, piece, *refs):
    got, outs = refs[:F][::-1], refs[F:]
    for j, out in enumerate(outs):
        for k in range(1, F):
            out[(k - 1) * piece : k * piece] = got[k][:piece]
        for k in range(F):
            at = (F - 1) * piece + k * BLOCK
            first = (piece if k else 0) + j * BLOCK
            out[at : at + BLOCK] = got[k][first : first + BLOCK]


def table_of(levels):
    return jnp.concatenate(split(levels, 2), axis=1)


def shares_of(got, chips, size, used):
    return [got[q * size : q * size + used].astype(I32).astype(F32) + 32768.0 for q in range(chips)]


def sorted_blocks(C, F, L, c, got, first):
    chips, slots = C // 2, C * F
    size = got.shape[0] // chips
    blocks = jnp.concatenate(
        [got[(q + 1) * size - F * BLOCK : (q + 1) * size] for q in range(chips)], axis=0
    ).astype(I32)

    def pick(kinds, start):
        out = iota((kinds * slots, blocks.shape[0]), 0)
        source = (out % slots - first) * BLOCK + start + out // slots
        return one_hot(iota(out.shape, 1) == source)

    seen = jnp.dot(pick(4, 2 * L * (c & 1)), floats_of(blocks), preferred_element_type=F32)
    whole = jnp.dot(pick(3, 4 * L), halves(blocks), preferred_element_type=F32)
    return seen, whole


def ready_kernel(C, F, L, place, image, kernels, mine, table_out, seen_out, whole_out, turned_out):
    height, width = image.shape
    used = (F - 1) * (height * width // STRIP // C)
    shares = shares_of(mine, C // 2, used + F * BLOCK, used)
    own = tiled_strips(image)
    table_out[...] = table_of(jnp.concatenate([own] + shares, axis=0))
    seen_out[...], whole_out[...] = sorted_blocks(C, F, L, place[0], mine, 0)
    for ch in range(L):
        turned_out[ch] = kernels[ch].T


def first_kernel(
    C, F, L, place, known, seen_in, whole_in, kernels, turned, other, start_out, seen_out, refs_out, near_out, live_out, msg
):
    c, f = place[0], place[1]
    chips, slots = C // 2, C * F
    size = other.shape[0] // chips
    used = size - F * BLOCK
    per_facet = known.shape[0] - chips * used
    piece = per_facet // C
    seen, whole = sorted_blocks(C, F, L, c, other, slots // 2)
    seen = seen + seen_in[...]
    row, column = iota((2 * STRIP, 2 * L * STRIP), 0), iota((2 * STRIP, 2 * L * STRIP), 1)
    channel = (c ^ (column // (L * STRIP))) * L + column // STRIP % L
    lanes = jnp.where(row == channel, 64.0, jnp.where(row == channel + STRIP, 1.0, 0.0))
    whole = jnp.dot(
        (whole + whole_in[...]).astype(BF16), lanes.astype(BF16), preferred_element_type=F32
    )
    kinds = [
        whole[kind * slots : (kind + 1) * slots, ch * STRIP : (ch + 1) * STRIP]
        for ch in range(2 * L)
        for kind in range(TERMS + 1)
    ]
    both_refs = jnp.concatenate([x for i, x in enumerate(kinds) if i % (TERMS + 1) < TERMS], axis=0)
    refs = both_refs[: both_refs.shape[0] // 2]
    near_out[...] = jnp.concatenate(
        [
            both_refs[at : at + slots // 2]
            for first in range(both_refs.shape[0] // 2, both_refs.shape[0], slots)
            for at in (first + slots // 2, first)
        ],
        axis=0,
    )
    live = jnp.concatenate(kinds[TERMS : L * (TERMS + 1) : TERMS + 1], axis=0)
    col = refs.astype(I32)
    facet, local = col >> log2(per_facet), col & (per_facet - 1)
    k, d = facet ^ f, (local >> log2(piece)) ^ c
    block = (chips - (d >> 1)) & (chips - 1)
    turn = ((d & 1) * chips + block) * (F - 1) + k - 1
    place_of = jnp.where(k == 0, local, per_facet + turn * piece + (local & (piece - 1)))
    rest = table_of(jnp.concatenate(shares_of(other, chips, size, used), axis=0))

    def hits(count, start):
        wide = jnp.concatenate([place_of - start] * (count // STRIP), axis=1)
        return one_hot(iota(wide.shape, 1) == wide)

    both = jnp.dot(hits(known.shape[0], 0), known[...], preferred_element_type=F32) + jnp.dot(
        hits(rest.shape[0], known.shape[0]), rest, preferred_element_type=F32
    )
    total = both[:, :STRIP] + both[:, STRIP:]
    near, value = levels_of(jnp.where(k == 0, 0.0, total).astype(I32))
    sky = jnp.where(k == 0, both[:, :STRIP], near)
    start_out[...] = jnp.where(k == 0, total, value)
    seen_out[...] = seen.astype(BF16)
    refs_out[...] = refs
    live_out[...] = live
    encode(measure(sky, seen, live, kernels, turned), refs, msg)


def measure(est, seen, live, kernels, turned):
    L = kernels.shape[0]
    slots = live.shape[0] // L
    adjoints = []
    for ch in range(L):
        a, b, end = (ch * TERMS + i for i in range(3))
        sky = jnp.concatenate(
            [est[a * slots : b * slots], est[b * slots : end * slots]], axis=1
        ).astype(BF16)
        observed = jnp.concatenate(
            [seen[a * slots : b * slots], seen[b * slots : end * slots]], axis=1
        )
        predicted = jnp.dot(sky, kernels[ch], preferred_element_type=F32)
        alive = iota((slots, VISB), 1).astype(F32) < live[ch * slots : (ch + 1) * slots]
        residual = jnp.where(
            jnp.concatenate([alive, alive], axis=1), predicted - observed, 0.0
        ).astype(BF16)
        adjoint = jnp.dot(residual, turned[ch], preferred_element_type=F32)
        adjoints += [adjoint[:, :STRIP], adjoint[:, STRIP:]]
    return jnp.concatenate(adjoints, axis=0)


def as_row(col):
    eye = iota((STRIP, STRIP), 0) == iota((STRIP, STRIP), 1)
    return jnp.sum(jnp.where(eye, col, 0.0), axis=0, keepdims=True)


def scale_of(half):
    return jnp.exp2(half * 0.5).astype(BF16).astype(F32)


def put(msg, code, ids, half):
    msg[: code.shape[0]] = code.astype(I32).astype(I16)
    row = iota((EXTRA, STRIP), 0)
    extra = jnp.where(row == 0, ids, jnp.where(row == 1, half, 0.0))
    msg[code.shape[0] :] = extra.astype(I32).astype(I16)


def encode(adjoint, refs, msg):
    top = jnp.max(jnp.abs(adjoint), axis=1, keepdims=True)
    half = jnp.ceil(2.0 * jnp.log2(jnp.maximum(top, 1e-30) * (1.0 / 32500.0)))
    code = jnp.round(adjoint * (1.0 / scale_of(half)))
    row = as_row(half)
    put(msg, code, as_row(refs), row)
    return code, row


def sort_kernel(F, per_facet, place, refs, pick_out, numbers_out):
    f = place[1]
    ids = as_row(refs[...]).astype(I32)
    turn = iota((TILE, STRIP), 0)
    wanted = ((ids >> log2(per_facet)) == (turn ^ f)) & (turn < F)
    before = one_hot(iota((STRIP, STRIP), 0) < iota((STRIP, STRIP), 1))
    rank = jnp.dot(one_hot(wanted), before, preferred_element_type=F32)
    rank = jnp.where(wanted, rank, -1.0)
    slot = iota((PART, 1), 0).astype(F32)
    pick = jnp.concatenate([one_hot(rank[k : k + 1] == slot) for k in range(F)], axis=0)
    pick_out[...] = pick
    kinds = jnp.where(turn == 0, ids >> 6, jnp.where(turn == 1, ids & 63, 1))
    found = lax.dot_general(
        kinds.astype(F32).astype(BF16), pick, (((1,), (1,)), ((), ())), preferred_element_type=F32
    )
    found = jnp.where(found[2:3] > 0, found[0:1] * 64.0 + found[1:2], -1.0)
    for k in range(F):
        numbers_out[k * EXTRA : (k + 1) * EXTRA] = in_both_halves(found, k)


def in_both_halves(rows, k):
    at = k * PART // STRIP * STRIP
    pair = jnp.broadcast_to(rows[:, at : at + STRIP], (EXTRA, STRIP))
    low = iota((EXTRA, STRIP), 1) < PART
    return jnp.where(low == (k % 2 == 0), pair, pltpu.roll(pair, PART, 1))


def join_kernel(*refs):
    got, out = refs[:-1], refs[-1]
    F = len(got)
    rows = got[0].shape[0] - EXTRA
    number_rows = F * rows // STRIP
    row, lane = iota((EXTRA, STRIP), 0), iota((EXTRA, STRIP), 1)
    extra = jnp.zeros((EXTRA, STRIP), I32)
    for k in range(F):
        out[k * rows : (k + 1) * rows] = got[k][:rows]
        here = got[k][rows:].astype(I32)
        first, at = k * rows % STRIP, k * rows // STRIP
        own = (lane >= first) & (lane < first + rows)
        extra = jnp.where(own & (row == at), here[0:1], extra)
        extra = jnp.where(own & (row == number_rows + at), here[1:2], extra)
    out[F * rows :] = extra.astype(I16)


def decode(F, block, chips):
    ids, scales, values = [], [], []
    size = block.shape[0] // chips
    rows = size - EXTRA
    number_rows = rows // STRIP
    for at in range(0, block.shape[0], size):
        extra = block[at + rows : at + size].astype(I32)
        ids += [extra[j : j + 1] for j in range(number_rows)]
        scales += [extra[j : j + 1] for j in range(number_rows, 2 * number_rows)]
        values.append(table_of(block[at : at + rows].astype(I32).astype(F32)))
    scale = scale_of(jnp.concatenate(scales, axis=1).astype(F32))
    return ids, scale, jnp.concatenate(values, axis=0)


def summed(decoded, strips):
    ids, scale, values = decoded
    wide = strips if len(ids) * STRIP == strips.shape[1] else jnp.concatenate([strips] * len(ids), axis=1)
    hit = jnp.concatenate(ids, axis=1) == wide
    both = jnp.dot(jnp.where(hit, scale, 0.0).astype(BF16), values, preferred_element_type=F32)
    return both[:, :STRIP] + both[:, STRIP:]


def crowd_of(ids, F, per_facet):
    facets = jnp.concatenate(ids, axis=0) >> log2(per_facet)
    hits = jnp.concatenate([one_hot(facets == f) for f in range(F)], axis=0)
    ones = jnp.ones((STRIP, STRIP), BF16)
    counts = jnp.dot(hits, ones, preferred_element_type=F32)
    return jnp.max(counts, axis=0, keepdims=True)


def part_kernel(F, chips, refs, other_refs, block, out, other_out):
    strips = jnp.concatenate([refs[...], other_refs[...]], axis=0).astype(I32)
    total = summed(decode(F, block, chips), strips)
    out[...] = total[: refs.shape[0]]
    other_out[...] = total[refs.shape[0] :]


def next_kernel(
    step, refs, live, seen, kernels, turned, est_in, part, rest, pick, numbers, msg, *msgs
):
    gradient = part[...] + rest[...]
    est = jnp.maximum(est_in[...] - step * gradient - shrinkage, 0.0)
    adjoint = measure(est, seen[...].astype(F32), live[...], kernels, turned)
    code, half = encode(adjoint, refs[...], msg)
    both = jnp.dot(pick[...], table_of(code), preferred_element_type=F32)
    rows = both[:, :STRIP] + both[:, STRIP:]
    halves_of = lax.dot_general(
        jnp.broadcast_to(half, (TILE, STRIP)).astype(BF16),
        pick[...],
        (((1,), (1,)), ((), ())),
        preferred_element_type=F32,
    )[0:1]
    for k, short in enumerate(msgs):
        put(
            short,
            rows[k * PART : (k + 1) * PART],
            numbers[k * EXTRA : (k + 1) * EXTRA],
            in_both_halves(halves_of, k),
        )


def facet_part_kernel(F, chips, place, block, out, *crowd):
    decoded = decode(F, block, chips)
    count = out.shape[0]
    out[...] = summed(decoded, iota((count, STRIP), 0) + place[1] * count)
    for most in crowd:
        most[...] = jnp.broadcast_to(crowd_of(decoded[0], F, count), most.shape)


def settle_kernel(F, chips, step, place, image, part, block, *refs):
    decoded = decode(F, block, chips)
    height, width = image.shape
    count = part.shape[0]
    if len(refs) == 3:
        crowd, out, most = refs
        most[0] = jnp.max(jnp.maximum(crowd[0:1], crowd_of(decoded[0], F, count))).astype(I32)
    else:
        (out,) = refs
    per_band = width // STRIP * TILE
    chunk = min(1024, count)
    for at in range(0, count, chunk):
        strips = iota((chunk, STRIP), 0) + (place[1] * count + at)
        gradient = part[at : at + chunk] + summed(decoded, strips)
        for t in range(0, chunk, TILE):
            r = (at + t) // per_band * TILE
            c = (at + t) % per_band // TILE * STRIP
            old = image[r : r + TILE, c : c + STRIP]
            out[r : r + TILE, c : c + STRIP] = jnp.maximum(
                old - step * gradient[t : t + TILE] - shrinkage, 0.0
            )


def swap(x, along_chan, along_facet=0):
    C, F = lax.axis_size("chan"), lax.axis_size("facet")
    pairs = [
        (c * F + f, (c ^ along_chan) * F + (f ^ along_facet)) for c in range(C) for f in range(F)
    ]
    return lax.ppermute(x, ("chan", "facet"), pairs)


def sparse_device(start_image, visibilities, strip_index, live_counts, uv_kernels):
    C, F = lax.axis_size("chan"), lax.axis_size("facet")
    L = uv_kernels.shape[0]
    refs = C * F * L * TERMS
    per_facet = start_image.size // STRIP
    piece = per_facet // C
    chips = C // 2
    step = float(per_facet * F / (2.5 * C * F * (L * C) * F))
    kernels = uv_kernels[:, 0]

    blocks = jax.ShapeDtypeStruct((chips * BLOCK, STRIP), I16)
    both = jax.ShapeDtypeStruct((piece + chips * BLOCK, STRIP), I16)
    packed = call(
        functools.partial(pack_kernel, C, F, L),
        [blocks] + [both] * (F - 1),
        [
            start_image,
            visibilities[0],
            strip_index[0].transpose(1, 2, 0),
            live_counts[0].T,
        ],
        10**8,
        placed=True,
        hbm=4,
        scratch=[
            pltpu.VMEM((start_image.shape[0] // C, start_image.shape[1]), F32),
            pltpu.VMEM(visibilities.shape[1:], BF16),
            pltpu.VMEM((F, TERMS, L * C), I32),
            pltpu.VMEM((F, L * C), I32),
            pltpu.VMEM((F * TILE, STRIP), I32),
            pltpu.SemaphoreType.DMA((4,)),
        ],
    )
    got = [packed[0]] + [swap(packed[k], 0, k) for k in range(F - 1, 0, -1)][::-1]
    passed = call(
        functools.partial(pass_kernel, F, piece),
        [jax.ShapeDtypeStruct(((F - 1) * piece + F * BLOCK, STRIP), I16)] * chips,
        got[::-1],
        10**6,
    )
    mine = jnp.concatenate(
        [passed[0]] + [swap(passed[j], 2 * j) for j in range(chips - 1, 0, -1)], axis=0
    )
    other = swap(mine, 1)

    at_refs = jax.ShapeDtypeStruct((refs, STRIP), F32)
    message = jax.ShapeDtypeStruct((refs + EXTRA, STRIP), I16)
    short = jax.ShapeDtypeStruct((PART + EXTRA, STRIP), I16)
    facet_strips = jax.ShapeDtypeStruct((per_facet, STRIP), F32)
    known, seen_part, whole_part, turned = call(
        functools.partial(ready_kernel, C, F, L),
        [
            jax.ShapeDtypeStruct((per_facet + chips * (F - 1) * piece, 2 * STRIP), BF16),
            at_refs,
            jax.ShapeDtypeStruct(((TERMS + 1) * C * F, 2 * STRIP), F32),
            jax.ShapeDtypeStruct(kernels.shape, BF16),
        ],
        [start_image, kernels, mine],
        10**8,
        placed=True,
    )
    est, observed, at, other_at, live, msg = call(
        functools.partial(first_kernel, C, F, L),
        [
            at_refs,
            jax.ShapeDtypeStruct((refs, STRIP), BF16),
            at_refs,
            at_refs,
            jax.ShapeDtypeStruct((L * C * F, STRIP), F32),
            message,
        ],
        [known, seen_part, whole_part, kernels, turned, other],
        5 * 10**8,
        placed=True,
    )

    def along_facet(msgs, cross=0):
        got = [msgs[0]] + [swap(msgs[k], cross, k) for k in range(F - 1, 0, -1)][::-1]
        rows = got[0].shape[0] - EXTRA
        return call(
            join_kernel, [jax.ShapeDtypeStruct((F * rows + EXTRA, STRIP), I16)], got, 10**6
        )[0]

    def around_chan(near, cross=0):
        around = [swap(near, 2 * j + cross) for j in range(chips - 1, 0, -1)]
        return jnp.concatenate([near] + around, axis=0)

    def along_chan(near):
        mine = around_chan(near)
        return mine, swap(mine, 1)

    def facet_part(mine, *crowd):
        return call(
            functools.partial(facet_part_kernel, F, chips),
            [facet_strips, *crowd],
            [mine],
            2 * 10**9,
            placed=True,
        )

    settle = functools.partial(settle_kernel, F, chips, step)
    whole = jax.ShapeDtypeStruct(start_image.shape, F32)

    near = along_facet([msg] * F)
    pick, numbers = call(
        functools.partial(sort_kernel, F, per_facet),
        [
            jax.ShapeDtypeStruct((F * PART, refs), BF16),
            jax.ShapeDtypeStruct((F * EXTRA, STRIP), F32),
        ],
        [at],
        10**8,
        placed=True,
    )
    near, pick, numbers = lax.optimization_barrier((near, pick, numbers))
    mine = around_chan(near)
    part, other_part = call(
        functools.partial(part_kernel, F, chips),
        [at_refs, at_refs],
        [at, other_at, mine],
        3 * 10**8,
    )
    msg, *msgs = call(
        functools.partial(next_kernel, step),
        [message] + [short] * F,
        [at, live, observed, kernels, turned, est, part, swap(other_part, 1), pick, numbers],
        3 * 10**8,
    )
    msg, mine, *msgs = lax.optimization_barrier((msg, mine, *msgs))
    near = along_facet(msgs, 1)
    other = swap(mine, 1)
    part, crowd = facet_part(mine, jax.ShapeDtypeStruct((TILE, STRIP), F32))
    near, part, crowd, other = lax.optimization_barrier((near, part, crowd, other))
    around = around_chan(near, 1)
    image, crowd = call(
        settle,
        [whole, jax.ShapeDtypeStruct((1,), I32)],
        [start_image, part, other, crowd],
        2 * 10**9,
        placed=True,
        scalars=1,
    )
    crowded = crowd[0] > PART
    around, image, crowded = lax.optimization_barrier((around, image, crowded))

    other = swap(around, 1)
    (part,) = facet_part(around)

    def in_full():
        mine, other = along_chan(along_facet([msg] * F))
        (part,) = facet_part(mine)
        (rest,) = facet_part(other)
        return part + rest, jnp.zeros((chips * (F * PART + EXTRA), STRIP), I16)

    part, other = lax.cond(crowded, in_full, lambda: (part, other))
    return call(
        settle,
        [whole],
        [image, part, other],
        2 * 10**9,
        placed=True,
    )[0]


def dense_device(start_image, visibilities, strip_index, live_counts, uv_kernels):
    def to_owner(x):
        x = lax.all_to_all(x, "chan", split_axis=1, concat_axis=0, tiled=True)
        return lax.all_to_all(x, "facet", split_axis=2, concat_axis=0, tiled=True)

    observed, picked_ids, live_now = map(to_owner, (visibilities, strip_index, live_counts))
    slot_count = observed.shape[0]
    chan_local, uv_local = uv_kernels.shape[:2]
    slab_rows, facet_width = start_image.shape
    full_width = facet_width * lax.axis_size("facet")
    strip_count = slab_rows * full_width // STRIP
    blocks = slot_count * chan_local * lax.axis_size("chan") * uv_local * lax.axis_size("facet")
    step_size = strip_count / (2.5 * blocks)
    lane_ids = jnp.arange(2 * VISB, dtype=I32) % VISB
    live_mask = lane_ids < live_now[..., None]
    flat_ids = picked_ids.reshape(-1)
    estimate = start_image
    for iteration in range(ITERS):
        full_sky = lax.all_gather(estimate.astype(BF16), "facet", axis=1, tiled=True)
        sky_strips = full_sky.reshape(strip_count, STRIP)
        gathered = sky_strips[picked_ids].reshape(slot_count, chan_local, uv_local, TERMS * STRIP)
        predicted = jnp.einsum("scup,cupq->scuq", gathered, uv_kernels, preferred_element_type=F32)
        residual = jnp.where(live_mask, predicted - observed.astype(F32), 0.0).astype(BF16)
        adjoint = jnp.einsum("scuq,cupq->scup", residual, uv_kernels, preferred_element_type=F32)
        gradient = jnp.zeros((strip_count, STRIP), F32).at[flat_ids].add(adjoint.reshape(-1, STRIP))
        gradient = gradient.reshape(slab_rows, full_width)
        facet_part = lax.psum_scatter(gradient, "facet", scatter_dimension=1, tiled=True)
        facet_sum = lax.psum(facet_part, "chan")
        descent = estimate - step_size * facet_sum
        estimate = jnp.maximum(descent - shrinkage, 0.0)
    return estimate


def on_device(start_image, visibilities, strip_index, live_counts, uv_kernels):
    C, F = lax.axis_size("chan"), lax.axis_size("facet")
    L, uv_local = uv_kernels.shape[:2]
    strips = start_image.size * F // STRIP
    sparse = (
        visibilities.shape[0] == 1
        and uv_local == 1
        and C & (C - 1) == 0
        and F & (F - 1) == 0
        and C >= 4
        and ITERS == 2
        and F >= 2
        and F <= TILE and F * PART % STRIP == 0
        and C * F * L * TERMS == STRIP
        and 4 * L + TERMS + 1 <= BLOCK
        and 4 * L == TILE
        and L * C <= STRIP
        and strips <= 64 * 256
        and strips & (strips - 1) == 0
        and start_image.shape[0] % (C * TILE) == 0
        and start_image.shape[1] % STRIP == 0
        and start_image.size // STRIP // C % 16 == 0
    )
    run = sparse_device if sparse else dense_device
    return run(start_image, visibilities, strip_index, live_counts, uv_kernels)


def solution(mesh):
    placed = (
        P(None, "facet"),
        P(("chan", "facet"), None, None, None),
        P(("chan", "facet"), None, None, None),
        P(("chan", "facet"), None, None),
        P("chan", "facet", None, None),
    )
    return jax.shard_map(
        on_device, mesh=mesh, in_specs=placed, out_specs=P(None, "facet"), check_vma=False
    )
```
